256 devices in a mesh: seq: 32 (over y, z), exp: 8 (over x, core).
Axes of the slice: x: 4, y: 4, z: 8, core: 2. Of those that a mesh axis runs over, the one named last changes fastest.
Arguments:
- residual_in: bfloat16 [4096, 4096], P('seq'), may hold values from -3 to 3
- mamba_in: bfloat16 [3, 4096, 8192], P(None, 'seq', 'exp'), may hold values from -6 to 6
- bc_proj: float32 [32, 4096], P(None, 'seq'), may hold values from -6 to 6
- decay: float32 [16, 8192], P(None, 'exp'), may hold values from 2.4414063e-05 to 0.08
- conv_w: float32 [4, 8192], P(None, 'exp'), may hold values from -3 to 3
- mamba_vec: float32 [3, 8192], P(None, 'exp'), may hold values from -1 to 1
- doc_len: int32 [8], replicated, may hold values from 1 to 2048, 4096 in all
- w_out: bfloat16 [8192, 4096], P('exp', 'seq'), may hold values from -0.0625 to 0.0625
- norm_gain: float32 [4096], replicated, may hold values from 0.1 to 1.9
- routes: int32 [4096, 2], P('seq'), may hold values from 0 to 7, all different within a row; in each aligned block of 128 rows (0 to 127, 128 to 255, ...) at most 36 rows name the same one
- gate_w: float32 [4096, 2], P('seq'), may hold values from 0.5 to 3
- w_gate_up: bfloat16 [8, 2, 4096, 12288], P('exp', None, None, 'seq'), may hold values from -0.09375 to 0.09375
- w_down: bfloat16 [8, 12288, 4096], P('exp', 'seq'), may hold values from -0.3125 to 0.3125
Outputs:
- layer_out: bfloat16 [4096, 4096], P('seq', 'exp')
The draws below stay inside these ranges and needn't reach their ends.
Inputs may be any that keep to these rules, and one draw needn't show every extreme that they name: `routes`: in each aligned block of 128 rows no expert is named by more than 36 rows, a bound that some block reaches; the two experts of a row differ.
All inputs are finite; a program needn't handle non-finite values.
Results may differ from the reference program's by a relative error of at most 0.03.
Values may be sent and summed in bfloat16 or wider, within the bound.
A program may use at most 128 MiB of HBM per device.

```python
import math
import jax
import jax.numpy as jnp
import numpy as np
from jax import lax

D = 4096
INNER = 8192
NSTATE = 16
CONV = 4
FFW = 12288
DOCS = 8
TOK_DEV = 128
TOKENS = 4096
EXPERTS = 8
CAP = 36
N_SEQ = 32
N_EXP = 8


def steps_of(rng, shape, split, smallest, high):
    loudness = 1.0
    for axis_at, parts in split:
        draws = jax.random.uniform(jax.random.fold_in(jax.random.fold_in(rng, 6), axis_at), (parts,), jnp.float32, smallest / len(split), high / len(split))
        loudness = loudness * jnp.repeat(jnp.exp(draws), shape[axis_at] // parts).reshape((-1,) + (1,) * (len(shape) - 1 - axis_at))
    return loudness


def split_up(number_of, total, reach, skew):
    loads = [(1 << 20) // math.isqrt(rank ** skew) + 1 for rank in range(2, number_of + 1)]
    spare, given = total - reach - (number_of - 1), [1] * (number_of - 1)
    while spare > 0:
        movable = [i for i in range(number_of - 1) if given[i] < reach]
        whole, remaining = sum([loads[i] for i in movable]), spare
        for i in movable:
            more = min(reach - given[i], max(1, remaining * loads[i] // whole), spare)
            given[i] = given[i] + more
            spare = spare - more
    return np.array([reach] + given)


def ragged(rng, amount, total, reach, slope):
    if amount == 2:
        one = jax.random.randint(rng, (), max(1, total - reach), min(reach, total - 1) + 1)
        return jnp.stack([one, total - one])
    tallies = jnp.asarray(split_up(amount, total, reach, slope), jnp.int32)
    pairs = (amount - 1) // 2
    source_of, taker = tallies[1:1 + 2 * pairs:2], tallies[2:2 + 2 * pairs:2]
    margin = jnp.minimum(source_of - 1, reach - taker)
    shifted = jax.random.randint(jax.random.fold_in(rng, 1), (pairs,), 0, 1 << 20) % (margin + 1)
    tallies = tallies.at[1:1 + 2 * pairs:2].set(source_of - shifted).at[2:2 + 2 * pairs:2].set(taker + shifted)
    return tallies[jax.random.permutation(jax.random.fold_in(rng, 2), amount)]


def deal_out(key, own, number, rows, count, top, limit, lean):
    order = jax.random.permutation(key, count)
    packed, usual = load_shares(count, rows * top, limit, lean, True), load_shares(count, rows * top, limit, lean, False)
    places = jnp.arange(count)

    def named(tallies, turn):
        used = int((tallies > 0).sum())
        fixed = max(1, used // 4)
        passed = fixed + (places - fixed + turn * (used - fixed)) % max(1, count - fixed)
        return jnp.zeros((count,), jnp.int32).at[order[jnp.where(places < fixed, places, passed)]].set(jnp.asarray(tallies, jnp.int32))

    tallies = jnp.where(number % 4 == 0, named(packed, number // 4), named(usual, number - number // 4 - 1))
    mixed = jax.random.permutation(jax.random.fold_in(own, 3), count)
    source_of, receiver = mixed[0:count // 2 * 2:2], mixed[1:count // 2 * 2:2]
    slack = jnp.minimum(tallies[source_of] - 1, limit - tallies[receiver]) // 2
    slack = jnp.where((source_of == order[0]) | (receiver == order[0]) | (tallies[receiver] == 0), 0, jnp.maximum(slack, 0))
    passed = jax.random.randint(jax.random.fold_in(own, 4), (count // 2,), 0, 1 << 20) % (slack + 1)
    tallies = tallies.at[source_of].add(-passed).at[receiver].add(passed)
    labels = jnp.searchsorted(jnp.cumsum(tallies), jnp.arange(rows * top), side="right").astype(jnp.int32)
    grid = labels.reshape(top, rows).T
    grid = grid[jax.random.permutation(jax.random.fold_in(own, 1), rows)]
    turn = jax.random.randint(jax.random.fold_in(own, 2), (rows, 1), 0, top)
    return jnp.take_along_axis(grid, (jnp.arange(top)[None, :] + turn) % top, axis=1)


def load_shares(count, total, reach, lean, full):
    portions = [(1 << 20) // math.isqrt(standing ** lean) + 1 for standing in range(1, count + 1)]
    largest = reach if full else min(reach, max(-(-total // count), total * portions[0] // sum(portions)))
    least = 1 if total - largest >= count - 1 else 0
    given, rest = [largest] + [least] * (count - 1), total - largest - least * (count - 1)
    while rest > 0:
        free = [i for i in range(1, count) if given[i] < largest] or [i for i in range(1, count) if given[i] < reach]
        pool, budget = sum([portions[i] for i in free]), rest
        for i in free:
            extra = min(reach - given[i], max(1, budget * portions[i] // pool), rest)
            given[i] = given[i] + extra
            rest = rest - extra
    return np.array(given)


def normal_values(key, extent, width, reach, split=(), kind=jnp.bfloat16):
    level = steps_of(key, extent, split, -0.22, 0.18) if split else 1.0
    entries = jax.random.normal(key, extent, jnp.float32) * width * level
    return jnp.minimum(jnp.maximum(entries, -reach), reach).astype(kind)


def setup_inputs(seed: int = 0) -> dict:
    seeds = jax.random.split(jax.random.key(seed), 14)
    residual_in = normal_values(seeds[0], (TOKENS, D), 0.5, 3.0, ((0, 32),))
    mamba_in = normal_values(seeds[1], (3, TOKENS, INNER), 1.0, 6.0, ((1, 32), (2, 8)))
    bc_proj = normal_values(seeds[2], (2 * NSTATE, TOKENS), 1.0, 6.0, ((1, 32),), jnp.float32)
    decay = jnp.clip(jnp.exp(math.log(0.08) - 8.094623 * jax.random.uniform(seeds[3], (NSTATE, INNER), jnp.float32) ** steps_of(seeds[3], (NSTATE, INNER), ((1, 8),), -0.2, 0.2)), 2.441406286379788e-05, 0.08)
    conv_w = normal_values(seeds[4], (CONV, INNER), 0.5, 3.0, ((1, 8),), jnp.float32)
    mamba_vec = jnp.clip(jax.random.uniform(seeds[5], (3, INNER), jnp.float32, -1.0, 1.0) * steps_of(seeds[5], (3, INNER), ((1, 8),), -0.4, 0.0), -1.0, 1.0)
    doc_len = ragged(seeds[6], DOCS, TOKENS, TOKENS // 2, 2).astype(jnp.int32)
    w_out = normal_values(seeds[7], (INNER, D), INNER ** -0.5, 0.0625, ((0, 8), (1, 32)))
    norm_gain = jnp.clip(1.0 + 0.18 * jax.random.normal(seeds[8], (D,), jnp.float32), 0.1, 1.9)
    routes_keys = jax.random.split(jax.random.fold_in(seeds[9], 1), TOKENS // TOK_DEV)
    routes_turns = jax.random.permutation(jax.random.fold_in(seeds[9], 3), TOKENS // TOK_DEV)
    routes = jax.vmap(lambda own, number: deal_out(jax.random.fold_in(seeds[9], 2), own, number, TOK_DEV, EXPERTS, 2, CAP, 2))(routes_keys, routes_turns).reshape((TOKENS, 2))
    gate_w = jnp.clip(0.5 + 2.5 * jax.random.uniform(seeds[10], (TOKENS, 2), jnp.float32) ** steps_of(seeds[10], (TOKENS, 2), ((0, 32),), -0.2, 0.2), 0.5, 3.0)
    w_gate_up = normal_values(seeds[11], (EXPERTS, 2, D, FFW), D ** -0.5, 0.09375, ((0, 8), (3, 32)))
    w_down = normal_values(seeds[12], (EXPERTS, FFW, D), (FFW // N_SEQ) ** -0.5, 0.3125, ((0, 8), (1, 32)))
    return dict(residual_in=residual_in, mamba_in=mamba_in, bc_proj=bc_proj, decay=decay, conv_w=conv_w, mamba_vec=mamba_vec, doc_len=doc_len, w_out=w_out, norm_gain=norm_gain, routes=routes, gate_w=gate_w, w_gate_up=w_gate_up, w_down=w_down)


def document_index(positions, doc_len):
    ends = jnp.cumsum(doc_len).astype(jnp.int32)
    return lax.optimization_barrier(jnp.sum((ends[None, :] <= positions[:, None]).astype(jnp.int32), axis=1))

def reference(residual_in, mamba_in, bc_proj, decay, conv_w, mamba_vec, doc_len, w_out, norm_gain, routes, gate_w, w_gate_up, w_down):
    x_values = mamba_in[0].astype(jnp.float32)
    z_values = mamba_in[1].astype(jnp.float32)
    dt_values = mamba_in[2].astype(jnp.float32)
    positions = jnp.arange(TOKENS, dtype=jnp.int32)
    docs = document_index(positions, doc_len)
    padded = jnp.pad(x_values, ((CONV - 1, 0), (0, 0)))
    total = jnp.zeros((TOKENS, INNER), jnp.float32) + mamba_vec[0][None, :]
    for offset in range(CONV):
        source = positions - (CONV - 1) + offset
        valid = ((source >= 0) & (document_index(source, doc_len) == docs)).astype(jnp.float32)
        total = total + conv_w[offset][None, :] * padded[offset:offset + TOKENS] * valid[:, None]
    u_values = jax.nn.silu(total)
    step_size = jax.nn.softplus(dt_values + mamba_vec[1][None, :])
    keep = jnp.concatenate([jnp.ones((1,), jnp.float32), (docs[1:] == docs[:-1]).astype(jnp.float32)])
    decay_t = decay.T

    def advance(state, inputs):
        dt_row, u_row, b_row, c_row, keep_row = inputs
        state = jnp.exp(-dt_row[:, None] * decay_t) * keep_row * state + (dt_row * u_row)[:, None] * b_row[None, :]
        return (state, lax.optimization_barrier(jnp.sum(state * c_row[None, :], axis=1)))
    start_state = jnp.zeros((INNER, NSTATE), jnp.float32)
    _, scanned = lax.scan(advance, start_state, (step_size, u_values, bc_proj[:NSTATE].T, bc_proj[NSTATE:].T, keep))
    mixer_y = scanned + mamba_vec[2][None, :] * u_values
    gated = (mixer_y * jax.nn.silu(z_values)).astype(jnp.bfloat16)
    block = INNER // N_EXP
    mix = jnp.zeros((TOKENS, D), jnp.float32)
    for index in range(N_EXP):
        partial_mix = jnp.dot(gated[:, index * block:(index + 1) * block], w_out[index * block:(index + 1) * block], preferred_element_type=jnp.float32)
        mix = mix + partial_mix.astype(jnp.bfloat16).astype(jnp.float32)
    resid = residual_in.astype(jnp.float32) + mix
    mean_sq = lax.optimization_barrier(jnp.mean(resid * resid, axis=1, keepdims=True))
    normed = (resid * lax.rsqrt(mean_sq + 1e-05) * norm_gain[None, :]).astype(jnp.bfloat16)
    flat_routes = routes.reshape(-1)
    flat_gates = gate_w.reshape(-1)
    token_of = jnp.arange(2 * TOKENS, dtype=jnp.int32) // 2
    row_count = N_SEQ * CAP
    unit_block = FFW // N_SEQ
    moe = jnp.zeros((TOKENS, D), jnp.float32)
    for expert in range(EXPERTS):
        chosen = jnp.nonzero(flat_routes == expert, size=row_count, fill_value=0)[0].astype(jnp.int32)
        valid = (jnp.arange(row_count) < jnp.sum((flat_routes == expert).astype(jnp.int32))).astype(jnp.float32)
        tokens_here = token_of[chosen]
        rows = normed[tokens_here]
        gate_part = jnp.dot(rows, w_gate_up[expert, 0], preferred_element_type=jnp.float32)
        up_part = jnp.dot(rows, w_gate_up[expert, 1], preferred_element_type=jnp.float32)
        hidden = (jax.nn.silu(gate_part) * up_part).astype(jnp.bfloat16)

        def add_block(index, running):
            hidden_block = lax.dynamic_slice_in_dim(hidden, index * unit_block, unit_block, 1)
            down_block = lax.dynamic_slice_in_dim(w_down[expert], index * unit_block, unit_block, 0)
            partial_out = jnp.dot(hidden_block, down_block, preferred_element_type=jnp.float32)
            return running + partial_out.astype(jnp.bfloat16).astype(jnp.float32)
        summed = lax.fori_loop(0, N_SEQ, add_block, jnp.zeros((row_count, D), jnp.float32))
        expert_out = summed.astype(jnp.bfloat16).astype(jnp.float32)
        weighted = (flat_gates[chosen][:, None] * expert_out).astype(jnp.bfloat16).astype(jnp.float32)
        moe = moe.at[tokens_here].add(weighted * valid[:, None])
    return (resid + moe).astype(jnp.bfloat16)
```

```python
import functools

import jax
import jax.numpy as jnp
from jax import lax
from jax.experimental import pallas as pl
from jax.experimental.pallas import tpu as pltpu
from jax.sharding import PartitionSpec as P

MESH = pl.DeviceIdType.MESH
LOG2E = 1.4426950408889634
LANES = 128
F32 = jnp.float32
BF16 = jnp.bfloat16
YS, ZS = 4, 8
CORES = 2
SLAB = 48
CAP_MAIN = 32

Y_OFFSETS = (0, 1, -1, 2)
Z_OFFSETS = (0, 1, -1, 2, -2, 3, -3, 4)
SLOTS = [(dy, dz) for dz in Z_OFFSETS for dy in Y_OFFSETS]
GROUP = 8


def far_steps(offset, size):
    top = size // 2
    if offset == 0:
        return [(1, 1, None), (-1, -1, None)]
    if offset == top:
        return []
    if offset > 0:
        return [(offset + 1, 1, 0 if offset + 1 == top else None)]
    return [(offset - 1, -1, None)] if offset - 1 > -top else [(top, -1, 1)]


def messages():
    found = []
    for tree in range(2):
        for dy, dz in SLOTS:
            if tree == 1 or dz == 0:
                for to, way, part in far_steps(dy, YS):
                    found.append((tree, (dy, dz), (to, dz), part, ("y", way)))
            if tree == 0 or dy == 0:
                for to, way, part in far_steps(dz, ZS):
                    found.append((tree, (dy, dz), (dy, to), part, ("z", way)))
    return found


MESSAGES = messages()
DEPTH = {slot: abs(slot[0]) + abs(slot[1]) for slot in SLOTS}
DEEPEST = max(DEPTH.values())


ORDER = [
    1, 2, 39, 40, 37, 38, 3, 4, -1, 5, 6, 7, -2, 8, -39, 43, 44, 45, -40, 50, -37, 41, -38, 42, 9,
    10, 48, 49, -3, -4, -5, -8, 13, 17, -6, -7, -43, 46, -44, 47, -45, 55, -50, 60, 53, 54, -41,
    -42, 11, 12, -48, 51, -49, 52, -9, -10, 14, 18, 58, 59, -13, -17, -46, -47, -55, 65, -60, 70,
    -53, 56, -54, 57, 15, 19, 63, 64, 21, 25, -11, -12, -51, -52, 16, 20, -58, 61, -59, 62, -14,
    -18, 68, 69, -65, -70, 22, 26, -56, -57, -15, -19, 23, 27, -63, 66, -64, 67, -21, -25, 29, 33,
    73, 74, -16, 24, -20, 28, -61, -62, -22, 30, -26, 34, -68, 71, -69, 72, -23, 31, -27, 35, -24,
    32, -28, 36, -73, 75, -74, 76, -66, -67, -29, -33, -30, -34, -71, -72, -31, -35, -32, -36, -75,
    -76,
]


def groups_full_at(at):
    last = {}
    for place, item in enumerate(ORDER):
        if item < 0:
            last[SLOTS.index(MESSAGES[-item - 1][2]) // GROUP] = place
    return [group for group in sorted(last) if last[group] == at]


def silu(v):
    return v / (1.0 + jnp.exp(-v))


def seq_id(index):
    return {"seq": index}


def exp_id(index):
    return {"exp": index}


def neighbour(axis, way):
    me = lax.axis_index("seq")
    y, z = me // ZS, me % ZS
    if axis == "y":
        return ((y + way + YS) % YS) * ZS + z
    return y * ZS + (z + way + ZS) % ZS


def spread(view, send_sems, recv_sems):
    def copy(k):
        tree, source, target, part, way = MESSAGES[k]
        return pltpu.make_async_remote_copy(
            src_ref=view(tree, SLOTS.index(source), part),
            dst_ref=view(tree, SLOTS.index(target), part),
            send_sem=send_sems.at[k],
            recv_sem=recv_sems.at[k],
            device_id=seq_id(neighbour(*way)),
            device_id_type=MESH,
        )

    def run(when_full, start=0, stop=len(ORDER)):
        for at in range(start, stop):
            item = ORDER[at]
            if item > 0:
                copy(item - 1).start()
            else:
                copy(-item - 1).wait_recv()
                for group in groups_full_at(at):
                    when_full(group)

    def finish():
        for k in range(len(MESSAGES)):
            copy(k).wait_send()

    return run, finish


def gather_sum(view, landing, add, send_sems, recv_sems):
    def copy(k):
        tree, _, child, part, (axis, way) = MESSAGES[k]
        return pltpu.make_async_remote_copy(
            src_ref=view(tree, SLOTS.index(child), part),
            dst_ref=landing(tree, SLOTS.index(child), part),
            send_sem=send_sems.at[k],
            recv_sem=recv_sems.at[k],
            device_id=seq_id(neighbour(axis, -way)),
            device_id_type=MESH,
        )

    def run():
        for item in reversed(ORDER):
            k = abs(item) - 1
            if item < 0:
                copy(k).start()
            else:
                copy(k).wait_recv()
                _, parent, child, part, _ = MESSAGES[k]
                add(MESSAGES[k][0], SLOTS.index(parent), SLOTS.index(child), part)

    def finish():
        for k in range(len(MESSAGES)):
            copy(k).wait_send()

    return run, finish


def dot(a, b):
    return jnp.dot(a, b, preferred_element_type=F32)


def one_hot(condition):
    return condition.astype(F32).astype(BF16)


def slot_table(routes):
    toks = routes.shape[0]
    expert = lax.broadcasted_iota(jnp.int32, (toks, LANES), 1)
    hits = jnp.logical_or(routes[:, 0:1] == expert, routes[:, 1:2] == expert)
    row = lax.broadcasted_iota(jnp.int32, (toks, toks), 0)
    col = lax.broadcasted_iota(jnp.int32, (toks, toks), 1)
    places = dot(one_hot(col <= row), one_hot(hits)) - 1.0
    return jnp.where(hits, places, -1.0)


def places_of(table_t, expert):
    place = lax.broadcasted_iota(jnp.int32, (SLAB, table_t.shape[1]), 0).astype(F32)
    return (place == table_t[expert : expert + 1, :]).astype(F32)


def split_lanes(width):
    first = (width * 13 // 32) // LANES * LANES
    quarter = width // 4
    rest = (quarter * 13 // 32) // LANES * LANES
    return (first, width - first), (rest, quarter - rest)


CHUNKS = 4
SHARES = [6, 12, 16, 22, 28, 34, 40, 46, 52, 60]


def mixer_kernel(
    reach,
    mamba_ref,
    bc_ref,
    decay_ref,
    conv_ref,
    vec_ref,
    doc_ref,
    residual_ref,
    w_ref,
    gain_ref,
    routes_ref,
    resid_ref,
    own_a,
    own_b,
    xs,
    dts,
    us,
    zs,
    neg,
    tail,
    end_out,
    end_in,
    sum_out,
    sum_in,
    held_a,
    held_b,
    gated,
    partial,
    pair_in,
    pair_sum,
    cross_in,
    disp,
    disp_in,
    squares,
    rows_n,
    send_sems,
    recv_sems,
    w_send_sems,
    w_recv_sems,
    exp_send_sems,
    exp_recv_sems,
):
    count = lax.axis_size("seq")
    me = lax.axis_index("seq")
    toks = mamba_ref.shape[1]
    blocks = mamba_ref.shape[2] // LANES
    nstate = decay_ref.shape[0]
    rows = blocks
    first = me * toks
    e = lax.axis_index("exp")
    experts_count = lax.axis_size("exp")
    x, core = e // CORES, e % CORES
    xs_count = experts_count // CORES

    barrier = pltpu.get_barrier_semaphore()

    def greet(step, _):
        pl.semaphore_signal(
            barrier, inc=1, device_id=seq_id(lax.rem(me + step, count)), device_id_type=MESH
        )
        return 0

    lax.fori_loop(1, count, greet, 0)
    for step in range(1, experts_count):
        pl.semaphore_signal(
            barrier,
            inc=1,
            device_id=exp_id(lax.rem(e + step, experts_count)),
            device_id_type=MESH,
        )

    depth = w_ref.shape[0]
    upper = held_a.shape[1]
    held_a[0] = w_ref[pl.ds(0, upper), :]
    held_b[0] = w_ref[pl.ds(upper, depth - upper), :]
    for j in range(blocks):
        lanes = pl.ds(j * LANES, LANES)
        xs[pl.ds(8 * rows + j, toks, stride=rows), :] = mamba_ref[0, :, lanes].astype(F32)
        zs[pl.ds(j, toks, stride=rows), :] = mamba_ref[1, :, lanes].astype(F32)
        dts[pl.ds(j, toks, stride=rows), :] = mamba_ref[2, :, lanes].astype(F32)
    pl.semaphore_wait(barrier, count - 1 + experts_count - 1)

    def held_view(tree, slot, part):
        ref = (held_a, held_b)[tree]
        size = ref.shape[1]
        if part is None:
            return ref.at[slot]
        return ref.at[slot, pl.ds(part * (size // 2), size // 2)]

    gather, gather_end = spread(held_view, w_send_sems, w_recv_sems)
    tail_copy = pltpu.make_async_remote_copy(
        src_ref=mamba_ref.at[0, pl.ds(toks - 16, 16)],
        dst_ref=tail,
        send_sem=send_sems.at[0],
        recv_sem=recv_sems.at[0],
        device_id=seq_id(lax.rem(me + 1, count)),
        device_id_type=MESH,
    )
    tail_copy.start()

    waiting = []
    reached = [0]

    def product(group):
        for pair in range(GROUP // 2):
            first_slot = group * GROUP + 2 * pair
            sides = [
                jnp.concatenate([held_a[first_slot + n], held_b[first_slot + n]], axis=0)
                for n in range(2)
            ]
            made = dot(gated[...], jnp.concatenate(sides, axis=1)).astype(BF16)
            for n in range(2):
                dy, dz = SLOTS[first_slot + n]
                y, z = me // ZS, me % ZS
                owner = ((y - dy + YS) % YS) * ZS + (z - dz + ZS) % ZS
                block = owner // tiles_per
                lane = pl.multiple_of((owner % tiles_per) * LANES, LANES)
                partial[block % CORES, block // CORES, :, pl.ds(lane, LANES)] = made[
                    :, n * LANES : (n + 1) * LANES
                ]

    tiles_per = resid_ref.shape[1] // LANES

    def forward(share, act=False):
        stop = len(ORDER) * share // 100
        gather(product if act else waiting.append, reached[0], stop)
        reached[0] = stop

    forward(SHARES[0])
    neg[...] = decay_ref[...] * (-LOG2E)
    step_bias = vec_ref[1]

    def tok(t):
        return pl.ds(pl.multiple_of(t * rows, rows), rows)

    def prepare(t, total):
        raw = dts[tok(t), :] + step_bias
        step = jnp.maximum(raw, 0.0) + jnp.log1p(jnp.exp(-jnp.abs(raw)))
        dts[tok(t), :] = step
        zs[tok(t), :] = silu(zs[tok(t), :])
        return total + step

    total_step = lax.fori_loop(0, toks, prepare, jnp.zeros((rows, LANES), F32), unroll=8)

    forward(SHARES[1])
    tail_copy.wait()
    there = jnp.where(me > 0, 1.0, 0.0).astype(F32)
    for j in range(blocks):
        rest = tail[:, pl.ds(j * LANES, LANES)].astype(F32) * there
        xs[pl.ds(j, 8, stride=rows), :] = rest[8:16, :]

    ends = []
    so_far = jnp.int32(0)
    for j in range(doc_ref.shape[0]):
        so_far = so_far + doc_ref[j]
        ends.append(so_far)

    def goes_on(position):
        keep = jnp.float32(1.0)
        for end in ends:
            keep = jnp.where(end == position, jnp.float32(0.0), keep)
        return keep

    taps = [conv_ref[k] for k in range(conv_ref.shape[0])]
    conv_bias = vec_ref[0]

    def advance(t, states, keep, step, drive):
        new = []
        for n in range(nstate):
            growth = jnp.exp2(step * neg[n]) * keep
            new.append(growth * states[n] + drive * bc_ref[n, t])
        return tuple(new)

    def local_pass(t, carry):
        states, before, before2 = carry
        keep = goes_on(first + t)
        x0, x1, x2, x3 = [xs[tok(t + 8 - 3 + k), :] for k in range(4)]
        v2 = keep
        v1 = keep * before
        v0 = v1 * before2
        total = conv_bias + (taps[0] * x0) * v0 + (taps[1] * x1) * v1
        total = total + (taps[2] * x2) * v2 + taps[3] * x3
        u_row = silu(total)
        us[tok(t), :] = u_row
        step = dts[tok(t), :]
        return advance(t, states, keep, step, step * u_row), keep, before

    zero = tuple(jnp.zeros((rows, LANES), F32) for _ in range(nstate))
    carry = (zero, goes_on(first - 1), goes_on(first - 2))
    for i in range(CHUNKS):
        carry = lax.fori_loop(
            i * toks // CHUNKS, (i + 1) * toks // CHUNKS, local_pass, carry, unroll=2
        )
        if i < CHUNKS - 1:
            forward(SHARES[2 + i])
    states = carry[0]
    for n in range(0, nstate, 2):
        pair = jnp.concatenate([states[n], states[n + 1]], axis=0)
        end_out[pl.ds(n * rows, 2 * rows), :] = pair.astype(BF16)
    sum_out[...] = total_step

    def copies(k):
        target = seq_id(lax.rem(me + k, count))
        one = pltpu.make_async_remote_copy(
            src_ref=end_out,
            dst_ref=end_in.at[k - 1],
            send_sem=send_sems.at[2 * k - 1],
            recv_sem=recv_sems.at[2 * k - 1],
            device_id=target,
            device_id_type=MESH,
        )
        two = pltpu.make_async_remote_copy(
            src_ref=sum_out,
            dst_ref=sum_in.at[k - 1],
            send_sem=send_sems.at[2 * k],
            recv_sem=recv_sems.at[2 * k],
            device_id=target,
            device_id_type=MESH,
        )
        return one, two

    def send(k, _):
        one, two = copies(k)
        one.start()
        two.start()
        return 0

    lax.fori_loop(1, reach + 1, send, 0)

    forward(SHARES[1 + CHUNKS])

    def finish(k, _):
        one, two = copies(k)
        one.wait()
        two.wait()
        return 0

    lax.fori_loop(1, reach + 1, finish, 0)

    def enter(i, states):
        k = reach - i
        source = me - k
        whole = jnp.where(source >= 0, jnp.float32(1.0), jnp.float32(0.0))
        start = source * toks
        unbroken = whole
        for end in ends:
            inside = jnp.logical_and(end >= start, end < start + toks)
            unbroken = jnp.where(inside, jnp.float32(0.0), unbroken)
        sums = sum_in[k - 1]
        new = []
        for n in range(0, nstate, 2):
            pair = end_in[k - 1, pl.ds(n * rows, 2 * rows), :].astype(F32)
            for m in range(2):
                growth = jnp.exp2(sums * neg[n + m]) * unbroken
                new.append(growth * states[n + m] + whole * pair[m * rows : (m + 1) * rows, :])
        return tuple(new)

    entering = lax.fori_loop(0, reach, enter, zero)
    forward(SHARES[2 + CHUNKS])
    skip = vec_ref[2]

    def full_pass(t, states):
        keep = goes_on(first + t)
        u_row = us[tok(t), :]
        step = dts[tok(t), :]
        states = advance(t, states, keep, step, step * u_row)
        total = skip * u_row
        for n in range(nstate):
            total = total + states[n] * bc_ref[nstate + n, t]
        zs[tok(t), :] = zs[tok(t), :] * total
        return states

    states = entering
    for i in range(CHUNKS):
        states = lax.fori_loop(
            i * toks // CHUNKS, (i + 1) * toks // CHUNKS, full_pass, states, unroll=2
        )
        if i < CHUNKS - 1:
            forward(SHARES[3 + CHUNKS + i])
    for j in range(blocks):
        gated[:, pl.ds(j * LANES, LANES)] = zs[pl.ds(j, toks, stride=rows), :].astype(BF16)
    for group in waiting:
        product(group)
    routes = routes_ref[...]
    table_t = slot_table(routes).T
    forward(100, act=True)

    def pair_copy(k):
        to = lax.rem(x + k, xs_count)
        return pltpu.make_async_remote_copy(
            src_ref=partial.at[1 - core, to],
            dst_ref=pair_in.at[to],
            send_sem=exp_send_sems.at[k],
            recv_sem=exp_recv_sems.at[k],
            device_id=exp_id(x * CORES + 1 - core),
            device_id_type=MESH,
        )

    def cross_copy(k):
        to = lax.rem(x + k, xs_count)
        return pltpu.make_async_remote_copy(
            src_ref=pair_sum.at[to],
            dst_ref=cross_in.at[k - 1],
            send_sem=exp_send_sems.at[xs_count + k],
            recv_sem=exp_recv_sems.at[xs_count + k],
            device_id=exp_id(to * CORES + core),
            device_id_type=MESH,
        )

    order = [2, 1, 3, 0]
    for k in order:
        pair_copy(k).start()
    for k in order:
        pair_copy(k).wait_recv()
        to = lax.rem(x + k, xs_count)
        total = partial[core, to].astype(F32) + pair_in[to].astype(F32)
        if k > 0:
            pair_sum[to] = total.astype(BF16)
            cross_copy(k).start()
    width = residual_ref.shape[1]
    block = width // experts_count
    total = total + residual_ref[:, pl.ds(pl.multiple_of(e * block, block), block)].astype(F32)
    for k in (1, 3, 2):
        cross_copy(k).wait_recv()
        total = total + cross_in[k - 1].astype(F32)
    resid_ref[...] = total

    square = jnp.sum(total * total, axis=1, keepdims=True)
    squares[e] = (square * jnp.ones((1, LANES), F32)).T[0:8, :]
    sent_rows = total.astype(BF16)
    for j in range(experts_count):
        disp[j] = dot(places_of(table_t, j).astype(BF16), sent_rows).astype(BF16)

    def deal(k):
        to = lax.rem(e + k, experts_count)
        base = 2 * xs_count + 2 * (k - 1)
        return [
            pltpu.make_async_remote_copy(
                src_ref=source,
                dst_ref=target,
                send_sem=exp_send_sems.at[base + i],
                recv_sem=exp_recv_sems.at[base + i],
                device_id=exp_id(to),
                device_id_type=MESH,
            )
            for i, (source, target) in enumerate(
                [(disp.at[to], disp_in.at[e]), (squares.at[e], squares.at[e])]
            )
        ]

    for k in range(1, experts_count):
        for copy in deal(k):
            copy.start()
    disp_in[e] = disp[e]
    expert_row = lax.broadcasted_iota(jnp.int32, (LANES, toks), 0)
    place_t = jnp.sum(jnp.where(expert_row == e, table_t, 0.0), axis=0, keepdims=True)
    at = lax.broadcasted_iota(jnp.int32, (SLAB, toks), 0).astype(F32)
    mine = (at == place_t).astype(F32)
    for k in range(1, experts_count):
        for copy in deal(k):
            copy.wait_recv()
    mean = squares[0]
    for j in range(1, experts_count):
        mean = mean + squares[j]
    inverse = lax.rsqrt(mean * (1.0 / width) + 1e-05)
    scale = jnp.sum(mine * inverse[0:1, :], axis=1, keepdims=True)
    for j in range(experts_count):
        here = pl.ds(j * block, block)
        rows_n[:, here] = (disp_in[j].astype(F32) * scale * gain_ref[:, here]).astype(BF16)
    mains, rests = split_lanes(width)
    quarter = width // 4
    small_row = lax.broadcasted_iota(jnp.int32, (16, 16), 0)
    small_col = lax.broadcasted_iota(jnp.int32, (16, 16), 1)
    packed = jnp.zeros((16, quarter), F32)
    for q in range(4):
        choose = one_hot(jnp.logical_and(small_col < 4, small_row == q * 4 + small_col))
        packed = packed + dot(choose, rows_n[pl.ds(CAP_MAIN, 16), pl.ds(q * quarter, quarter)])
    packed = packed.astype(BF16)
    start = 0
    rest_start = 0
    for tree, own in enumerate((own_a, own_b)):
        wide = mains[tree]
        for tile in range(2):
            own[:, pl.ds(tile * wide, wide)] = rows_n[pl.ds(tile * 16, 16), pl.ds(start, wide)]
        own[:, pl.ds(2 * wide, rests[tree])] = packed[:, rest_start : rest_start + rests[tree]]
        start += wide
        rest_start += rests[tree]

    gather_end()
    for k in range(xs_count):
        pair_copy(k).wait_send()
        if k > 0:
            cross_copy(k).wait_send()
    for k in range(1, experts_count):
        for copy in deal(k):
            copy.wait_send()


def mixer(mamba_in, bc_proj, decay, conv_w, mamba_vec, doc_len, residual, w_out, gain, routes):
    toks, channels = mamba_in.shape[1:]
    nstate = decay.shape[0]
    rows = channels // LANES
    reach = 2048 // toks
    width = residual.shape[1]
    count = lax.axis_size("exp")
    block = width // count
    depth = w_out.shape[0]
    upper = depth * 13 // 32 // 32 * 32
    mains, rests = split_lanes(width)
    sizes = [2 * main + rest for main, rest in zip(mains, rests)]
    xs_count = count // CORES
    exp_sems = 2 * xs_count + 2 * (count - 1)
    tiles = lambda a: a.reshape(a.shape[0], rows, LANES)
    vmem = pl.BlockSpec(memory_space=pltpu.VMEM)
    smem = pl.BlockSpec(memory_space=pltpu.SMEM)
    return pl.pallas_call(
        functools.partial(mixer_kernel, reach),
        out_shape=[jax.ShapeDtypeStruct((toks, block), F32)]
        + [jax.ShapeDtypeStruct((16, size), BF16) for size in sizes],
        in_specs=[vmem, smem, vmem, vmem, vmem, smem, vmem, vmem, vmem, vmem],
        out_specs=[vmem] * 3,
        scratch_shapes=[
            pltpu.VMEM(((toks + 8) * rows, LANES), F32),
            pltpu.VMEM((toks * rows, LANES), F32),
            pltpu.VMEM((toks * rows, LANES), F32),
            pltpu.VMEM((toks * rows, LANES), F32),
            pltpu.VMEM((nstate, rows, LANES), F32),
            pltpu.VMEM((16, channels), BF16),
            pltpu.VMEM((nstate * rows, LANES), BF16),
            pltpu.VMEM((reach, nstate * rows, LANES), BF16),
            pltpu.VMEM((rows, LANES), F32),
            pltpu.VMEM((reach, rows, LANES), F32),
            pltpu.VMEM((len(SLOTS), upper, LANES), BF16),
            pltpu.VMEM((len(SLOTS), depth - upper, LANES), BF16),
            pltpu.VMEM((toks, channels), BF16),
            pltpu.VMEM((CORES, xs_count, toks, block), BF16),
            pltpu.VMEM((xs_count, toks, block), BF16),
            pltpu.VMEM((xs_count, toks, block), BF16),
            pltpu.VMEM((xs_count - 1, toks, block), BF16),
            pltpu.VMEM((count, SLAB, block), BF16),
            pltpu.VMEM((count, SLAB, block), BF16),
            pltpu.VMEM((count, 8, LANES), F32),
            pltpu.VMEM((SLAB, width), BF16),
            pltpu.SemaphoreType.DMA((2 * reach + 1,)),
            pltpu.SemaphoreType.DMA((2 * reach + 1,)),
            pltpu.SemaphoreType.DMA((len(MESSAGES),)),
            pltpu.SemaphoreType.DMA((len(MESSAGES),)),
            pltpu.SemaphoreType.DMA((exp_sems,)),
            pltpu.SemaphoreType.DMA((exp_sems,)),
        ],
        compiler_params=pltpu.CompilerParams(
            collective_id=1, has_side_effects=True, vmem_limit_bytes=56 * 1024 * 1024
        ),
        name="mixer",
    )(
        mamba_in,
        bc_proj,
        tiles(decay),
        tiles(conv_w),
        tiles(mamba_vec),
        doc_len,
        residual,
        w_out,
        gain.reshape(1, width),
        routes,
    )


def experts_kernel(
    own_a,
    own_b,
    resid_ref,
    routes_ref,
    gate_ref,
    w1_ref,
    w2_ref,
    out_ref,
    held_a,
    held_b,
    outs_a,
    outs_b,
    sums_a,
    sums_b,
    w1,
    w2,
    rows_x,
    acc,
    hidden,
    few_acc,
    made_rows,
    sent,
    got,
    local_sems,
    send_sems,
    recv_sems,
    sum_send_sems,
    sum_recv_sems,
    out_send_sems,
    out_recv_sems,
):
    units, width = w2_ref.shape
    quarter = width // 4
    mains, rests = split_lanes(width)
    e = lax.axis_index("exp")
    count = lax.axis_size("exp")
    group_main = GROUP * CAP_MAIN
    group_rest = GROUP * 4

    loads = [
        pltpu.make_async_copy(w1_ref.at[0], w1.at[:, pl.ds(0, units)], local_sems.at[0]),
        pltpu.make_async_copy(w1_ref.at[1], w1.at[:, pl.ds(units, units)], local_sems.at[1]),
        pltpu.make_async_copy(w2_ref, w2, local_sems.at[2]),
    ]
    for load in loads:
        load.start()

    barrier = pltpu.get_barrier_semaphore()
    for axis in ("y", "z"):
        for way in (1, -1):
            pl.semaphore_signal(
                barrier, inc=1, device_id=seq_id(neighbour(axis, way)), device_id_type=MESH
            )
    for k in range(1, count):
        pl.semaphore_signal(
            barrier, inc=1, device_id=exp_id(lax.rem(e + k, count)), device_id_type=MESH
        )
    held, outs, sums = (held_a, held_b), (outs_a, outs_b), (sums_a, sums_b)
    held_a[0] = own_a[...]
    held_b[0] = own_b[...]
    pl.semaphore_wait(barrier, 4 + count - 1)

    def lanes(tree, part):
        total = 2 * mains[tree] + rests[tree]
        cut = total // 2 // LANES * LANES
        if part is None:
            return pl.ds(0, total)
        return pl.ds(0, cut) if part == 0 else pl.ds(cut, total - cut)

    def view_of(refs):
        return lambda tree, slot, part: refs[tree].at[slot, :, lanes(tree, part)]

    gather, gather_end = spread(view_of(held), send_sems, recv_sems)

    row = lax.broadcasted_iota(jnp.int32, (group_rest, group_rest * 4), 0)
    col = lax.broadcasted_iota(jnp.int32, (group_rest, group_rest * 4), 1)
    row_t = lax.broadcasted_iota(jnp.int32, (group_rest * 4, group_rest), 0)
    col_t = lax.broadcasted_iota(jnp.int32, (group_rest * 4, group_rest), 1)

    def pick(q):
        return one_hot(col == (row // 4) * 16 + q * 4 + row % 4)

    def put(q):
        return one_hot(row_t == (col_t // 4) * 16 + q * 4 + col_t % 4)

    half = width // 2
    members = GROUP * 16

    def feed(g):
        base = pl.ds(g * GROUP, GROUP)
        start = 0
        packed = []
        for tree in range(2):
            wide = mains[tree]
            for tile in range(2):
                rows_x[pl.ds(tile * members, members), pl.ds(start, wide)] = held[tree][
                    base, :, pl.ds(tile * wide, wide)
                ].reshape(members, wide)
            packed.append(
                held[tree][base, :, pl.ds(2 * wide, rests[tree])].reshape(members, rests[tree])
            )
            start += wide
        packed = jnp.concatenate(packed, axis=1)
        for q in range(4):
            rows_x[pl.ds(group_main, group_rest), pl.ds(q * quarter, quarter)] = dot(
                pick(q), packed
            ).astype(BF16)
        acc[...] = dot(rows_x[:, pl.ds(0, half)], w1[pl.ds(0, half), :])
        both = acc[...] + dot(rows_x[:, pl.ds(half, half)], w1[pl.ds(half, half), :])
        hidden[...] = (silu(both[:, :units]) * both[:, units:]).astype(BF16)

        start = 0
        for tree in range(2):
            wide = mains[tree]
            made = dot(hidden[...], w2[:, pl.ds(start, wide)]).astype(BF16)
            for tile in range(2):
                outs[tree][base, :, pl.ds(tile * wide, wide)] = made[
                    tile * members : (tile + 1) * members
                ].reshape(GROUP, 16, wide)
            few_acc[:, pl.ds(start, wide)] = made[group_main:]
            start += wide
        few = jnp.zeros((members, quarter), F32)
        for q in range(4):
            few = few + dot(put(q), few_acc[:, pl.ds(q * quarter, quarter)])
        few = few.astype(BF16)
        outs_a[base, :, pl.ds(2 * mains[0], rests[0])] = few[:, : rests[0]].reshape(
            GROUP, 16, rests[0]
        )
        outs_b[base, :, pl.ds(2 * mains[1], rests[1])] = few[:, rests[0] :].reshape(
            GROUP, 16, rests[1]
        )

    def when_full(g):
        if g == 0:
            for load in loads:
                load.wait()
        feed(g)

    gather(when_full)

    def add(tree, slot, child, part):
        here = lanes(tree, part)
        total = outs[tree][slot, :, here].astype(F32) + sums[tree][child, :, here].astype(F32)
        outs[tree][slot, :, here] = total.astype(BF16)

    reduce, reduce_end = gather_sum(
        view_of(outs), view_of(sums), add, sum_send_sems, sum_recv_sems
    )
    reduce()

    start = 0
    for tree in range(2):
        wide = mains[tree]
        for tile in range(2):
            made_rows[pl.ds(tile * 16, 16), pl.ds(start, wide)] = outs[tree][
                0, :, pl.ds(tile * wide, wide)
            ]
        start += wide
    packed = jnp.concatenate(
        [outs[tree][0, :, pl.ds(2 * mains[tree], rests[tree])] for tree in range(2)], axis=1
    )
    small_row = lax.broadcasted_iota(jnp.int32, (16, 16), 0)
    small_col = lax.broadcasted_iota(jnp.int32, (16, 16), 1)
    for q in range(4):
        choose = one_hot(jnp.logical_and(small_row < 4, small_col == q * 4 + small_row))
        made_rows[pl.ds(CAP_MAIN, 16), pl.ds(q * quarter, quarter)] = dot(choose, packed).astype(
            BF16
        )
    routes = routes_ref[...]
    gates = gate_ref[...]
    toks = routes.shape[0]
    table = slot_table(routes)
    mine_c = jnp.where(routes == e, gates, 0.0)
    weight = (mine_c[:, 0:1] + mine_c[:, 1:2]) * jnp.ones((1, LANES), F32)
    weight_t = weight.T
    lane = lax.broadcasted_iota(jnp.int32, (toks, LANES), 1)
    place = jnp.sum(jnp.where(lane == e, table, 0.0), axis=1, keepdims=True)
    place_t = (place * jnp.ones((1, LANES), F32)).T
    at = lax.broadcasted_iota(jnp.int32, (SLAB, toks), 0).astype(F32)
    mine = (at == place_t[0:1, :]).astype(F32)
    row_weight = jnp.sum(mine * weight_t[0:1, :], axis=1, keepdims=True)
    block = width // count
    for j in range(count):
        part = made_rows[:, pl.ds(j * block, block)].astype(F32)
        sent[j] = (row_weight * part).astype(BF16)

    def give(k):
        to = lax.rem(e + k, count)
        return pltpu.make_async_remote_copy(
            src_ref=sent.at[to],
            dst_ref=got.at[e],
            send_sem=out_send_sems.at[k - 1],
            recv_sem=out_recv_sems.at[k - 1],
            device_id=exp_id(to),
            device_id_type=MESH,
        )

    for k in range(1, count):
        give(k).start()
    got[e] = sent[e]
    for k in range(1, count):
        give(k).wait_recv()
    total = resid_ref[...]
    place_lane = lax.broadcasted_iota(jnp.int32, (toks, SLAB), 1).astype(F32)
    for j in range(count):
        total = total + dot(one_hot(place_lane == table[:, j : j + 1]), got[j])
    out_ref[...] = total.astype(BF16)

    gather_end()
    reduce_end()
    for k in range(1, count):
        give(k).wait_send()


def experts(own_a, own_b, resid, routes, gate_w, w1, w2):
    units, width = w2.shape
    count = lax.axis_size("exp")
    slots = len(SLOTS)
    sizes = [own_a.shape[1], own_b.shape[1]]
    group_rows = GROUP * (CAP_MAIN + 4)
    vmem = pl.BlockSpec(memory_space=pltpu.VMEM)
    hbm = pl.BlockSpec(memory_space=pl.ANY)
    return pl.pallas_call(
        experts_kernel,
        out_shape=jax.ShapeDtypeStruct(resid.shape, BF16),
        in_specs=[vmem] * 5 + [hbm, hbm],
        out_specs=vmem,
        scratch_shapes=[pltpu.VMEM((slots, 16, size), BF16) for _ in range(3) for size in sizes]
        + [
            pltpu.VMEM((width, 2 * units), BF16),
            pltpu.VMEM((units, width), BF16),
            pltpu.VMEM((group_rows, width), BF16),
            pltpu.VMEM((group_rows, 2 * units), F32),
            pltpu.VMEM((group_rows, units), BF16),
            pltpu.VMEM((GROUP * 4, width), BF16),
            pltpu.VMEM((SLAB, width), BF16),
            pltpu.VMEM((count, SLAB, width // count), BF16),
            pltpu.VMEM((count, SLAB, width // count), BF16),
            pltpu.SemaphoreType.DMA((3,)),
        ]
        + [pltpu.SemaphoreType.DMA((len(MESSAGES),)) for _ in range(4)]
        + [pltpu.SemaphoreType.DMA((count - 1,)) for _ in range(2)],
        compiler_params=pltpu.CompilerParams(
            collective_id=2, has_side_effects=True, vmem_limit_bytes=60 * 1024 * 1024
        ),
        name="experts",
    )(own_a, own_b, resid, routes, gate_w, w1, w2)


def shards(
    residual_in,
    mamba_in,
    bc_proj,
    decay,
    conv_w,
    mamba_vec,
    doc_len,
    w_out,
    norm_gain,
    routes,
    gate_w,
    w_gate_up,
    w_down,
):
    resid, own_a, own_b = mixer(
        mamba_in, bc_proj, decay, conv_w, mamba_vec, doc_len, residual_in, w_out, norm_gain, routes
    )
    return experts(own_a, own_b, resid, routes, gate_w, w_gate_up[0], w_down[0])


def solution(mesh):
    in_specs = (
        P("seq", None),
        P(None, "seq", "exp"),
        P(None, "seq"),
        P(None, "exp"),
        P(None, "exp"),
        P(None, "exp"),
        P(),
        P("exp", "seq"),
        P(),
        P("seq", None),
        P("seq", None),
        P("exp", None, None, "seq"),
        P("exp", "seq", None),
    )
    out_specs = P("seq", "exp")
    return jax.shard_map(shards, mesh=mesh, in_specs=in_specs, out_specs=out_specs, check_vma=False)
```

```python
import jax
import jax.numpy as jnp
from jax import lax
from jax.experimental import pallas as pl
from jax.experimental.pallas import tpu as pltpu
from jax.sharding import PartitionSpec as P

MESH = pl.DeviceIdType.MESH
LOG2E = 1.4426950408889634
LANES = 128
F32 = jnp.float32
BF16 = jnp.bfloat16
YS, ZS = 4, 8
CORES = 2
SLAB = 48
CAP_MAIN = 32

Y_OFFSETS = (0, 1, -1, 2)
Z_OFFSETS = (0, 1, -1, 2, -2, 3, -3, 4)
SLOTS = [(dy, dz) for dz in Z_OFFSETS for dy in Y_OFFSETS]
GROUP = 8


def far_steps(offset, size):
    top = size // 2
    if offset == 0:
        return [(1, 1, None), (-1, -1, None)]
    if offset == top:
        return []
    if offset > 0:
        return [(offset + 1, 1, 0 if offset + 1 == top else None)]
    return [(offset - 1, -1, None)] if offset - 1 > -top else [(top, -1, 1)]


def messages():
    found = []
    for tree in range(2):
        for dy, dz in SLOTS:
            if tree == 1 or dz == 0:
                for to, way, part in far_steps(dy, YS):
                    found.append((tree, (dy, dz), (to, dz), part, ("y", way)))
            if tree == 0 or dy == 0:
                for to, way, part in far_steps(dz, ZS):
                    found.append((tree, (dy, dz), (dy, to), part, ("z", way)))
    return found


MESSAGES = messages()
DEPTH = {slot: abs(slot[0]) + abs(slot[1]) for slot in SLOTS}
DEEPEST = max(DEPTH.values())


ORDER = [
    1, 2, 39, 40, 37, 38, 3, 4, -1, 5, 6, 7, -2, 8, -39, 43, 44, 45, -40, 50, -37, 41, -38, 42, 9,
    10, 48, 49, -3, -4, -5, -8, 13, 17, -6, -7, -43, 46, -44, 47, -45, 55, -50, 60, 53, 54, -41,
    -42, 11, 12, -48, 51, -49, 52, -9, -10, 14, 18, 58, 59, -13, -17, -46, -47, -55, 65, -60, 70,
    -53, 56, -54, 57, 15, 19, 63, 64, 21, 25, -11, -12, -51, -52, 16, 20, -58, 61, -59, 62, -14,
    -18, 68, 69, -65, -70, 22, 26, -56, -57, -15, -19, 23, 27, -63, 66, -64, 67, -21, -25, 29, 33,
    73, 74, -16, 24, -20, 28, -61, -62, -22, 30, -26, 34, -68, 71, -69, 72, -23, 31, -27, 35, -24,
    32, -28, 36, -73, 75, -74, 76, -66, -67, -29, -33, -30, -34, -71, -72, -31, -35, -32, -36, -75,
    -76,
]


def groups_full_at(at):
    last = {}
    for place, item in enumerate(ORDER):
        if item < 0:
            last[SLOTS.index(MESSAGES[-item - 1][2]) // GROUP] = place
    return [group for group in sorted(last) if last[group] == at]


def silu(v):
    return v / (1.0 + jnp.exp(-v))


def seq_id(index):
    return {"seq": index}


def exp_id(index):
    return {"exp": index}


def neighbour(axis, way):
    me = lax.axis_index("seq")
    y, z = me // ZS, me % ZS
    if axis == "y":
        return ((y + way + YS) % YS) * ZS + z
    return y * ZS + (z + way + ZS) % ZS


def spread(view, send_sems, recv_sems):
    def copy(k):
        tree, source, target, part, way = MESSAGES[k]
        return pltpu.make_async_remote_copy(
            src_ref=view(tree, SLOTS.index(source), part),
            dst_ref=view(tree, SLOTS.index(target), part),
            send_sem=send_sems.at[k],
            recv_sem=recv_sems.at[k],
            device_id=seq_id(neighbour(*way)),
            device_id_type=MESH,
        )

    def run(when_full, start=0, stop=len(ORDER)):
        for at in range(start, stop):
            item = ORDER[at]
            if item > 0:
                copy(item - 1).start()
            else:
                copy(-item - 1).wait_recv()
                for group in groups_full_at(at):
                    when_full(group)

    def finish():
        for k in range(len(MESSAGES)):
            copy(k).wait_send()

    return run, finish


def gather_sum(view, landing, add, send_sems, recv_sems):
    def copy(k):
        tree, _, child, part, (axis, way) = MESSAGES[k]
        return pltpu.make_async_remote_copy(
            src_ref=view(tree, SLOTS.index(child), part),
            dst_ref=landing(tree, SLOTS.index(child), part),
            send_sem=send_sems.at[k],
            recv_sem=recv_sems.at[k],
            device_id=seq_id(neighbour(axis, -way)),
            device_id_type=MESH,
        )

    def run():
        for item in reversed(ORDER):
            k = abs(item) - 1
            if item < 0:
                copy(k).start()
            else:
                copy(k).wait_recv()
                _, parent, child, part, _ = MESSAGES[k]
                add(MESSAGES[k][0], SLOTS.index(parent), SLOTS.index(child), part)

    def finish():
        for k in range(len(MESSAGES)):
            copy(k).wait_send()

    return run, finish


def dot(a, b):
    return jnp.dot(a, b, preferred_element_type=F32)


def one_hot(condition):
    return condition.astype(F32).astype(BF16)


def slot_table(routes_t):
    toks = routes_t.shape[1]
    expert = lax.broadcasted_iota(jnp.int32, (LANES, toks), 0)
    hits = jnp.logical_or(routes_t[0:1, :] == expert, routes_t[1:2, :] == expert)
    row = lax.broadcasted_iota(jnp.int32, (toks, toks), 0)
    col = lax.broadcasted_iota(jnp.int32, (toks, toks), 1)
    places = dot(one_hot(hits), one_hot(row <= col)) - 1.0
    return jnp.where(hits, places, -1.0)


def places_of(table_t, expert):
    place = lax.broadcasted_iota(jnp.int32, (SLAB, table_t.shape[1]), 0).astype(F32)
    return (place == table_t[expert : expert + 1, :]).astype(F32)


def split_lanes(width):
    first = (width * 13 // 32) // LANES * LANES
    quarter = width // 4
    rest = (quarter * 13 // 32) // LANES * LANES
    return (first, width - first), (rest, quarter - rest)


CHUNKS = 4
SHARES = [6, 8, 10, 14, 18, 40, 50, 56, 62, 68]
LATE_SHARES = [76, 84, 92, 98]


def mixer_kernel(
    mamba_ref,
    bc_ref,
    decay_ref,
    conv_ref,
    vec_ref,
    doc_ref,
    residual_ref,
    w_ref,
    gain_ref,
    routes_ref,
    resid_ref,
    own_a,
    own_b,
    xs,
    dts,
    us,
    zs,
    neg,
    tail,
    end_out,
    end_in,
    start_out,
    start_in,
    held_a,
    held_b,
    gated,
    partial,
    pair_in,
    pair_sum,
    cross_in,
    disp,
    disp_in,
    squares,
    rows_n,
    send_sems,
    recv_sems,
    w_send_sems,
    w_recv_sems,
    exp_send_sems,
    exp_recv_sems,
):
    count = lax.axis_size("seq")
    me = lax.axis_index("seq")
    toks = mamba_ref.shape[1]
    blocks = mamba_ref.shape[2] // LANES
    nstate = decay_ref.shape[0]
    rows = blocks
    first = me * toks
    e = lax.axis_index("exp")
    experts_count = lax.axis_size("exp")
    x, core = e // CORES, e % CORES
    xs_count = experts_count // CORES

    barrier = pltpu.get_barrier_semaphore()

    def greet(step, _):
        pl.semaphore_signal(
            barrier, inc=1, device_id=seq_id(lax.rem(me + step, count)), device_id_type=MESH
        )
        return 0

    lax.fori_loop(1, count, greet, 0)
    for step in range(1, experts_count):
        pl.semaphore_signal(
            barrier,
            inc=1,
            device_id=exp_id(lax.rem(e + step, experts_count)),
            device_id_type=MESH,
        )

    depth = w_ref.shape[0]
    upper = held_a.shape[1]
    held_a[0] = w_ref[pl.ds(0, upper), :]
    held_b[0] = w_ref[pl.ds(upper, depth - upper), :]
    for j in range(blocks):
        lanes = pl.ds(j * LANES, LANES)
        xs[pl.ds(8 * rows + j, toks, stride=rows), :] = mamba_ref[0, :, lanes].astype(F32)
        zs[pl.ds(j, toks, stride=rows), :] = mamba_ref[1, :, lanes].astype(F32)
        dts[pl.ds(j, toks, stride=rows), :] = mamba_ref[2, :, lanes].astype(F32)
    pl.semaphore_wait(barrier, count - 1 + experts_count - 1)

    def held_view(tree, slot, part):
        ref = (held_a, held_b)[tree]
        size = ref.shape[1]
        if part is None:
            return ref.at[slot]
        return ref.at[slot, pl.ds(part * (size // 2), size // 2)]

    gather, gather_end = spread(held_view, w_send_sems, w_recv_sems)
    tail_copy = pltpu.make_async_remote_copy(
        src_ref=mamba_ref.at[0, pl.ds(toks - 16, 16)],
        dst_ref=tail,
        send_sem=send_sems.at[0],
        recv_sem=recv_sems.at[0],
        device_id=seq_id(lax.rem(me + 1, count)),
        device_id_type=MESH,
    )
    tail_copy.start()

    waiting = []
    reached = [0]

    def product(group):
        for pair in range(GROUP // 2):
            first_slot = group * GROUP + 2 * pair
            sides = [
                jnp.concatenate([held_a[first_slot + n], held_b[first_slot + n]], axis=0)
                for n in range(2)
            ]
            made = dot(gated[...], jnp.concatenate(sides, axis=1)).astype(BF16)
            for n in range(2):
                dy, dz = SLOTS[first_slot + n]
                y, z = me // ZS, me % ZS
                owner = ((y - dy + YS) % YS) * ZS + (z - dz + ZS) % ZS
                block = owner // tiles_per
                lane = pl.multiple_of((owner % tiles_per) * LANES, LANES)
                partial[block % CORES, block // CORES, :, pl.ds(lane, LANES)] = made[
                    :, n * LANES : (n + 1) * LANES
                ]

    tiles_per = resid_ref.shape[1] // LANES

    def forward(share, act=False):
        stop = len(ORDER) * share // 100
        gather(product if act else waiting.append, reached[0], stop)
        reached[0] = stop

    forward(SHARES[0])
    for j in range(blocks):
        lanes = pl.ds(j * LANES, LANES)
        neg[pl.ds(j, nstate, stride=rows), :] = decay_ref[:, lanes] * (-LOG2E)

    def tile_row(ref, n):
        return jnp.concatenate(
            [ref[n : n + 1, j * LANES : (j + 1) * LANES] for j in range(blocks)], axis=0
        )

    step_bias = tile_row(vec_ref, 1)

    def tok(t):
        return pl.ds(pl.multiple_of(t * rows, rows), rows)

    def prepare(t, total):
        raw = dts[tok(t), :] + step_bias
        step = jnp.maximum(raw, 0.0) + jnp.log1p(jnp.exp(-jnp.abs(raw)))
        dts[tok(t), :] = step
        zs[tok(t), :] = silu(zs[tok(t), :])
        return total + step

    total_step = lax.fori_loop(0, toks, prepare, jnp.zeros((rows, LANES), F32), unroll=8)

    forward(SHARES[1])
    tail_copy.wait()
    there = jnp.where(me > 0, jnp.float32(1.0), jnp.float32(0.0))
    for j in range(blocks):
        rest = tail[:, pl.ds(j * LANES, LANES)].astype(F32) * there
        xs[pl.ds(j, 8, stride=rows), :] = rest[8:16, :]

    ends = []
    so_far = jnp.int32(0)
    for j in range(doc_ref.shape[0]):
        so_far = so_far + doc_ref[j]
        ends.append(so_far)

    def goes_on(position):
        keep = jnp.float32(1.0)
        for end in ends:
            keep = jnp.where(end == position, jnp.float32(0.0), keep)
        return keep

    taps = [tile_row(conv_ref, k) for k in range(conv_ref.shape[0])]
    conv_bias = tile_row(vec_ref, 0)

    def advance(t, states, keep, step, drive):
        new = []
        for n in range(nstate):
            growth = jnp.exp2(step * neg[pl.ds(n * rows, rows), :]) * keep
            new.append(growth * states[n] + drive * bc_ref[n, t])
        return tuple(new)

    def local_pass(t, carry):
        states, before, before2 = carry
        keep = goes_on(first + t)
        x0, x1, x2, x3 = [xs[tok(t + 8 - 3 + k), :] for k in range(4)]
        v2 = keep
        v1 = keep * before
        v0 = v1 * before2
        total = conv_bias + (taps[0] * x0) * v0 + (taps[1] * x1) * v1
        total = total + (taps[2] * x2) * v2 + taps[3] * x3
        u_row = silu(total)
        us[tok(t), :] = u_row
        step = dts[tok(t), :]
        return advance(t, states, keep, step, step * u_row), keep, before

    zero = tuple(jnp.zeros((rows, LANES), F32) for _ in range(nstate))
    carry = (zero, goes_on(first - 1), goes_on(first - 2))
    for i in range(CHUNKS):
        carry = lax.fori_loop(
            i * toks // CHUNKS, (i + 1) * toks // CHUNKS, local_pass, carry, unroll=2
        )
        if i < CHUNKS - 1:
            forward(SHARES[2 + i])
    states = carry[0]
    high = total_step.astype(BF16)
    low = (total_step - high.astype(F32)).astype(BF16)
    for n in range(0, nstate, 2):
        pair = jnp.concatenate([states[n], states[n + 1]], axis=0).astype(BF16)
        end_out[n // 2] = jnp.concatenate([pair, high, low], axis=0)
    y, z = me // ZS, me % ZS
    before = 2
    end_in[before * ZS + z] = end_out[z]

    def scatter(i):
        row, step = i // ZS, i % ZS
        holder = lax.rem(z + step, ZS)
        return pltpu.make_async_remote_copy(
            src_ref=end_out.at[holder],
            dst_ref=end_in.at[(before - row) * ZS + z],
            send_sem=send_sems.at[i],
            recv_sem=recv_sems.at[i],
            device_id=seq_id(lax.rem(y + row, YS) * ZS + holder),
            device_id_type=MESH,
        )

    def give_back(step):
        return pltpu.make_async_remote_copy(
            src_ref=start_out.at[lax.rem(z + step, ZS)],
            dst_ref=start_in.at[z],
            send_sem=send_sems.at[(before + 1) * ZS + step],
            recv_sem=recv_sems.at[(before + 1) * ZS + step],
            device_id=seq_id(y * ZS + lax.rem(z + step, ZS)),
            device_id_type=MESH,
        )

    def send(i, _):
        scatter(i).start()
        return 0

    later = jnp.minimum(before + 1, YS - y) * ZS
    earlier = jnp.minimum(before, y)
    lax.fori_loop(1, later, send, 0)
    forward(SHARES[1 + CHUNKS])

    def arrive(i, _):
        scatter(i).wait_recv()
        return 0

    lax.fori_loop(1, (earlier + 1) * ZS, arrive, 0)

    def fold(at, held):
        begin = ((y - before) * ZS + at) * toks
        unbroken = jnp.float32(1.0)
        for end in ends:
            inside = jnp.logical_and(end >= begin, end < begin + toks)
            unbroken = jnp.where(inside, jnp.float32(0.0), unbroken)
        halves = end_in[at, pl.ds(2 * rows, 2 * rows), :].astype(F32)
        sums = halves[:rows] + halves[rows:]
        pair = end_in[at, pl.ds(0, 2 * rows), :].astype(F32)
        new = []
        for n in range(2):
            rate = neg[pl.ds(pl.multiple_of((2 * z + n) * rows, rows), rows), :]
            growth = jnp.exp2(sums * rate) * unbroken
            new.append(growth * held[n] + pair[n * rows : (n + 1) * rows, :])
        return tuple(new)

    def fold_own(at, held):
        start_out[at - before * ZS] = jnp.concatenate(held, axis=0).astype(BF16)
        return fold(at, held)

    held = lax.fori_loop((before - earlier) * ZS, before * ZS, fold, zero[:2])
    lax.fori_loop(before * ZS, (before + 1) * ZS, fold_own, held)

    def return_start(step, _):
        give_back(step).start()
        return 0

    lax.fori_loop(1, ZS, return_start, 0)
    start_in[z] = start_out[z]
    forward(SHARES[2 + CHUNKS])

    def return_arrive(step, _):
        give_back(step).wait_recv()
        return 0

    lax.fori_loop(1, ZS, return_arrive, 0)
    entering = []
    for n in range(0, nstate, 2):
        pair = start_in[n // 2].astype(F32)
        entering += [pair[:rows], pair[rows:]]
    entering = tuple(entering)
    skip = tile_row(vec_ref, 2)

    def full_pass(t, states):
        keep = goes_on(first + t)
        u_row = us[tok(t), :]
        step = dts[tok(t), :]
        states = advance(t, states, keep, step, step * u_row)
        total = skip * u_row
        for n in range(nstate):
            total = total + states[n] * bc_ref[nstate + n, t]
        zs[tok(t), :] = zs[tok(t), :] * total
        return states

    states = entering
    for i in range(CHUNKS):
        states = lax.fori_loop(
            i * toks // CHUNKS, (i + 1) * toks // CHUNKS, full_pass, states, unroll=2
        )
        if i < CHUNKS - 1:
            forward(SHARES[3 + CHUNKS + i])
    for j in range(blocks):
        gated[:, pl.ds(j * LANES, LANES)] = zs[pl.ds(j, toks, stride=rows), :].astype(BF16)
    for i, group in enumerate(list(waiting)):
        product(group)
        forward(LATE_SHARES[i], act=True)
    table_t = slot_table(routes_ref[...])
    forward(100, act=True)

    def pair_copy(k):
        to = lax.rem(x + k, xs_count)
        return pltpu.make_async_remote_copy(
            src_ref=partial.at[1 - core, to],
            dst_ref=pair_in.at[to],
            send_sem=exp_send_sems.at[k],
            recv_sem=exp_recv_sems.at[k],
            device_id=exp_id(x * CORES + 1 - core),
            device_id_type=MESH,
        )

    def cross_copy(k):
        to = lax.rem(x + k, xs_count)
        return pltpu.make_async_remote_copy(
            src_ref=pair_sum.at[to],
            dst_ref=cross_in.at[k - 1],
            send_sem=exp_send_sems.at[xs_count + k],
            recv_sem=exp_recv_sems.at[xs_count + k],
            device_id=exp_id(to * CORES + core),
            device_id_type=MESH,
        )

    order = [2, 1, 3, 0]
    for k in order:
        pair_copy(k).start()
    for k in order:
        pair_copy(k).wait_recv()
        to = lax.rem(x + k, xs_count)
        total = partial[core, to].astype(F32) + pair_in[to].astype(F32)
        if k > 0:
            pair_sum[to] = total.astype(BF16)
            cross_copy(k).start()
    width = residual_ref.shape[1]
    block = width // experts_count
    total = total + residual_ref[:, pl.ds(pl.multiple_of(e * block, block), block)].astype(F32)
    for k in (1, 3, 2):
        cross_copy(k).wait_recv()
        total = total + cross_in[k - 1].astype(F32)
    resid_ref[...] = total

    square = jnp.sum(total * total, axis=1, keepdims=True)
    squares[e] = (square * jnp.ones((1, LANES), F32)).T[0:8, :]
    sent_rows = total.astype(BF16)
    for j in range(experts_count):
        disp[j] = dot(places_of(table_t, j).astype(BF16), sent_rows).astype(BF16)

    def deal(k):
        to = lax.rem(e + k, experts_count)
        base = 2 * xs_count + 2 * (k - 1)
        return [
            pltpu.make_async_remote_copy(
                src_ref=source,
                dst_ref=target,
                send_sem=exp_send_sems.at[base + i],
                recv_sem=exp_recv_sems.at[base + i],
                device_id=exp_id(to),
                device_id_type=MESH,
            )
            for i, (source, target) in enumerate(
                [(disp.at[to], disp_in.at[e]), (squares.at[e], squares.at[e])]
            )
        ]

    for k in range(1, experts_count):
        for copy in deal(k):
            copy.start()
    disp_in[e] = disp[e]
    expert_row = lax.broadcasted_iota(jnp.int32, (LANES, toks), 0)
    place_t = jnp.sum(jnp.where(expert_row == e, table_t, 0.0), axis=0, keepdims=True)
    at = lax.broadcasted_iota(jnp.int32, (SLAB, toks), 0).astype(F32)
    mine = (at == place_t).astype(F32)
    for k in range(1, experts_count):
        for copy in deal(k):
            copy.wait_recv()
    mean = squares[0]
    for j in range(1, experts_count):
        mean = mean + squares[j]
    inverse = lax.rsqrt(mean * (1.0 / width) + 1e-05)
    scale = jnp.sum(mine * inverse[0:1, :], axis=1, keepdims=True)
    for j in range(experts_count):
        here = pl.ds(j * block, block)
        rows_n[:, here] = (disp_in[j].astype(F32) * scale * gain_ref[:, here]).astype(BF16)
    mains, rests = split_lanes(width)
    quarter = width // 4
    small_row = lax.broadcasted_iota(jnp.int32, (16, 16), 0)
    small_col = lax.broadcasted_iota(jnp.int32, (16, 16), 1)
    packed = jnp.zeros((16, quarter), F32)
    for q in range(4):
        choose = one_hot(jnp.logical_and(small_col < 4, small_row == q * 4 + small_col))
        packed = packed + dot(choose, rows_n[pl.ds(CAP_MAIN, 16), pl.ds(q * quarter, quarter)])
    packed = packed.astype(BF16)
    start = 0
    rest_start = 0
    for tree, own in enumerate((own_a, own_b)):
        wide = mains[tree]
        for tile in range(2):
            own[:, pl.ds(tile * wide, wide)] = rows_n[pl.ds(tile * 16, 16), pl.ds(start, wide)]
        own[:, pl.ds(2 * wide, rests[tree])] = packed[:, rest_start : rest_start + rests[tree]]
        start += wide
        rest_start += rests[tree]

    def sent(i, _):
        scatter(i).wait_send()
        return 0

    lax.fori_loop(1, later, sent, 0)

    def returned(step, _):
        give_back(step).wait_send()
        return 0

    lax.fori_loop(1, ZS, returned, 0)
    gather_end()
    for k in range(xs_count):
        pair_copy(k).wait_send()
        if k > 0:
            cross_copy(k).wait_send()
    for k in range(1, experts_count):
        for copy in deal(k):
            copy.wait_send()


def mixer(mamba_in, bc_proj, decay, conv_w, mamba_vec, doc_len, residual, w_out, gain, routes):
    toks, channels = mamba_in.shape[1:]
    nstate = decay.shape[0]
    rows = channels // LANES
    width = residual.shape[1]
    count = lax.axis_size("exp")
    block = width // count
    depth = w_out.shape[0]
    upper = depth * 13 // 32 // 32 * 32
    mains, rests = split_lanes(width)
    sizes = [2 * main + rest for main, rest in zip(mains, rests)]
    xs_count = count // CORES
    exp_sems = 2 * xs_count + 2 * (count - 1)
    vmem = pl.BlockSpec(memory_space=pltpu.VMEM)
    smem = pl.BlockSpec(memory_space=pltpu.SMEM)
    return pl.pallas_call(
        mixer_kernel,
        out_shape=[jax.ShapeDtypeStruct((toks, block), F32)]
        + [jax.ShapeDtypeStruct((16, size), BF16) for size in sizes],
        in_specs=[vmem, smem, vmem, vmem, vmem, smem, vmem, vmem, vmem, vmem],
        out_specs=[vmem] * 3,
        scratch_shapes=[
            pltpu.VMEM(((toks + 8) * rows, LANES), F32),
            pltpu.VMEM((toks * rows, LANES), F32),
            pltpu.VMEM((toks * rows, LANES), F32),
            pltpu.VMEM((toks * rows, LANES), F32),
            pltpu.VMEM((nstate * rows, LANES), F32),
            pltpu.VMEM((16, channels), BF16),
            pltpu.VMEM((ZS, 4 * rows, LANES), BF16),
            pltpu.VMEM((3 * ZS, 4 * rows, LANES), BF16),
            pltpu.VMEM((ZS, 2 * rows, LANES), BF16),
            pltpu.VMEM((ZS, 2 * rows, LANES), BF16),
            pltpu.VMEM((len(SLOTS), upper, LANES), BF16),
            pltpu.VMEM((len(SLOTS), depth - upper, LANES), BF16),
            pltpu.VMEM((toks, channels), BF16),
            pltpu.VMEM((CORES, xs_count, toks, block), BF16),
            pltpu.VMEM((xs_count, toks, block), BF16),
            pltpu.VMEM((xs_count, toks, block), BF16),
            pltpu.VMEM((xs_count - 1, toks, block), BF16),
            pltpu.VMEM((count, SLAB, block), BF16),
            pltpu.VMEM((count, SLAB, block), BF16),
            pltpu.VMEM((count, 8, LANES), F32),
            pltpu.VMEM((SLAB, width), BF16),
            pltpu.SemaphoreType.DMA((4 * ZS,)),
            pltpu.SemaphoreType.DMA((4 * ZS,)),
            pltpu.SemaphoreType.DMA((len(MESSAGES),)),
            pltpu.SemaphoreType.DMA((len(MESSAGES),)),
            pltpu.SemaphoreType.DMA((exp_sems,)),
            pltpu.SemaphoreType.DMA((exp_sems,)),
        ],
        compiler_params=pltpu.CompilerParams(
            collective_id=1, has_side_effects=True, vmem_limit_bytes=56 * 1024 * 1024
        ),
        name="mixer",
    )(
        mamba_in,
        bc_proj,
        decay,
        conv_w,
        mamba_vec,
        doc_len,
        residual,
        w_out,
        gain.reshape(1, width),
        routes,
    )


def experts_kernel(
    own_a,
    own_b,
    resid_ref,
    routes_ref,
    gate_ref,
    w1_ref,
    w2_ref,
    out_ref,
    held_a,
    held_b,
    outs_a,
    outs_b,
    sums_a,
    sums_b,
    w1,
    w2,
    rows_x,
    acc,
    hidden,
    few_acc,
    made_rows,
    sent,
    got,
    local_sems,
    send_sems,
    recv_sems,
    sum_send_sems,
    sum_recv_sems,
    out_send_sems,
    out_recv_sems,
):
    units, width = w2_ref.shape
    quarter = width // 4
    mains, rests = split_lanes(width)
    e = lax.axis_index("exp")
    count = lax.axis_size("exp")
    group_main = GROUP * CAP_MAIN
    group_rest = GROUP * 4

    loads = [
        pltpu.make_async_copy(w1_ref.at[0], w1.at[:, pl.ds(0, units)], local_sems.at[0]),
        pltpu.make_async_copy(w1_ref.at[1], w1.at[:, pl.ds(units, units)], local_sems.at[1]),
        pltpu.make_async_copy(w2_ref, w2, local_sems.at[2]),
    ]
    for load in loads:
        load.start()

    barrier = pltpu.get_barrier_semaphore()
    for axis in ("y", "z"):
        for way in (1, -1):
            pl.semaphore_signal(
                barrier, inc=1, device_id=seq_id(neighbour(axis, way)), device_id_type=MESH
            )
    for k in range(1, count):
        pl.semaphore_signal(
            barrier, inc=1, device_id=exp_id(lax.rem(e + k, count)), device_id_type=MESH
        )
    held, outs, sums = (held_a, held_b), (outs_a, outs_b), (sums_a, sums_b)
    held_a[0] = own_a[...]
    held_b[0] = own_b[...]
    pl.semaphore_wait(barrier, 4 + count - 1)

    def lanes(tree, part):
        total = 2 * mains[tree] + rests[tree]
        cut = total // 2 // LANES * LANES
        if part is None:
            return pl.ds(0, total)
        return pl.ds(0, cut) if part == 0 else pl.ds(cut, total - cut)

    def view_of(refs):
        return lambda tree, slot, part: refs[tree].at[slot, :, lanes(tree, part)]

    gather, gather_end = spread(view_of(held), send_sems, recv_sems)

    row = lax.broadcasted_iota(jnp.int32, (group_rest, group_rest * 4), 0)
    col = lax.broadcasted_iota(jnp.int32, (group_rest, group_rest * 4), 1)
    row_t = lax.broadcasted_iota(jnp.int32, (group_rest * 4, group_rest), 0)
    col_t = lax.broadcasted_iota(jnp.int32, (group_rest * 4, group_rest), 1)

    def pick(q):
        return one_hot(col == (row // 4) * 16 + q * 4 + row % 4)

    def put(q):
        return one_hot(row_t == (col_t // 4) * 16 + q * 4 + col_t % 4)

    half = width // 2
    members = GROUP * 16

    def feed(g):
        base = pl.ds(g * GROUP, GROUP)
        start = 0
        packed = []
        for tree in range(2):
            wide = mains[tree]
            for tile in range(2):
                rows_x[pl.ds(tile * members, members), pl.ds(start, wide)] = held[tree][
                    base, :, pl.ds(tile * wide, wide)
                ].reshape(members, wide)
            packed.append(
                held[tree][base, :, pl.ds(2 * wide, rests[tree])].reshape(members, rests[tree])
            )
            start += wide
        packed = jnp.concatenate(packed, axis=1)
        for q in range(4):
            rows_x[pl.ds(group_main, group_rest), pl.ds(q * quarter, quarter)] = dot(
                pick(q), packed
            ).astype(BF16)
        acc[...] = dot(rows_x[:, pl.ds(0, half)], w1[pl.ds(0, half), :])
        both = acc[...] + dot(rows_x[:, pl.ds(half, half)], w1[pl.ds(half, half), :])
        hidden[...] = (silu(both[:, :units]) * both[:, units:]).astype(BF16)

        start = 0
        for tree in range(2):
            wide = mains[tree]
            made = dot(hidden[...], w2[:, pl.ds(start, wide)]).astype(BF16)
            for tile in range(2):
                outs[tree][base, :, pl.ds(tile * wide, wide)] = made[
                    tile * members : (tile + 1) * members
                ].reshape(GROUP, 16, wide)
            few_acc[:, pl.ds(start, wide)] = made[group_main:]
            start += wide
        few = jnp.zeros((members, quarter), F32)
        for q in range(4):
            few = few + dot(put(q), few_acc[:, pl.ds(q * quarter, quarter)])
        few = few.astype(BF16)
        outs_a[base, :, pl.ds(2 * mains[0], rests[0])] = few[:, : rests[0]].reshape(
            GROUP, 16, rests[0]
        )
        outs_b[base, :, pl.ds(2 * mains[1], rests[1])] = few[:, rests[0] :].reshape(
            GROUP, 16, rests[1]
        )

    def when_full(g):
        if g == 0:
            for load in loads:
                load.wait()
        feed(g)

    gather(when_full)

    def add(tree, slot, child, part):
        here = lanes(tree, part)
        total = outs[tree][slot, :, here].astype(F32) + sums[tree][child, :, here].astype(F32)
        outs[tree][slot, :, here] = total.astype(BF16)

    reduce, reduce_end = gather_sum(
        view_of(outs), view_of(sums), add, sum_send_sems, sum_recv_sems
    )
    reduce()

    start = 0
    for tree in range(2):
        wide = mains[tree]
        for tile in range(2):
            made_rows[pl.ds(tile * 16, 16), pl.ds(start, wide)] = outs[tree][
                0, :, pl.ds(tile * wide, wide)
            ]
        start += wide
    packed = jnp.concatenate(
        [outs[tree][0, :, pl.ds(2 * mains[tree], rests[tree])] for tree in range(2)], axis=1
    )
    small_row = lax.broadcasted_iota(jnp.int32, (16, 16), 0)
    small_col = lax.broadcasted_iota(jnp.int32, (16, 16), 1)
    for q in range(4):
        choose = one_hot(jnp.logical_and(small_row < 4, small_col == q * 4 + small_row))
        made_rows[pl.ds(CAP_MAIN, 16), pl.ds(q * quarter, quarter)] = dot(choose, packed).astype(
            BF16
        )
    routes_t = routes_ref[...]
    toks = routes_t.shape[1]
    table_t = slot_table(routes_t)
    table = table_t.T
    chosen = jnp.where(routes_t == e, gate_ref[...], 0.0)
    weight_t = chosen[0:1, :] + chosen[1:2, :]
    expert_row = lax.broadcasted_iota(jnp.int32, (LANES, toks), 0)
    place_t = jnp.sum(jnp.where(expert_row == e, table_t, 0.0), axis=0, keepdims=True)
    at = lax.broadcasted_iota(jnp.int32, (SLAB, toks), 0).astype(F32)
    mine = (at == place_t).astype(F32)
    row_weight = jnp.sum(mine * weight_t, axis=1, keepdims=True)
    block = width // count
    for j in range(count):
        part = made_rows[:, pl.ds(j * block, block)].astype(F32)
        sent[j] = (row_weight * part).astype(BF16)

    def give(k):
        to = lax.rem(e + k, count)
        return pltpu.make_async_remote_copy(
            src_ref=sent.at[to],
            dst_ref=got.at[e],
            send_sem=out_send_sems.at[k - 1],
            recv_sem=out_recv_sems.at[k - 1],
            device_id=exp_id(to),
            device_id_type=MESH,
        )

    for k in range(1, count):
        give(k).start()
    got[e] = sent[e]
    for k in range(1, count):
        give(k).wait_recv()
    total = resid_ref[...]
    place_lane = lax.broadcasted_iota(jnp.int32, (toks, SLAB), 1).astype(F32)
    for j in range(count):
        total = total + dot(one_hot(place_lane == table[:, j : j + 1]), got[j])
    out_ref[...] = total.astype(BF16)

    gather_end()
    reduce_end()
    for k in range(1, count):
        give(k).wait_send()


def experts(own_a, own_b, resid, routes, gate_w, w1, w2):
    units, width = w2.shape
    count = lax.axis_size("exp")
    slots = len(SLOTS)
    sizes = [own_a.shape[1], own_b.shape[1]]
    group_rows = GROUP * (CAP_MAIN + 4)
    vmem = pl.BlockSpec(memory_space=pltpu.VMEM)
    hbm = pl.BlockSpec(memory_space=pl.ANY)
    return pl.pallas_call(
        experts_kernel,
        out_shape=jax.ShapeDtypeStruct(resid.shape, BF16),
        in_specs=[vmem] * 5 + [hbm, hbm],
        out_specs=vmem,
        scratch_shapes=[pltpu.VMEM((slots, 16, size), BF16) for _ in range(3) for size in sizes]
        + [
            pltpu.VMEM((width, 2 * units), BF16),
            pltpu.VMEM((units, width), BF16),
            pltpu.VMEM((group_rows, width), BF16),
            pltpu.VMEM((group_rows, 2 * units), F32),
            pltpu.VMEM((group_rows, units), BF16),
            pltpu.VMEM((GROUP * 4, width), BF16),
            pltpu.VMEM((SLAB, width), BF16),
            pltpu.VMEM((count, SLAB, width // count), BF16),
            pltpu.VMEM((count, SLAB, width // count), BF16),
            pltpu.SemaphoreType.DMA((3,)),
        ]
        + [pltpu.SemaphoreType.DMA((len(MESSAGES),)) for _ in range(4)]
        + [pltpu.SemaphoreType.DMA((count - 1,)) for _ in range(2)],
        compiler_params=pltpu.CompilerParams(
            collective_id=2, has_side_effects=True, vmem_limit_bytes=60 * 1024 * 1024
        ),
        name="experts",
    )(own_a, own_b, resid, routes, gate_w, w1, w2)


def shards(
    residual_in,
    mamba_in,
    bc_proj,
    decay,
    conv_w,
    mamba_vec,
    doc_len,
    w_out,
    norm_gain,
    routes,
    gate_w,
    w_gate_up,
    w_down,
):
    resid, own_a, own_b = mixer(
        mamba_in,
        bc_proj,
        decay,
        conv_w,
        mamba_vec,
        doc_len,
        residual_in,
        w_out,
        norm_gain,
        routes.T,
    )
    return experts(own_a, own_b, resid, routes.T, gate_w.T, w_gate_up[0], w_down[0])


def solution(mesh):
    in_specs = (
        P("seq", None),
        P(None, "seq", "exp"),
        P(None, "seq"),
        P(None, "exp"),
        P(None, "exp"),
        P(None, "exp"),
        P(),
        P("exp", "seq"),
        P(),
        P("seq", None),
        P("seq", None),
        P("exp", None, None, "seq"),
        P("exp", "seq", None),
    )
    out_specs = P("seq", "exp")
    return jax.shard_map(shards, mesh=mesh, in_specs=in_specs, out_specs=out_specs, check_vma=False)
```

```python
import jax
import jax.numpy as jnp
from jax import lax
from jax.experimental import pallas as pl
from jax.experimental.pallas import tpu as pltpu
from jax.sharding import PartitionSpec as P

MESH = pl.DeviceIdType.MESH
LOG2E = 1.4426950408889634
LANES = 128
F32 = jnp.float32
BF16 = jnp.bfloat16
YS, ZS = 4, 8
CORES = 2
SLAB = 48
CAP_MAIN = 32

Y_OFFSETS = (0, 1, -1, 2)
Z_OFFSETS = (0, 1, -1, 2, -2, 3, -3, 4)
SLOTS = [(dy, dz) for dz in Z_OFFSETS for dy in Y_OFFSETS]
GROUP = 8


def far_steps(offset, size):
    top = size // 2
    if offset == 0:
        return [(1, 1, None), (-1, -1, None)]
    if offset == top:
        return []
    if offset > 0:
        return [(offset + 1, 1, 0 if offset + 1 == top else None)]
    return [(offset - 1, -1, None)] if offset - 1 > -top else [(top, -1, 1)]


def messages():
    found = []
    for tree in range(2):
        for dy, dz in SLOTS:
            if tree == 1 or dz == 0:
                for to, way, part in far_steps(dy, YS):
                    found.append((tree, (dy, dz), (to, dz), part, ("y", way)))
            if tree == 0 or dy == 0:
                for to, way, part in far_steps(dz, ZS):
                    found.append((tree, (dy, dz), (dy, to), part, ("z", way)))
    return found


MESSAGES = messages()
DEPTH = {slot: abs(slot[0]) + abs(slot[1]) for slot in SLOTS}
DEEPEST = max(DEPTH.values())


ORDER = [
    1, 2, 39, 40, 37, 38, 3, 4, -1, 5, 6, 7, -2, 8, -39, 43, 44, 45, -40, 50, -37, 41, -38, 42, 9,
    10, 48, 49, -3, -4, -5, -8, 13, 17, -6, -7, -43, 46, -44, 47, -45, 55, -50, 60, 53, 54, -41,
    -42, 11, 12, -48, 51, -49, 52, -9, -10, 14, 18, 58, 59, -13, -17, -46, -47, -55, 65, -60, 70,
    -53, 56, -54, 57, 15, 19, 63, 64, 21, 25, -11, -12, -51, -52, 16, 20, -58, 61, -59, 62, -14,
    -18, 68, 69, -65, -70, 22, 26, -56, -57, -15, -19, 23, 27, -63, 66, -64, 67, -21, -25, 29, 33,
    73, 74, -16, 24, -20, 28, -61, -62, -22, 30, -26, 34, -68, 71, -69, 72, -23, 31, -27, 35, -24,
    32, -28, 36, -73, 75, -74, 76, -66, -67, -29, -33, -30, -34, -71, -72, -31, -35, -32, -36, -75,
    -76,
]


def groups_full_at(at):
    last = {}
    for place, item in enumerate(ORDER):
        if item < 0:
            last[SLOTS.index(MESSAGES[-item - 1][2]) // GROUP] = place
    return [group for group in sorted(last) if last[group] == at]


def silu(v):
    return v / (1.0 + jnp.exp(-v))


def seq_id(index):
    return {"seq": index}


def exp_id(index):
    return {"exp": index}


def neighbour(axis, way):
    me = lax.axis_index("seq")
    y, z = me // ZS, me % ZS
    if axis == "y":
        return ((y + way + YS) % YS) * ZS + z
    return y * ZS + (z + way + ZS) % ZS


def spread(view, send_sems, recv_sems):
    def copy(k):
        tree, source, target, part, way = MESSAGES[k]
        return pltpu.make_async_remote_copy(
            src_ref=view(tree, SLOTS.index(source), part),
            dst_ref=view(tree, SLOTS.index(target), part),
            send_sem=send_sems.at[k],
            recv_sem=recv_sems.at[k],
            device_id=seq_id(neighbour(*way)),
            device_id_type=MESH,
        )

    def run(when_full, start=0, stop=len(ORDER)):
        for at in range(start, stop):
            item = ORDER[at]
            if item > 0:
                copy(item - 1).start()
            else:
                copy(-item - 1).wait_recv()
                for group in groups_full_at(at):
                    when_full(group)

    def finish():
        for k in range(len(MESSAGES)):
            copy(k).wait_send()

    return run, finish


def gather_sum(view, landing, add, send_sems, recv_sems):
    def copy(k):
        tree, _, child, part, (axis, way) = MESSAGES[k]
        return pltpu.make_async_remote_copy(
            src_ref=view(tree, SLOTS.index(child), part),
            dst_ref=landing(tree, SLOTS.index(child), part),
            send_sem=send_sems.at[k],
            recv_sem=recv_sems.at[k],
            device_id=seq_id(neighbour(axis, -way)),
            device_id_type=MESH,
        )

    def run():
        for item in reversed(ORDER):
            k = abs(item) - 1
            if item < 0:
                copy(k).start()
            else:
                copy(k).wait_recv()
                _, parent, child, part, _ = MESSAGES[k]
                add(MESSAGES[k][0], SLOTS.index(parent), SLOTS.index(child), part)

    def finish():
        for k in range(len(MESSAGES)):
            copy(k).wait_send()

    return run, finish


def dot(a, b):
    return jnp.dot(a, b, preferred_element_type=F32)


def one_hot(condition):
    return condition.astype(F32).astype(BF16)


def slot_table(routes_t):
    toks = routes_t.shape[1]
    expert = lax.broadcasted_iota(jnp.int32, (LANES, toks), 0)
    hits = jnp.logical_or(routes_t[0:1, :] == expert, routes_t[1:2, :] == expert)
    row = lax.broadcasted_iota(jnp.int32, (toks, toks), 0)
    col = lax.broadcasted_iota(jnp.int32, (toks, toks), 1)
    places = dot(one_hot(hits), one_hot(row <= col)) - 1.0
    return jnp.where(hits, places, -1.0)


def places_of(table_t, expert):
    place = lax.broadcasted_iota(jnp.int32, (SLAB, table_t.shape[1]), 0).astype(F32)
    return (place == table_t[expert : expert + 1, :]).astype(F32)


def split_lanes(width):
    first = (width * 13 // 32) // LANES * LANES
    quarter = width // 4
    rest = (quarter * 13 // 32) // LANES * LANES
    return (first, width - first), (rest, quarter - rest)


def ring_steps(offsets, size):
    return [
        (offset, to, way, part)
        for offset in offsets
        for to, way, part in far_steps(offset, size)
    ]


W_SLOTS = Z_OFFSETS
W_STEPS = ring_steps(Z_OFFSETS, ZS)
GATED_STEPS = ring_steps(Y_OFFSETS, YS)


def mixer_kernel(
    mamba_ref,
    bc_ref,
    decay_ref,
    conv_ref,
    vec_ref,
    doc_ref,
    residual_ref,
    w_ref,
    gain_ref,
    routes_ref,
    resid_ref,
    own_a,
    own_b,
    xs,
    dts,
    us,
    zs,
    neg,
    tail,
    end_out,
    end_in,
    start_out,
    start_in,
    held_w,
    gated,
    partial,
    pair_in,
    pair_sum,
    cross_in,
    disp,
    disp_in,
    squares,
    rows_n,
    mix_out,
    mix_in,
    final_out,
    final_in,
    send_sems,
    recv_sems,
    w_send_sems,
    w_recv_sems,
    g_send_sems,
    g_recv_sems,
    y_send_sems,
    y_recv_sems,
    exp_send_sems,
    exp_recv_sems,
):
    count = lax.axis_size("seq")
    me = lax.axis_index("seq")
    toks = mamba_ref.shape[1]
    blocks = mamba_ref.shape[2] // LANES
    nstate = decay_ref.shape[0]
    rows = blocks
    first = me * toks
    e = lax.axis_index("exp")
    experts_count = lax.axis_size("exp")
    x, core = e // CORES, e % CORES
    xs_count = experts_count // CORES

    barrier = pltpu.get_barrier_semaphore()

    def greet(step, _):
        pl.semaphore_signal(
            barrier, inc=1, device_id=seq_id(lax.rem(me + step, count)), device_id_type=MESH
        )
        return 0

    lax.fori_loop(1, count, greet, 0)
    for step in range(1, experts_count):
        pl.semaphore_signal(
            barrier,
            inc=1,
            device_id=exp_id(lax.rem(e + step, experts_count)),
            device_id_type=MESH,
        )

    depth = w_ref.shape[0]
    held_w[0] = w_ref[...]
    y, z = me // ZS, me % ZS
    for j in range(blocks):
        lanes = pl.ds(j * LANES, LANES)
        xs[pl.ds(8 * rows + j, toks, stride=rows), :] = mamba_ref[0, :, lanes].astype(F32)
        zs[pl.ds(j, toks, stride=rows), :] = mamba_ref[1, :, lanes].astype(F32)
        dts[pl.ds(j, toks, stride=rows), :] = mamba_ref[2, :, lanes].astype(F32)
    pl.semaphore_wait(barrier, count - 1 + experts_count - 1)

    flows = 2
    flow_rows = depth // flows

    def w_copy(k, flow):
        source, target, way, part = W_STEPS[k]
        size = flow_rows if part is None else flow_rows // 2
        here = pl.ds(flow * flow_rows + (part or 0) * size, size)
        return pltpu.make_async_remote_copy(
            src_ref=held_w.at[W_SLOTS.index(source), here],
            dst_ref=held_w.at[W_SLOTS.index(target), here],
            send_sem=w_send_sems.at[k * flows + flow],
            recv_sem=w_recv_sems.at[k * flows + flow],
            device_id=seq_id(neighbour("z", way)),
            device_id_type=MESH,
        )

    def forward(round):
        for flow in range(flows):
            for way in (1, -1):
                for k, step in enumerate(W_STEPS):
                    if step[2] == way and abs(step[0]) == round - 1:
                        w_copy(k, flow).wait_recv()
                for k, step in enumerate(W_STEPS):
                    if step[2] == way and abs(step[0]) == round:
                        w_copy(k, flow).start()


    tail_copy = pltpu.make_async_remote_copy(
        src_ref=mamba_ref.at[0, pl.ds(toks - 16, 16)],
        dst_ref=tail,
        send_sem=send_sems.at[0],
        recv_sem=recv_sems.at[0],
        device_id=seq_id(lax.rem(me + 1, count)),
        device_id_type=MESH,
    )
    tail_copy.start()

    forward(0)
    for j in range(blocks):
        lanes = pl.ds(j * LANES, LANES)
        neg[pl.ds(j, nstate, stride=rows), :] = decay_ref[:, lanes] * (-LOG2E)

    def tile_row(ref, n):
        return jnp.concatenate(
            [ref[n : n + 1, j * LANES : (j + 1) * LANES] for j in range(blocks)], axis=0
        )

    step_bias = tile_row(vec_ref, 1)

    def tok(t):
        return pl.ds(pl.multiple_of(t * rows, rows), rows)

    def prepare(t, total):
        raw = dts[tok(t), :] + step_bias
        step = jnp.maximum(raw, 0.0) + jnp.log1p(jnp.exp(-jnp.abs(raw)))
        dts[tok(t), :] = step
        zs[tok(t), :] = silu(zs[tok(t), :])
        return total + step

    total_step = lax.fori_loop(0, toks, prepare, jnp.zeros((rows, LANES), F32), unroll=8)

    tail_copy.wait()
    there = jnp.where(me > 0, jnp.float32(1.0), jnp.float32(0.0))
    for j in range(blocks):
        rest = tail[:, pl.ds(j * LANES, LANES)].astype(F32) * there
        xs[pl.ds(j, 8, stride=rows), :] = rest[8:16, :]

    ends = []
    so_far = jnp.int32(0)
    for j in range(doc_ref.shape[0]):
        so_far = so_far + doc_ref[j]
        ends.append(so_far)

    def goes_on(position):
        keep = jnp.float32(1.0)
        for end in ends:
            keep = jnp.where(end == position, jnp.float32(0.0), keep)
        return keep

    taps = [tile_row(conv_ref, k) for k in range(conv_ref.shape[0])]
    conv_bias = tile_row(vec_ref, 0)

    def advance(t, states, keep, step, drive):
        new = []
        for n in range(nstate):
            growth = jnp.exp2(step * neg[pl.ds(n * rows, rows), :]) * keep
            new.append(growth * states[n] + drive * bc_ref[n, t])
        return tuple(new)

    def local_pass(t, carry):
        states, before, before2 = carry
        keep = goes_on(first + t)
        x0, x1, x2, x3 = [xs[tok(t + 8 - 3 + k), :] for k in range(4)]
        v2 = keep
        v1 = keep * before
        v0 = v1 * before2
        total = conv_bias + (taps[0] * x0) * v0 + (taps[1] * x1) * v1
        total = total + (taps[2] * x2) * v2 + taps[3] * x3
        u_row = silu(total)
        us[tok(t), :] = u_row
        step = dts[tok(t), :]
        return advance(t, states, keep, step, step * u_row), keep, before

    zero = tuple(jnp.zeros((rows, LANES), F32) for _ in range(nstate))
    carry = (zero, goes_on(first - 1), goes_on(first - 2))
    states, _, _ = lax.fori_loop(0, toks, local_pass, carry, unroll=2)
    high = total_step.astype(BF16)
    low = (total_step - high.astype(F32)).astype(BF16)
    for n in range(0, nstate, 2):
        pair = jnp.concatenate([states[n], states[n + 1]], axis=0).astype(BF16)
        end_out[n // 2] = jnp.concatenate([pair, high, low], axis=0)
    before = 2
    end_in[before * ZS + z] = end_out[z]

    def scatter(i):
        row, step = i // ZS, i % ZS
        holder = lax.rem(z + step, ZS)
        return pltpu.make_async_remote_copy(
            src_ref=end_out.at[holder],
            dst_ref=end_in.at[(before - row) * ZS + z],
            send_sem=send_sems.at[i],
            recv_sem=recv_sems.at[i],
            device_id=seq_id(lax.rem(y + row, YS) * ZS + holder),
            device_id_type=MESH,
        )

    def give_back(step):
        return pltpu.make_async_remote_copy(
            src_ref=start_out.at[lax.rem(z + step, ZS)],
            dst_ref=start_in.at[z],
            send_sem=send_sems.at[(before + 1) * ZS + step],
            recv_sem=recv_sems.at[(before + 1) * ZS + step],
            device_id=seq_id(y * ZS + lax.rem(z + step, ZS)),
            device_id_type=MESH,
        )

    def send(i, _):
        scatter(i).start()
        return 0

    later = jnp.minimum(before + 1, YS - y) * ZS
    earlier = jnp.minimum(before, y)
    lax.fori_loop(1, later, send, 0)
    forward(1)

    def arrive(i, _):
        scatter(i).wait_recv()
        return 0

    lax.fori_loop(1, (earlier + 1) * ZS, arrive, 0)

    def fold(at, held):
        begin = ((y - before) * ZS + at) * toks
        unbroken = jnp.float32(1.0)
        for end in ends:
            inside = jnp.logical_and(end >= begin, end < begin + toks)
            unbroken = jnp.where(inside, jnp.float32(0.0), unbroken)
        halves = end_in[at, pl.ds(2 * rows, 2 * rows), :].astype(F32)
        sums = halves[:rows] + halves[rows:]
        pair = end_in[at, pl.ds(0, 2 * rows), :].astype(F32)
        new = []
        for n in range(2):
            rate = neg[pl.ds(pl.multiple_of((2 * z + n) * rows, rows), rows), :]
            growth = jnp.exp2(sums * rate) * unbroken
            new.append(growth * held[n] + pair[n * rows : (n + 1) * rows, :])
        return tuple(new)

    def fold_own(at, held):
        start_out[at - before * ZS] = jnp.concatenate(held, axis=0).astype(BF16)
        return fold(at, held)

    held = lax.fori_loop((before - earlier) * ZS, before * ZS, fold, zero[:2])
    lax.fori_loop(before * ZS, (before + 1) * ZS, fold_own, held)

    def return_start(step, _):
        give_back(step).start()
        return 0

    lax.fori_loop(1, ZS, return_start, 0)
    start_in[z] = start_out[z]
    forward(2)

    def return_arrive(step, _):
        give_back(step).wait_recv()
        return 0

    lax.fori_loop(1, ZS, return_arrive, 0)
    entering = []
    for n in range(0, nstate, 2):
        pair = start_in[n // 2].astype(F32)
        entering += [pair[:rows], pair[rows:]]
    entering = tuple(entering)
    skip = tile_row(vec_ref, 2)

    def full_pass(t, states):
        keep = goes_on(first + t)
        u_row = us[tok(t), :]
        step = dts[tok(t), :]
        states = advance(t, states, keep, step, step * u_row)
        total = skip * u_row
        for n in range(nstate):
            total = total + states[n] * bc_ref[nstate + n, t]
        zs[tok(t), :] = zs[tok(t), :] * total
        return states

    half = toks // 2

    def gated_copy(k, piece):
        source, target, way, part = GATED_STEPS[k]
        size = half if part is None else half // 2
        here = pl.ds(piece * half + (part or 0) * size, size)
        return pltpu.make_async_remote_copy(
            src_ref=gated.at[Y_OFFSETS.index(source), here],
            dst_ref=gated.at[Y_OFFSETS.index(target), here],
            send_sem=g_send_sems.at[k * 2 + piece],
            recv_sem=g_recv_sems.at[k * 2 + piece],
            device_id=seq_id(neighbour("y", way)),
            device_id_type=MESH,
        )

    states = entering
    for piece in range(2):
        states = lax.fori_loop(piece * half, (piece + 1) * half, full_pass, states, unroll=2)
        for j in range(blocks):
            gated[0, pl.ds(piece * half, half), pl.ds(j * LANES, LANES)] = zs[
                pl.ds(piece * half * rows + j, half, stride=rows), :
            ].astype(BF16)
        for k, step in enumerate(GATED_STEPS):
            if step[0] == 0:
                gated_copy(k, piece).start()
    forward(3)
    table_t = slot_table(routes_ref[...])

    def product(slots):
        left = jnp.concatenate([gated[i] for i in slots], axis=0)
        for pair in range(ZS // 2):
            right = jnp.concatenate([held_w[2 * pair], held_w[2 * pair + 1]], axis=1)
            made = dot(left, right).astype(BF16)
            for n in range(2):
                owner = (z - W_SLOTS[2 * pair + n] + ZS) % ZS
                for i, slot in enumerate(slots):
                    shard = (y - Y_OFFSETS[slot] + YS) % YS
                    partial[owner % CORES, owner // CORES, shard] = made[
                        i * toks : (i + 1) * toks, n * LANES : (n + 1) * LANES
                    ]

    for piece in range(2):
        for k, step in enumerate(GATED_STEPS):
            if step[0] == 0:
                gated_copy(k, piece).wait_recv()
                for k2, step2 in enumerate(GATED_STEPS):
                    if step2[0] == step[1]:
                        gated_copy(k2, piece).start()
    forward(4)
    product([0, 1, 2])
    for piece in range(2):
        for k, step in enumerate(GATED_STEPS):
            if step[0] != 0:
                gated_copy(k, piece).wait_recv()
    product([3])

    def pair_copy(k):
        to = lax.rem(x + k, xs_count)
        return pltpu.make_async_remote_copy(
            src_ref=partial.at[1 - core, to],
            dst_ref=pair_in.at[to],
            send_sem=exp_send_sems.at[k],
            recv_sem=exp_recv_sems.at[k],
            device_id=exp_id(x * CORES + 1 - core),
            device_id_type=MESH,
        )

    def cross_copy(k):
        to = lax.rem(x + k, xs_count)
        return pltpu.make_async_remote_copy(
            src_ref=pair_sum.at[to],
            dst_ref=cross_in.at[k - 1],
            send_sem=exp_send_sems.at[xs_count + k],
            recv_sem=exp_recv_sems.at[xs_count + k],
            device_id=exp_id(to * CORES + core),
            device_id_type=MESH,
        )

    order = [2, 1, 3, 0]
    for k in order:
        pair_copy(k).start()
    for k in order:
        pair_copy(k).wait_recv()
        to = lax.rem(x + k, xs_count)
        total = partial[core, to].astype(F32) + pair_in[to].astype(F32)
        if k > 0:
            pair_sum[to] = total.astype(BF16)
            cross_copy(k).start()
    for k in (1, 3, 2):
        cross_copy(k).wait_recv()
        total = total + cross_in[k - 1].astype(F32)

    mix_out[...] = total.astype(BF16)

    def shard_copy(k):
        to = lax.rem(y + k, YS)
        return pltpu.make_async_remote_copy(
            src_ref=mix_out.at[to],
            dst_ref=mix_in.at[y],
            send_sem=y_send_sems.at[k - 1],
            recv_sem=y_recv_sems.at[k - 1],
            device_id=seq_id(to * ZS + z),
            device_id_type=MESH,
        )

    for k in (2, 1, 3):
        shard_copy(k).start()
    mix_in[y] = mix_out[y]
    for k in (1, 3, 2):
        shard_copy(k).wait_recv()
    width = residual_ref.shape[1]
    block = width // experts_count
    quarter = width // YS
    sides = []
    for q in range(YS):
        lane = pl.multiple_of(q * quarter + e * LANES, LANES)
        sides.append(residual_ref[:, pl.ds(lane, LANES)].astype(F32) + mix_in[q].astype(F32))
        final_out[q] = sides[q].astype(BF16)
    total = jnp.concatenate(sides, axis=1)

    def final_copy(q):
        return pltpu.make_async_remote_copy(
            src_ref=final_out.at[q],
            dst_ref=final_in.at[e % YS],
            send_sem=y_send_sems.at[YS - 1 + q],
            recv_sem=y_recv_sems.at[YS - 1 + e % YS],
            device_id=exp_id(CORES * q + e // YS),
            device_id_type=MESH,
        )

    def final_wait(j):
        return pltpu.make_async_remote_copy(
            src_ref=final_out.at[0],
            dst_ref=final_in.at[j],
            send_sem=y_send_sems.at[YS - 1],
            recv_sem=y_recv_sems.at[YS - 1 + j],
            device_id=exp_id(lax.rem(e + 1, experts_count)),
            device_id_type=MESH,
        )

    square = jnp.sum(total * total, axis=1, keepdims=True)
    squares[e] = (square * jnp.ones((1, LANES), F32)).T[0:8, :]
    sent_rows = total.astype(BF16)
    for j in range(experts_count):
        disp[j] = dot(places_of(table_t, j).astype(BF16), sent_rows).astype(BF16)

    def deal(k):
        to = lax.rem(e + k, experts_count)
        base = 2 * xs_count + 2 * (k - 1)
        return [
            pltpu.make_async_remote_copy(
                src_ref=source,
                dst_ref=target,
                send_sem=exp_send_sems.at[base + i],
                recv_sem=exp_recv_sems.at[base + i],
                device_id=exp_id(to),
                device_id_type=MESH,
            )
            for i, (source, target) in enumerate(
                [(disp.at[to], disp_in.at[e]), (squares.at[e], squares.at[e])]
            )
        ]

    for k in range(1, experts_count):
        for copy in deal(k):
            copy.start()
    for q in range(YS):
        home = CORES * q + e // YS == e

        @pl.when(home)
        def _():
            final_in[e % YS] = final_out[q]

        @pl.when(jnp.logical_not(home))
        def _():
            final_copy(q).start()

    disp_in[e] = disp[e]
    expert_row = lax.broadcasted_iota(jnp.int32, (LANES, toks), 0)
    place_t = jnp.sum(jnp.where(expert_row == e, table_t, 0.0), axis=0, keepdims=True)
    at = lax.broadcasted_iota(jnp.int32, (SLAB, toks), 0).astype(F32)
    mine = (at == place_t).astype(F32)
    for k in range(1, experts_count):
        for copy in deal(k):
            copy.wait_recv()
    mean = squares[0]
    for j in range(1, experts_count):
        mean = mean + squares[j]
    inverse = lax.rsqrt(mean * (1.0 / width) + 1e-05)
    scale = jnp.sum(mine * inverse[0:1, :], axis=1, keepdims=True)
    for j in range(experts_count):
        for q in range(YS):
            here = pl.ds(q * quarter + j * LANES, LANES)
            dealt = disp_in[j, :, pl.ds(q * LANES, LANES)].astype(F32)
            rows_n[:, here] = (dealt * scale * gain_ref[:, here]).astype(BF16)
    mains, rests = split_lanes(width)
    small_row = lax.broadcasted_iota(jnp.int32, (16, 16), 0)
    small_col = lax.broadcasted_iota(jnp.int32, (16, 16), 1)
    packed = jnp.zeros((16, quarter), F32)
    for q in range(4):
        choose = one_hot(jnp.logical_and(small_col < 4, small_row == q * 4 + small_col))
        packed = packed + dot(choose, rows_n[pl.ds(CAP_MAIN, 16), pl.ds(q * quarter, quarter)])
    packed = packed.astype(BF16)
    start = 0
    rest_start = 0
    for tree, own in enumerate((own_a, own_b)):
        wide = mains[tree]
        for tile in range(2):
            own[:, pl.ds(tile * wide, wide)] = rows_n[pl.ds(tile * 16, 16), pl.ds(start, wide)]
        own[:, pl.ds(2 * wide, rests[tree])] = packed[:, rest_start : rest_start + rests[tree]]
        start += wide
        rest_start += rests[tree]

    for j in range(YS):
        source = (e % CORES) * YS + j

        @pl.when(source != e)
        def _():
            final_wait(j).wait_recv()

        resid_ref[:, pl.ds(j * LANES, LANES)] = final_in[j].astype(F32)
    for q in range(YS):

        @pl.when(CORES * q + e // YS != e)
        def _():
            final_copy(q).wait_send()

    for k in range(1, YS):
        shard_copy(k).wait_send()
    for k in range(len(GATED_STEPS)):
        for piece in range(2):
            gated_copy(k, piece).wait_send()
    for k in range(len(W_STEPS)):
        for flow in range(flows):
            w_copy(k, flow).wait_send()

    def sent(i, _):
        scatter(i).wait_send()
        return 0

    lax.fori_loop(1, later, sent, 0)

    def returned(step, _):
        give_back(step).wait_send()
        return 0

    lax.fori_loop(1, ZS, returned, 0)
    for k in range(xs_count):
        pair_copy(k).wait_send()
        if k > 0:
            cross_copy(k).wait_send()
    for k in range(1, experts_count):
        for copy in deal(k):
            copy.wait_send()


def mixer(mamba_in, bc_proj, decay, conv_w, mamba_vec, doc_len, residual, w_out, gain, routes):
    toks, channels = mamba_in.shape[1:]
    nstate = decay.shape[0]
    rows = channels // LANES
    width = residual.shape[1]
    count = lax.axis_size("exp")
    block = width // count
    depth = w_out.shape[0]
    mains, rests = split_lanes(width)
    sizes = [2 * main + rest for main, rest in zip(mains, rests)]
    xs_count = count // CORES
    exp_sems = 2 * xs_count + 2 * (count - 1)
    vmem = pl.BlockSpec(memory_space=pltpu.VMEM)
    smem = pl.BlockSpec(memory_space=pltpu.SMEM)
    return pl.pallas_call(
        mixer_kernel,
        out_shape=[jax.ShapeDtypeStruct((toks, block), F32)]
        + [jax.ShapeDtypeStruct((16, size), BF16) for size in sizes],
        in_specs=[vmem, smem, vmem, vmem, vmem, smem, vmem, vmem, vmem, vmem],
        out_specs=[vmem] * 3,
        scratch_shapes=[
            pltpu.VMEM(((toks + 8) * rows, LANES), F32),
            pltpu.VMEM((toks * rows, LANES), F32),
            pltpu.VMEM((toks * rows, LANES), F32),
            pltpu.VMEM((toks * rows, LANES), F32),
            pltpu.VMEM((nstate * rows, LANES), F32),
            pltpu.VMEM((16, channels), BF16),
            pltpu.VMEM((ZS, 4 * rows, LANES), BF16),
            pltpu.VMEM((3 * ZS, 4 * rows, LANES), BF16),
            pltpu.VMEM((ZS, 2 * rows, LANES), BF16),
            pltpu.VMEM((ZS, 2 * rows, LANES), BF16),
            pltpu.VMEM((ZS, depth, LANES), BF16),
            pltpu.VMEM((YS, toks, channels), BF16),
            pltpu.VMEM((CORES, xs_count, YS, toks, LANES), BF16),
            pltpu.VMEM((xs_count, YS, toks, LANES), BF16),
            pltpu.VMEM((xs_count, YS, toks, LANES), BF16),
            pltpu.VMEM((xs_count - 1, YS, toks, LANES), BF16),
            pltpu.VMEM((count, SLAB, block), BF16),
            pltpu.VMEM((count, SLAB, block), BF16),
            pltpu.VMEM((count, 8, LANES), F32),
            pltpu.VMEM((SLAB, width), BF16),
            pltpu.VMEM((YS, toks, LANES), BF16),
            pltpu.VMEM((YS, toks, LANES), BF16),
            pltpu.VMEM((YS, toks, LANES), BF16),
            pltpu.VMEM((YS, toks, LANES), BF16),
            pltpu.SemaphoreType.DMA((4 * ZS,)),
            pltpu.SemaphoreType.DMA((4 * ZS,)),
            pltpu.SemaphoreType.DMA((2 * len(W_STEPS),)),
            pltpu.SemaphoreType.DMA((2 * len(W_STEPS),)),
            pltpu.SemaphoreType.DMA((2 * len(GATED_STEPS),)),
            pltpu.SemaphoreType.DMA((2 * len(GATED_STEPS),)),
            pltpu.SemaphoreType.DMA((2 * YS - 1,)),
            pltpu.SemaphoreType.DMA((2 * YS - 1,)),
            pltpu.SemaphoreType.DMA((exp_sems,)),
            pltpu.SemaphoreType.DMA((exp_sems,)),
        ],
        compiler_params=pltpu.CompilerParams(
            collective_id=1, has_side_effects=True, vmem_limit_bytes=56 * 1024 * 1024
        ),
        name="mixer",
    )(
        mamba_in,
        bc_proj,
        decay,
        conv_w,
        mamba_vec,
        doc_len,
        residual,
        w_out,
        gain.reshape(1, width),
        routes,
    )


def experts_kernel(
    own_a,
    own_b,
    resid_ref,
    routes_ref,
    gate_ref,
    w1_ref,
    w2_ref,
    out_ref,
    held_a,
    held_b,
    outs_a,
    outs_b,
    sums_a,
    sums_b,
    w1,
    w2,
    rows_x,
    acc,
    hidden,
    few_acc,
    made_rows,
    sent,
    got,
    local_sems,
    send_sems,
    recv_sems,
    sum_send_sems,
    sum_recv_sems,
    out_send_sems,
    out_recv_sems,
):
    units, width = w2_ref.shape
    quarter = width // 4
    mains, rests = split_lanes(width)
    e = lax.axis_index("exp")
    count = lax.axis_size("exp")
    group_main = GROUP * CAP_MAIN
    group_rest = GROUP * 4

    loads = [
        pltpu.make_async_copy(w1_ref.at[0], w1.at[:, pl.ds(0, units)], local_sems.at[0]),
        pltpu.make_async_copy(w1_ref.at[1], w1.at[:, pl.ds(units, units)], local_sems.at[1]),
        pltpu.make_async_copy(w2_ref, w2, local_sems.at[2]),
    ]
    for load in loads:
        load.start()

    barrier = pltpu.get_barrier_semaphore()
    for axis in ("y", "z"):
        for way in (1, -1):
            pl.semaphore_signal(
                barrier, inc=1, device_id=seq_id(neighbour(axis, way)), device_id_type=MESH
            )
    for k in range(1, count):
        pl.semaphore_signal(
            barrier, inc=1, device_id=exp_id(lax.rem(e + k, count)), device_id_type=MESH
        )
    held, outs, sums = (held_a, held_b), (outs_a, outs_b), (sums_a, sums_b)
    held_a[0] = own_a[...]
    held_b[0] = own_b[...]
    pl.semaphore_wait(barrier, 4 + count - 1)

    def lanes(tree, part):
        total = 2 * mains[tree] + rests[tree]
        cut = total // 2 // LANES * LANES
        if part is None:
            return pl.ds(0, total)
        return pl.ds(0, cut) if part == 0 else pl.ds(cut, total - cut)

    def view_of(refs):
        return lambda tree, slot, part: refs[tree].at[slot, :, lanes(tree, part)]

    gather, gather_end = spread(view_of(held), send_sems, recv_sems)

    row = lax.broadcasted_iota(jnp.int32, (group_rest, group_rest * 4), 0)
    col = lax.broadcasted_iota(jnp.int32, (group_rest, group_rest * 4), 1)
    row_t = lax.broadcasted_iota(jnp.int32, (group_rest * 4, group_rest), 0)
    col_t = lax.broadcasted_iota(jnp.int32, (group_rest * 4, group_rest), 1)

    def pick(q):
        return one_hot(col == (row // 4) * 16 + q * 4 + row % 4)

    def put(q):
        return one_hot(row_t == (col_t // 4) * 16 + q * 4 + col_t % 4)

    half = width // 2
    members = GROUP * 16

    def feed(g):
        base = pl.ds(g * GROUP, GROUP)
        start = 0
        packed = []
        for tree in range(2):
            wide = mains[tree]
            for tile in range(2):
                rows_x[pl.ds(tile * members, members), pl.ds(start, wide)] = held[tree][
                    base, :, pl.ds(tile * wide, wide)
                ].reshape(members, wide)
            packed.append(
                held[tree][base, :, pl.ds(2 * wide, rests[tree])].reshape(members, rests[tree])
            )
            start += wide
        packed = jnp.concatenate(packed, axis=1)
        for q in range(4):
            rows_x[pl.ds(group_main, group_rest), pl.ds(q * quarter, quarter)] = dot(
                pick(q), packed
            ).astype(BF16)
        acc[...] = dot(rows_x[:, pl.ds(0, half)], w1[pl.ds(0, half), :])
        both = acc[...] + dot(rows_x[:, pl.ds(half, half)], w1[pl.ds(half, half), :])
        hidden[...] = (silu(both[:, :units]) * both[:, units:]).astype(BF16)

        start = 0
        for tree in range(2):
            wide = mains[tree]
            made = dot(hidden[...], w2[:, pl.ds(start, wide)]).astype(BF16)
            for tile in range(2):
                outs[tree][base, :, pl.ds(tile * wide, wide)] = made[
                    tile * members : (tile + 1) * members
                ].reshape(GROUP, 16, wide)
            few_acc[:, pl.ds(start, wide)] = made[group_main:]
            start += wide
        few = jnp.zeros((members, quarter), F32)
        for q in range(4):
            few = few + dot(put(q), few_acc[:, pl.ds(q * quarter, quarter)])
        few = few.astype(BF16)
        outs_a[base, :, pl.ds(2 * mains[0], rests[0])] = few[:, : rests[0]].reshape(
            GROUP, 16, rests[0]
        )
        outs_b[base, :, pl.ds(2 * mains[1], rests[1])] = few[:, rests[0] :].reshape(
            GROUP, 16, rests[1]
        )

    def when_full(g):
        if g == 0:
            for load in loads:
                load.wait()
        feed(g)

    gather(when_full)

    def add(tree, slot, child, part):
        here = lanes(tree, part)
        total = outs[tree][slot, :, here].astype(F32) + sums[tree][child, :, here].astype(F32)
        outs[tree][slot, :, here] = total.astype(BF16)

    reduce, reduce_end = gather_sum(
        view_of(outs), view_of(sums), add, sum_send_sems, sum_recv_sems
    )
    reduce()

    start = 0
    for tree in range(2):
        wide = mains[tree]
        for tile in range(2):
            made_rows[pl.ds(tile * 16, 16), pl.ds(start, wide)] = outs[tree][
                0, :, pl.ds(tile * wide, wide)
            ]
        start += wide
    packed = jnp.concatenate(
        [outs[tree][0, :, pl.ds(2 * mains[tree], rests[tree])] for tree in range(2)], axis=1
    )
    small_row = lax.broadcasted_iota(jnp.int32, (16, 16), 0)
    small_col = lax.broadcasted_iota(jnp.int32, (16, 16), 1)
    for q in range(4):
        choose = one_hot(jnp.logical_and(small_row < 4, small_col == q * 4 + small_row))
        made_rows[pl.ds(CAP_MAIN, 16), pl.ds(q * quarter, quarter)] = dot(choose, packed).astype(
            BF16
        )
    routes_t = routes_ref[...]
    toks = routes_t.shape[1]
    table_t = slot_table(routes_t)
    table = table_t.T
    chosen = jnp.where(routes_t == e, gate_ref[...], 0.0)
    weight_t = chosen[0:1, :] + chosen[1:2, :]
    expert_row = lax.broadcasted_iota(jnp.int32, (LANES, toks), 0)
    place_t = jnp.sum(jnp.where(expert_row == e, table_t, 0.0), axis=0, keepdims=True)
    at = lax.broadcasted_iota(jnp.int32, (SLAB, toks), 0).astype(F32)
    mine = (at == place_t).astype(F32)
    row_weight = jnp.sum(mine * weight_t, axis=1, keepdims=True)
    block = width // count
    for j in range(count):
        part = made_rows[:, pl.ds(j * block, block)].astype(F32)
        sent[j] = (row_weight * part).astype(BF16)

    def give(k):
        to = lax.rem(e + k, count)
        return pltpu.make_async_remote_copy(
            src_ref=sent.at[to],
            dst_ref=got.at[e],
            send_sem=out_send_sems.at[k - 1],
            recv_sem=out_recv_sems.at[k - 1],
            device_id=exp_id(to),
            device_id_type=MESH,
        )

    for k in range(1, count):
        give(k).start()
    got[e] = sent[e]
    for k in range(1, count):
        give(k).wait_recv()
    total = resid_ref[...]
    place_lane = lax.broadcasted_iota(jnp.int32, (toks, SLAB), 1).astype(F32)
    for j in range(count):
        total = total + dot(one_hot(place_lane == table[:, j : j + 1]), got[j])
    out_ref[...] = total.astype(BF16)

    gather_end()
    reduce_end()
    for k in range(1, count):
        give(k).wait_send()


def experts(own_a, own_b, resid, routes, gate_w, w1, w2):
    units, width = w2.shape
    count = lax.axis_size("exp")
    slots = len(SLOTS)
    sizes = [own_a.shape[1], own_b.shape[1]]
    group_rows = GROUP * (CAP_MAIN + 4)
    vmem = pl.BlockSpec(memory_space=pltpu.VMEM)
    hbm = pl.BlockSpec(memory_space=pl.ANY)
    return pl.pallas_call(
        experts_kernel,
        out_shape=jax.ShapeDtypeStruct(resid.shape, BF16),
        in_specs=[vmem] * 5 + [hbm, hbm],
        out_specs=vmem,
        scratch_shapes=[pltpu.VMEM((slots, 16, size), BF16) for _ in range(3) for size in sizes]
        + [
            pltpu.VMEM((width, 2 * units), BF16),
            pltpu.VMEM((units, width), BF16),
            pltpu.VMEM((group_rows, width), BF16),
            pltpu.VMEM((group_rows, 2 * units), F32),
            pltpu.VMEM((group_rows, units), BF16),
            pltpu.VMEM((GROUP * 4, width), BF16),
            pltpu.VMEM((SLAB, width), BF16),
            pltpu.VMEM((count, SLAB, width // count), BF16),
            pltpu.VMEM((count, SLAB, width // count), BF16),
            pltpu.SemaphoreType.DMA((3,)),
        ]
        + [pltpu.SemaphoreType.DMA((len(MESSAGES),)) for _ in range(4)]
        + [pltpu.SemaphoreType.DMA((count - 1,)) for _ in range(2)],
        compiler_params=pltpu.CompilerParams(
            collective_id=2, has_side_effects=True, vmem_limit_bytes=60 * 1024 * 1024
        ),
        name="experts",
    )(own_a, own_b, resid, routes, gate_w, w1, w2)


def shards(
    residual_in,
    mamba_in,
    bc_proj,
    decay,
    conv_w,
    mamba_vec,
    doc_len,
    w_out,
    norm_gain,
    routes,
    gate_w,
    w_gate_up,
    w_down,
):
    resid, own_a, own_b = mixer(
        mamba_in,
        bc_proj,
        decay,
        conv_w,
        mamba_vec,
        doc_len,
        residual_in,
        w_out,
        norm_gain,
        routes.T,
    )
    return experts(own_a, own_b, resid, routes.T, gate_w.T, w_gate_up[0], w_down[0])


def solution(mesh):
    in_specs = (
        P("seq", None),
        P(None, "seq", "exp"),
        P(None, "seq"),
        P(None, "exp"),
        P(None, "exp"),
        P(None, "exp"),
        P(),
        P("exp", "seq"),
        P(),
        P("seq", None),
        P("seq", None),
        P("exp", None, None, "seq"),
        P("exp", "seq", None),
    )
    out_specs = P("seq", "exp")
    return jax.shard_map(shards, mesh=mesh, in_specs=in_specs, out_specs=out_specs, check_vma=False)
```

```python
import jax
import jax.numpy as jnp
from jax import lax
from jax.experimental import pallas as pl
from jax.experimental.pallas import tpu as pltpu
from jax.sharding import PartitionSpec as P

MESH = pl.DeviceIdType.MESH
LOG2E = 1.4426950408889634
LANES = 128
F32 = jnp.float32
BF16 = jnp.bfloat16
YS, ZS = 4, 8
CORES = 2
SLAB = 48
CAP_MAIN = 32

Y_OFFSETS = (0, 1, -1, 2)
Z_OFFSETS = (0, 1, -1, 2, -2, 3, -3, 4)
SLOTS = [(dy, dz) for dz in Z_OFFSETS for dy in Y_OFFSETS]
GROUP = 8


def far_steps(offset, size):
    top = size // 2
    if offset == 0:
        return [(1, 1, None), (-1, -1, None)]
    if offset == top:
        return []
    if offset > 0:
        return [(offset + 1, 1, 0 if offset + 1 == top else None)]
    return [(offset - 1, -1, None)] if offset - 1 > -top else [(top, -1, 1)]


def messages():
    found = []
    for tree in range(2):
        for dy, dz in SLOTS:
            if tree == 1 or dz == 0:
                for to, way, part in far_steps(dy, YS):
                    found.append((tree, (dy, dz), (to, dz), part, ("y", way)))
            if tree == 0 or dy == 0:
                for to, way, part in far_steps(dz, ZS):
                    found.append((tree, (dy, dz), (dy, to), part, ("z", way)))
    return found


MESSAGES = messages()
DEPTH = {slot: abs(slot[0]) + abs(slot[1]) for slot in SLOTS}
DEEPEST = max(DEPTH.values())


ORDER = [
    1, 2, 39, 40, 37, 38, 3, 4, -1, 5, 6, 7, -2, 8, -39, 43, 44, 45, -40, 50, -37, 41, -38, 42, 9,
    10, 48, 49, -3, -4, -5, -8, 13, 17, -6, -7, -43, 46, -44, 47, -45, 55, -50, 60, 53, 54, -41,
    -42, 11, 12, -48, 51, -49, 52, -9, -10, 14, 18, 58, 59, -13, -17, -46, -47, -55, 65, -60, 70,
    -53, 56, -54, 57, 15, 19, 63, 64, 21, 25, -11, -12, -51, -52, 16, 20, -58, 61, -59, 62, -14,
    -18, 68, 69, -65, -70, 22, 26, -56, -57, -15, -19, 23, 27, -63, 66, -64, 67, -21, -25, 29, 33,
    73, 74, -16, 24, -20, 28, -61, -62, -22, 30, -26, 34, -68, 71, -69, 72, -23, 31, -27, 35, -24,
    32, -28, 36, -73, 75, -74, 76, -66, -67, -29, -33, -30, -34, -71, -72, -31, -35, -32, -36, -75,
    -76,
]


def groups_full_at(at):
    last = {}
    for place, item in enumerate(ORDER):
        if item < 0:
            last[SLOTS.index(MESSAGES[-item - 1][2]) // GROUP] = place
    return [group for group in sorted(last) if last[group] == at]


def silu(v):
    return v / (1.0 + jnp.exp(-v))


def seq_id(index):
    return {"seq": index}


def exp_id(index):
    return {"exp": index}


def neighbour(axis, way):
    me = lax.axis_index("seq")
    y, z = me // ZS, me % ZS
    if axis == "y":
        return ((y + way + YS) % YS) * ZS + z
    return y * ZS + (z + way + ZS) % ZS


def spread(view, send_sems, recv_sems):
    def copy(k):
        tree, source, target, part, way = MESSAGES[k]
        return pltpu.make_async_remote_copy(
            src_ref=view(tree, SLOTS.index(source), part),
            dst_ref=view(tree, SLOTS.index(target), part),
            send_sem=send_sems.at[k],
            recv_sem=recv_sems.at[k],
            device_id=seq_id(neighbour(*way)),
            device_id_type=MESH,
        )

    def run(when_full, start=0, stop=len(ORDER)):
        for at in range(start, stop):
            item = ORDER[at]
            if item > 0:
                copy(item - 1).start()
            else:
                copy(-item - 1).wait_recv()
                for group in groups_full_at(at):
                    when_full(group)

    def finish():
        for k in range(len(MESSAGES)):
            copy(k).wait_send()

    return run, finish


def gather_sum(view, landing, add, send_sems, recv_sems):
    def copy(k):
        tree, _, child, part, (axis, way) = MESSAGES[k]
        return pltpu.make_async_remote_copy(
            src_ref=view(tree, SLOTS.index(child), part),
            dst_ref=landing(tree, SLOTS.index(child), part),
            send_sem=send_sems.at[k],
            recv_sem=recv_sems.at[k],
            device_id=seq_id(neighbour(axis, -way)),
            device_id_type=MESH,
        )

    def run():
        for item in reversed(ORDER):
            k = abs(item) - 1
            if item < 0:
                copy(k).start()
            else:
                copy(k).wait_recv()
                _, parent, child, part, _ = MESSAGES[k]
                add(MESSAGES[k][0], SLOTS.index(parent), SLOTS.index(child), part)

    def finish():
        for k in range(len(MESSAGES)):
            copy(k).wait_send()

    return run, finish


def dot(a, b):
    return jnp.dot(a, b, preferred_element_type=F32)


def one_hot(condition):
    return condition.astype(F32).astype(BF16)


def slot_table(routes_t):
    toks = routes_t.shape[1]
    expert = lax.broadcasted_iota(jnp.int32, (LANES, toks), 0)
    hits = jnp.logical_or(routes_t[0:1, :] == expert, routes_t[1:2, :] == expert)
    row = lax.broadcasted_iota(jnp.int32, (toks, toks), 0)
    col = lax.broadcasted_iota(jnp.int32, (toks, toks), 1)
    places = dot(one_hot(hits), one_hot(row <= col)) - 1.0
    return jnp.where(hits, places, -1.0)


def places_of(table_t, expert):
    place = lax.broadcasted_iota(jnp.int32, (SLAB, table_t.shape[1]), 0).astype(F32)
    return (place == table_t[expert : expert + 1, :]).astype(F32)


def split_lanes(width):
    first = (width * 13 // 32) // LANES * LANES
    quarter = width // 4
    rest = (quarter * 13 // 32) // LANES * LANES
    return (first, width - first), (rest, quarter - rest)


def ring_steps(offsets, size):
    return [
        (offset, to, way, part)
        for offset in offsets
        for to, way, part in far_steps(offset, size)
    ]


W_SLOTS = Z_OFFSETS
W_STEPS = ring_steps(Z_OFFSETS, ZS)
GATED_STEPS = ring_steps(Y_OFFSETS, YS)


def mixer_part(
    mamba_ref,
    bc_ref,
    decay_ref,
    conv_ref,
    vec_ref,
    doc_ref,
    residual_ref,
    w_ref,
    gain_ref,
    routes_ref,
    resid_ref,
    own_a,
    own_b,
    xs,
    dts,
    us,
    zs,
    neg,
    tail,
    end_out,
    end_in,
    start_out,
    start_in,
    held_w,
    gated,
    partial,
    pair_in,
    pair_sum,
    cross_in,
    disp,
    disp_in,
    squares,
    rows_n,
    mix_out,
    mix_in,
    final_out,
    final_in,
    send_sems,
    recv_sems,
    w_send_sems,
    w_recv_sems,
    g_send_sems,
    g_recv_sems,
    y_send_sems,
    y_recv_sems,
    exp_send_sems,
    exp_recv_sems,
):
    count = lax.axis_size("seq")
    me = lax.axis_index("seq")
    toks = mamba_ref.shape[1]
    blocks = mamba_ref.shape[2] // LANES
    nstate = decay_ref.shape[0]
    rows = blocks
    first = me * toks
    e = lax.axis_index("exp")
    experts_count = lax.axis_size("exp")
    x, core = e // CORES, e % CORES
    xs_count = experts_count // CORES

    barrier = pltpu.get_barrier_semaphore()

    def greet(step, _):
        pl.semaphore_signal(
            barrier, inc=1, device_id=seq_id(lax.rem(me + step, count)), device_id_type=MESH
        )
        return 0

    lax.fori_loop(1, count, greet, 0)
    for step in range(1, experts_count):
        pl.semaphore_signal(
            barrier,
            inc=1,
            device_id=exp_id(lax.rem(e + step, experts_count)),
            device_id_type=MESH,
        )

    depth = w_ref.shape[0]
    held_w[0] = w_ref[...]
    y, z = me // ZS, me % ZS
    for j in range(blocks):
        lanes = pl.ds(j * LANES, LANES)
        xs[pl.ds(8 * rows + j, toks, stride=rows), :] = mamba_ref[0, :, lanes].astype(F32)
        zs[pl.ds(j, toks, stride=rows), :] = mamba_ref[1, :, lanes].astype(F32)
        dts[pl.ds(j, toks, stride=rows), :] = mamba_ref[2, :, lanes].astype(F32)
    pl.semaphore_wait(barrier, count - 1 + experts_count - 1)

    flows = 2
    flow_rows = depth // flows

    def w_copy(k, flow):
        source, target, way, part = W_STEPS[k]
        size = flow_rows if part is None else flow_rows // 2
        here = pl.ds(flow * flow_rows + (part or 0) * size, size)
        return pltpu.make_async_remote_copy(
            src_ref=held_w.at[W_SLOTS.index(source), here],
            dst_ref=held_w.at[W_SLOTS.index(target), here],
            send_sem=w_send_sems.at[k * flows + flow],
            recv_sem=w_recv_sems.at[k * flows + flow],
            device_id=seq_id(neighbour("z", way)),
            device_id_type=MESH,
        )

    def forward(round):
        for flow in range(flows):
            for way in (1, -1):
                for k, step in enumerate(W_STEPS):
                    if step[2] == way and abs(step[0]) == round - 1:
                        w_copy(k, flow).wait_recv()
                for k, step in enumerate(W_STEPS):
                    if step[2] == way and abs(step[0]) == round:
                        w_copy(k, flow).start()


    tail_copy = pltpu.make_async_remote_copy(
        src_ref=mamba_ref.at[0, pl.ds(toks - 16, 16)],
        dst_ref=tail,
        send_sem=send_sems.at[0],
        recv_sem=recv_sems.at[0],
        device_id=seq_id(lax.rem(me + 1, count)),
        device_id_type=MESH,
    )
    tail_copy.start()

    forward(0)
    for j in range(blocks):
        lanes = pl.ds(j * LANES, LANES)
        neg[pl.ds(j, nstate, stride=rows), :] = decay_ref[:, lanes] * (-LOG2E)

    def tile_row(ref, n):
        return jnp.concatenate(
            [ref[n : n + 1, j * LANES : (j + 1) * LANES] for j in range(blocks)], axis=0
        )

    step_bias = tile_row(vec_ref, 1)

    def tok(t):
        return pl.ds(pl.multiple_of(t * rows, rows), rows)

    def prepare(t, total):
        raw = dts[tok(t), :] + step_bias
        step = jnp.maximum(raw, 0.0) + jnp.log1p(jnp.exp(-jnp.abs(raw)))
        dts[tok(t), :] = step
        zs[tok(t), :] = silu(zs[tok(t), :])
        return total + step

    total_step = lax.fori_loop(0, toks, prepare, jnp.zeros((rows, LANES), F32), unroll=8)

    tail_copy.wait()
    there = jnp.where(me > 0, jnp.float32(1.0), jnp.float32(0.0))
    for j in range(blocks):
        rest = tail[:, pl.ds(j * LANES, LANES)].astype(F32) * there
        xs[pl.ds(j, 8, stride=rows), :] = rest[8:16, :]

    ends = []
    so_far = jnp.int32(0)
    for j in range(doc_ref.shape[0]):
        so_far = so_far + doc_ref[j]
        ends.append(so_far)

    def goes_on(position):
        keep = jnp.float32(1.0)
        for end in ends:
            keep = jnp.where(end == position, jnp.float32(0.0), keep)
        return keep

    taps = [tile_row(conv_ref, k) for k in range(conv_ref.shape[0])]
    conv_bias = tile_row(vec_ref, 0)

    def advance(t, states, keep, step, drive):
        new = []
        for n in range(nstate):
            growth = jnp.exp2(step * neg[pl.ds(n * rows, rows), :]) * keep
            new.append(growth * states[n] + drive * bc_ref[n, t])
        return tuple(new)

    def local_pass(t, carry):
        states, before, before2 = carry
        keep = goes_on(first + t)
        x0, x1, x2, x3 = [xs[tok(t + 8 - 3 + k), :] for k in range(4)]
        v2 = keep
        v1 = keep * before
        v0 = v1 * before2
        total = conv_bias + (taps[0] * x0) * v0 + (taps[1] * x1) * v1
        total = total + (taps[2] * x2) * v2 + taps[3] * x3
        u_row = silu(total)
        us[tok(t), :] = u_row
        step = dts[tok(t), :]
        return advance(t, states, keep, step, step * u_row), keep, before

    zero = tuple(jnp.zeros((rows, LANES), F32) for _ in range(nstate))
    carry = (zero, goes_on(first - 1), goes_on(first - 2))
    states, _, _ = lax.fori_loop(0, toks, local_pass, carry, unroll=2)
    high = total_step.astype(BF16)
    low = (total_step - high.astype(F32)).astype(BF16)
    for n in range(0, nstate, 2):
        pair = jnp.concatenate([states[n], states[n + 1]], axis=0).astype(BF16)
        end_out[n // 2] = jnp.concatenate([pair, high, low], axis=0)
    before = 2
    end_in[before * ZS + z] = end_out[z]

    def scatter(i):
        row, step = i // ZS, i % ZS
        holder = lax.rem(z + step, ZS)
        return pltpu.make_async_remote_copy(
            src_ref=end_out.at[holder],
            dst_ref=end_in.at[(before - row) * ZS + z],
            send_sem=send_sems.at[i],
            recv_sem=recv_sems.at[i],
            device_id=seq_id(lax.rem(y + row, YS) * ZS + holder),
            device_id_type=MESH,
        )

    def give_back(step):
        return pltpu.make_async_remote_copy(
            src_ref=start_out.at[lax.rem(z + step, ZS)],
            dst_ref=start_in.at[z],
            send_sem=send_sems.at[(before + 1) * ZS + step],
            recv_sem=recv_sems.at[(before + 1) * ZS + step],
            device_id=seq_id(y * ZS + lax.rem(z + step, ZS)),
            device_id_type=MESH,
        )

    def send(i, _):
        scatter(later - i).start()
        return 0

    later = jnp.minimum(before + 1, YS - y) * ZS
    earlier = jnp.minimum(before, y)
    lax.fori_loop(1, later, send, 0)
    forward(1)

    def arrive(i, _):
        scatter(i).wait_recv()
        return 0

    lax.fori_loop(1, (earlier + 1) * ZS, arrive, 0)

    def fold(at, held):
        begin = ((y - before) * ZS + at) * toks
        unbroken = jnp.float32(1.0)
        for end in ends:
            inside = jnp.logical_and(end >= begin, end < begin + toks)
            unbroken = jnp.where(inside, jnp.float32(0.0), unbroken)
        halves = end_in[at, pl.ds(2 * rows, 2 * rows), :].astype(F32)
        sums = halves[:rows] + halves[rows:]
        pair = end_in[at, pl.ds(0, 2 * rows), :].astype(F32)
        new = []
        for n in range(2):
            rate = neg[pl.ds(pl.multiple_of((2 * z + n) * rows, rows), rows), :]
            growth = jnp.exp2(sums * rate) * unbroken
            new.append(growth * held[n] + pair[n * rows : (n + 1) * rows, :])
        return tuple(new)

    def fold_own(at, held):
        start_out[at - before * ZS] = jnp.concatenate(held, axis=0).astype(BF16)
        return fold(at, held)

    held = lax.fori_loop((before - earlier) * ZS, before * ZS, fold, zero[:2])
    lax.fori_loop(before * ZS, (before + 1) * ZS, fold_own, held)

    def return_start(step, _):
        give_back(step).start()
        return 0

    lax.fori_loop(1, ZS, return_start, 0)
    start_in[z] = start_out[z]
    forward(2)

    def return_arrive(step, _):
        give_back(step).wait_recv()
        return 0

    lax.fori_loop(1, ZS, return_arrive, 0)
    entering = []
    for n in range(0, nstate, 2):
        pair = start_in[n // 2].astype(F32)
        entering += [pair[:rows], pair[rows:]]
    entering = tuple(entering)
    skip = tile_row(vec_ref, 2)

    def full_pass(t, states):
        keep = goes_on(first + t)
        u_row = us[tok(t), :]
        step = dts[tok(t), :]
        states = advance(t, states, keep, step, step * u_row)
        total = skip * u_row
        for n in range(nstate):
            total = total + states[n] * bc_ref[nstate + n, t]
        zs[tok(t), :] = zs[tok(t), :] * total
        return states

    half = toks // 2

    def gated_copy(k, piece):
        source, target, way, part = GATED_STEPS[k]
        size = half if part is None else half // 2
        here = pl.ds(piece * half + (part or 0) * size, size)
        return pltpu.make_async_remote_copy(
            src_ref=gated.at[Y_OFFSETS.index(source), here],
            dst_ref=gated.at[Y_OFFSETS.index(target), here],
            send_sem=g_send_sems.at[k * 2 + piece],
            recv_sem=g_recv_sems.at[k * 2 + piece],
            device_id=seq_id(neighbour("y", way)),
            device_id_type=MESH,
        )

    states = entering
    for piece in range(2):
        states = lax.fori_loop(piece * half, (piece + 1) * half, full_pass, states, unroll=2)
        for j in range(blocks):
            gated[0, pl.ds(piece * half, half), pl.ds(j * LANES, LANES)] = zs[
                pl.ds(piece * half * rows + j, half, stride=rows), :
            ].astype(BF16)
        for k, step in enumerate(GATED_STEPS):
            if step[0] == 0:
                gated_copy(k, piece).start()
    forward(3)
    table_t = slot_table(routes_ref[...])

    def product(slots):
        left = jnp.concatenate([gated[i] for i in slots], axis=0)
        for pair in range(ZS // 2):
            right = jnp.concatenate([held_w[2 * pair], held_w[2 * pair + 1]], axis=1)
            made = dot(left, right).astype(BF16)
            for n in range(2):
                owner = (z - W_SLOTS[2 * pair + n] + ZS) % ZS
                for i, slot in enumerate(slots):
                    shard = (y - Y_OFFSETS[slot] + YS) % YS
                    partial[owner % CORES, owner // CORES, shard] = made[
                        i * toks : (i + 1) * toks, n * LANES : (n + 1) * LANES
                    ]

    for piece in range(2):
        for k, step in enumerate(GATED_STEPS):
            if step[0] == 0:
                gated_copy(k, piece).wait_recv()
                for k2, step2 in enumerate(GATED_STEPS):
                    if step2[0] == step[1]:
                        gated_copy(k2, piece).start()
    forward(4)
    product([0, 1, 2])
    for piece in range(2):
        for k, step in enumerate(GATED_STEPS):
            if step[0] != 0:
                gated_copy(k, piece).wait_recv()
    product([3])

    def pair_copy(k):
        to = lax.rem(x + k, xs_count)
        return pltpu.make_async_remote_copy(
            src_ref=partial.at[1 - core, to],
            dst_ref=pair_in.at[to],
            send_sem=exp_send_sems.at[k],
            recv_sem=exp_recv_sems.at[k],
            device_id=exp_id(x * CORES + 1 - core),
            device_id_type=MESH,
        )

    def cross_copy(k):
        to = lax.rem(x + k, xs_count)
        return pltpu.make_async_remote_copy(
            src_ref=pair_sum.at[to],
            dst_ref=cross_in.at[k - 1],
            send_sem=exp_send_sems.at[xs_count + k],
            recv_sem=exp_recv_sems.at[xs_count + k],
            device_id=exp_id(to * CORES + core),
            device_id_type=MESH,
        )

    order = [2, 1, 3, 0]
    for k in order:
        pair_copy(k).start()
    for k in order:
        pair_copy(k).wait_recv()
        to = lax.rem(x + k, xs_count)
        total = partial[core, to].astype(F32) + pair_in[to].astype(F32)
        if k > 0:
            pair_sum[to] = total.astype(BF16)
            cross_copy(k).start()
    for k in (1, 3, 2):
        cross_copy(k).wait_recv()
        total = total + cross_in[k - 1].astype(F32)

    mix_out[...] = total.astype(BF16)

    def shard_copy(k):
        to = lax.rem(y + k, YS)
        return pltpu.make_async_remote_copy(
            src_ref=mix_out.at[to],
            dst_ref=mix_in.at[y],
            send_sem=y_send_sems.at[k - 1],
            recv_sem=y_recv_sems.at[k - 1],
            device_id=seq_id(to * ZS + z),
            device_id_type=MESH,
        )

    for k in (2, 1, 3):
        shard_copy(k).start()
    mix_in[y] = mix_out[y]
    for k in (1, 3, 2):
        shard_copy(k).wait_recv()
    width = residual_ref.shape[1]
    block = width // experts_count
    quarter = width // YS
    sides = []
    for q in range(YS):
        lane = pl.multiple_of(q * quarter + e * LANES, LANES)
        sides.append(residual_ref[:, pl.ds(lane, LANES)].astype(F32) + mix_in[q].astype(F32))
        final_out[q] = sides[q].astype(BF16)
    total = jnp.concatenate(sides, axis=1)

    def final_copy(q):
        return pltpu.make_async_remote_copy(
            src_ref=final_out.at[q],
            dst_ref=final_in.at[e % YS],
            send_sem=y_send_sems.at[YS - 1 + q],
            recv_sem=y_recv_sems.at[YS - 1 + e % YS],
            device_id=exp_id(CORES * q + e // YS),
            device_id_type=MESH,
        )

    def final_wait(j):
        return pltpu.make_async_remote_copy(
            src_ref=final_out.at[0],
            dst_ref=final_in.at[j],
            send_sem=y_send_sems.at[YS - 1],
            recv_sem=y_recv_sems.at[YS - 1 + j],
            device_id=exp_id(lax.rem(e + 1, experts_count)),
            device_id_type=MESH,
        )

    square = jnp.sum(total * total, axis=1, keepdims=True)
    squares[e] = (square * jnp.ones((1, LANES), F32)).T[0:8, :]
    sent_rows = total.astype(BF16)
    for j in range(experts_count):
        disp[j] = dot(places_of(table_t, j).astype(BF16), sent_rows).astype(BF16)

    def deal(k):
        to = lax.rem(e + k, experts_count)
        base = 2 * xs_count + 2 * (k - 1)
        return [
            pltpu.make_async_remote_copy(
                src_ref=source,
                dst_ref=target,
                send_sem=exp_send_sems.at[base + i],
                recv_sem=exp_recv_sems.at[base + i],
                device_id=exp_id(to),
                device_id_type=MESH,
            )
            for i, (source, target) in enumerate(
                [(disp.at[to], disp_in.at[e]), (squares.at[e], squares.at[e])]
            )
        ]

    for k in range(1, experts_count):
        for copy in deal(k):
            copy.start()
    for q in range(YS):
        home = CORES * q + e // YS == e

        @pl.when(home)
        def _():
            final_in[e % YS] = final_out[q]

        @pl.when(jnp.logical_not(home))
        def _():
            final_copy(q).start()

    disp_in[e] = disp[e]
    expert_row = lax.broadcasted_iota(jnp.int32, (LANES, toks), 0)
    place_t = jnp.sum(jnp.where(expert_row == e, table_t, 0.0), axis=0, keepdims=True)
    at = lax.broadcasted_iota(jnp.int32, (SLAB, toks), 0).astype(F32)
    mine = (at == place_t).astype(F32)
    for k in range(1, experts_count):
        for copy in deal(k):
            copy.wait_recv()
    mean = squares[0]
    for j in range(1, experts_count):
        mean = mean + squares[j]
    inverse = lax.rsqrt(mean * (1.0 / width) + 1e-05)
    scale = jnp.sum(mine * inverse[0:1, :], axis=1, keepdims=True)
    for j in range(experts_count):
        for q in range(YS):
            here = pl.ds(q * quarter + j * LANES, LANES)
            dealt = disp_in[j, :, pl.ds(q * LANES, LANES)].astype(F32)
            rows_n[:, here] = (dealt * scale * gain_ref[:, here]).astype(BF16)
    mains, rests = split_lanes(width)
    small_row = lax.broadcasted_iota(jnp.int32, (16, 16), 0)
    small_col = lax.broadcasted_iota(jnp.int32, (16, 16), 1)
    packed = jnp.zeros((16, quarter), F32)
    for q in range(4):
        choose = one_hot(jnp.logical_and(small_col < 4, small_row == q * 4 + small_col))
        packed = packed + dot(choose, rows_n[pl.ds(CAP_MAIN, 16), pl.ds(q * quarter, quarter)])
    packed = packed.astype(BF16)
    start = 0
    rest_start = 0
    for tree, own in enumerate((own_a, own_b)):
        wide = mains[tree]
        for tile in range(2):
            own[:, pl.ds(tile * wide, wide)] = rows_n[pl.ds(tile * 16, 16), pl.ds(start, wide)]
        own[:, pl.ds(2 * wide, rests[tree])] = packed[:, rest_start : rest_start + rests[tree]]
        start += wide
        rest_start += rests[tree]

    def finish():
        for j in range(YS):
            source = (e % CORES) * YS + j

            @pl.when(source != e)
            def _():
                final_wait(j).wait_recv()

            resid_ref[:, pl.ds(j * LANES, LANES)] = final_in[j].astype(F32)
        for q in range(YS):

            @pl.when(CORES * q + e // YS != e)
            def _():
                final_copy(q).wait_send()

        for k in range(1, YS):
            shard_copy(k).wait_send()
        for k in range(len(GATED_STEPS)):
            for piece in range(2):
                gated_copy(k, piece).wait_send()
        for k in range(len(W_STEPS)):
            for flow in range(flows):
                w_copy(k, flow).wait_send()

        def sent(i, _):
            scatter(i).wait_send()
            return 0

        lax.fori_loop(1, later, sent, 0)

        def returned(step, _):
            give_back(step).wait_send()
            return 0

        lax.fori_loop(1, ZS, returned, 0)
        for k in range(xs_count):
            pair_copy(k).wait_send()
            if k > 0:
                cross_copy(k).wait_send()
        for k in range(1, experts_count):
            for copy in deal(k):
                copy.wait_send()

    return finish


def experts_part(
    mixer_end,
    resid_ref,
    routes_ref,
    gate_ref,
    w1_ref,
    w2_ref,
    out_ref,
    held_a,
    held_b,
    outs_a,
    outs_b,
    sums_a,
    sums_b,
    w1,
    w2,
    rows_x,
    acc,
    hidden,
    few_acc,
    made_rows,
    sent,
    got,
    local_sems,
    send_sems,
    recv_sems,
    sum_send_sems,
    sum_recv_sems,
    out_send_sems,
    out_recv_sems,
):
    units, width = w2_ref.shape
    quarter = width // 4
    mains, rests = split_lanes(width)
    e = lax.axis_index("exp")
    count = lax.axis_size("exp")
    group_main = GROUP * CAP_MAIN
    group_rest = GROUP * 4

    loads = [
        pltpu.make_async_copy(w1_ref.at[0], w1.at[:, pl.ds(0, units)], local_sems.at[0]),
        pltpu.make_async_copy(w1_ref.at[1], w1.at[:, pl.ds(units, units)], local_sems.at[1]),
        pltpu.make_async_copy(w2_ref, w2, local_sems.at[2]),
    ]
    for load in loads:
        load.start()

    held, outs, sums = (held_a, held_b), (outs_a, outs_b), (sums_a, sums_b)

    def lanes(tree, part):
        total = 2 * mains[tree] + rests[tree]
        cut = total // 2 // LANES * LANES
        if part is None:
            return pl.ds(0, total)
        return pl.ds(0, cut) if part == 0 else pl.ds(cut, total - cut)

    def view_of(refs):
        return lambda tree, slot, part: refs[tree].at[slot, :, lanes(tree, part)]

    gather, gather_end = spread(view_of(held), send_sems, recv_sems)

    row = lax.broadcasted_iota(jnp.int32, (group_rest, group_rest * 4), 0)
    col = lax.broadcasted_iota(jnp.int32, (group_rest, group_rest * 4), 1)
    row_t = lax.broadcasted_iota(jnp.int32, (group_rest * 4, group_rest), 0)
    col_t = lax.broadcasted_iota(jnp.int32, (group_rest * 4, group_rest), 1)

    def pick(q):
        return one_hot(col == (row // 4) * 16 + q * 4 + row % 4)

    def put(q):
        return one_hot(row_t == (col_t // 4) * 16 + q * 4 + col_t % 4)

    half = width // 2
    members = GROUP * 16

    def feed(g):
        base = pl.ds(g * GROUP, GROUP)
        start = 0
        packed = []
        for tree in range(2):
            wide = mains[tree]
            for tile in range(2):
                rows_x[pl.ds(tile * members, members), pl.ds(start, wide)] = held[tree][
                    base, :, pl.ds(tile * wide, wide)
                ].reshape(members, wide)
            packed.append(
                held[tree][base, :, pl.ds(2 * wide, rests[tree])].reshape(members, rests[tree])
            )
            start += wide
        packed = jnp.concatenate(packed, axis=1)
        for q in range(4):
            rows_x[pl.ds(group_main, group_rest), pl.ds(q * quarter, quarter)] = dot(
                pick(q), packed
            ).astype(BF16)
        acc[...] = dot(rows_x[:, pl.ds(0, half)], w1[pl.ds(0, half), :])
        both = acc[...] + dot(rows_x[:, pl.ds(half, half)], w1[pl.ds(half, half), :])
        hidden[...] = (silu(both[:, :units]) * both[:, units:]).astype(BF16)

        start = 0
        for tree in range(2):
            wide = mains[tree]
            made = dot(hidden[...], w2[:, pl.ds(start, wide)]).astype(BF16)
            for tile in range(2):
                outs[tree][base, :, pl.ds(tile * wide, wide)] = made[
                    tile * members : (tile + 1) * members
                ].reshape(GROUP, 16, wide)
            few_acc[:, pl.ds(start, wide)] = made[group_main:]
            start += wide
        few = jnp.zeros((members, quarter), F32)
        for q in range(4):
            few = few + dot(put(q), few_acc[:, pl.ds(q * quarter, quarter)])
        few = few.astype(BF16)
        outs_a[base, :, pl.ds(2 * mains[0], rests[0])] = few[:, : rests[0]].reshape(
            GROUP, 16, rests[0]
        )
        outs_b[base, :, pl.ds(2 * mains[1], rests[1])] = few[:, rests[0] :].reshape(
            GROUP, 16, rests[1]
        )

    def when_full(g):
        if g == 0:
            for load in loads:
                load.wait()
        feed(g)

    gather(when_full)

    def add(tree, slot, child, part):
        here = lanes(tree, part)
        total = outs[tree][slot, :, here].astype(F32) + sums[tree][child, :, here].astype(F32)
        outs[tree][slot, :, here] = total.astype(BF16)

    reduce, reduce_end = gather_sum(
        view_of(outs), view_of(sums), add, sum_send_sems, sum_recv_sems
    )
    reduce()

    start = 0
    for tree in range(2):
        wide = mains[tree]
        for tile in range(2):
            made_rows[pl.ds(tile * 16, 16), pl.ds(start, wide)] = outs[tree][
                0, :, pl.ds(tile * wide, wide)
            ]
        start += wide
    packed = jnp.concatenate(
        [outs[tree][0, :, pl.ds(2 * mains[tree], rests[tree])] for tree in range(2)], axis=1
    )
    small_row = lax.broadcasted_iota(jnp.int32, (16, 16), 0)
    small_col = lax.broadcasted_iota(jnp.int32, (16, 16), 1)
    for q in range(4):
        choose = one_hot(jnp.logical_and(small_row < 4, small_col == q * 4 + small_row))
        made_rows[pl.ds(CAP_MAIN, 16), pl.ds(q * quarter, quarter)] = dot(choose, packed).astype(
            BF16
        )
    routes_t = routes_ref[...]
    toks = routes_t.shape[1]
    table_t = slot_table(routes_t)
    table = table_t.T
    chosen = jnp.where(routes_t == e, gate_ref[...], 0.0)
    weight_t = chosen[0:1, :] + chosen[1:2, :]
    expert_row = lax.broadcasted_iota(jnp.int32, (LANES, toks), 0)
    place_t = jnp.sum(jnp.where(expert_row == e, table_t, 0.0), axis=0, keepdims=True)
    at = lax.broadcasted_iota(jnp.int32, (SLAB, toks), 0).astype(F32)
    mine = (at == place_t).astype(F32)
    row_weight = jnp.sum(mine * weight_t, axis=1, keepdims=True)
    block = width // count
    for j in range(count):
        part = made_rows[:, pl.ds(j * block, block)].astype(F32)
        sent[j] = (row_weight * part).astype(BF16)

    def give(k):
        to = lax.rem(e + k, count)
        return pltpu.make_async_remote_copy(
            src_ref=sent.at[to],
            dst_ref=got.at[e],
            send_sem=out_send_sems.at[k - 1],
            recv_sem=out_recv_sems.at[k - 1],
            device_id=exp_id(to),
            device_id_type=MESH,
        )

    for k in range(1, count):
        give(k).start()
    got[e] = sent[e]
    for k in range(1, count):
        give(k).wait_recv()
    mixer_end()
    total = resid_ref[...]
    place_lane = lax.broadcasted_iota(jnp.int32, (toks, SLAB), 1).astype(F32)
    for j in range(count):
        total = total + dot(one_hot(place_lane == table[:, j : j + 1]), got[j])
    out_ref[...] = total.astype(BF16)

    gather_end()
    reduce_end()
    for k in range(1, count):
        give(k).wait_send()


def layer_kernel(
    mamba_ref,
    bc_ref,
    decay_ref,
    conv_ref,
    vec_ref,
    doc_ref,
    residual_ref,
    w_ref,
    gain_ref,
    routes_ref,
    gate_ref,
    w1_ref,
    w2_ref,
    out_ref,
    resid,
    held_a,
    held_b,
    *scratch,
):
    mixer_refs, expert_refs = scratch[:MIXER_SCRATCH], scratch[MIXER_SCRATCH:]
    mixer_end = mixer_part(
        mamba_ref,
        bc_ref,
        decay_ref,
        conv_ref,
        vec_ref,
        doc_ref,
        residual_ref,
        w_ref,
        gain_ref,
        routes_ref,
        resid,
        held_a.at[0],
        held_b.at[0],
        *mixer_refs,
    )
    experts_part(
        mixer_end,
        resid,
        routes_ref,
        gate_ref,
        w1_ref,
        w2_ref,
        out_ref,
        held_a,
        held_b,
        *expert_refs,
    )


MIXER_SCRATCH = 34


def layer(mamba_in, bc, decay, conv_w, vec, doc_len, residual, w_out, gain, routes, gates, w1, w2):
    toks, channels = mamba_in.shape[1:]
    nstate = decay.shape[0]
    rows = channels // LANES
    units, width = w2.shape
    count = lax.axis_size("exp")
    block = width // count
    depth = w_out.shape[0]
    mains, rests = split_lanes(width)
    sizes = [2 * main + rest for main, rest in zip(mains, rests)]
    xs_count = count // CORES
    exp_sems = 2 * xs_count + 2 * (count - 1)
    group_rows = GROUP * (CAP_MAIN + 4)
    vmem = pl.BlockSpec(memory_space=pltpu.VMEM)
    smem = pl.BlockSpec(memory_space=pltpu.SMEM)
    hbm = pl.BlockSpec(memory_space=pl.ANY)
    held = [pltpu.VMEM((len(SLOTS), 16, size), BF16) for size in sizes]
    mixer_scratch = [
        pltpu.VMEM(((toks + 8) * rows, LANES), F32),
        pltpu.VMEM((toks * rows, LANES), F32),
        pltpu.VMEM((toks * rows, LANES), F32),
        pltpu.VMEM((toks * rows, LANES), F32),
        pltpu.VMEM((nstate * rows, LANES), F32),
        pltpu.VMEM((16, channels), BF16),
        pltpu.VMEM((ZS, 4 * rows, LANES), BF16),
        pltpu.VMEM((3 * ZS, 4 * rows, LANES), BF16),
        pltpu.VMEM((ZS, 2 * rows, LANES), BF16),
        pltpu.VMEM((ZS, 2 * rows, LANES), BF16),
        pltpu.VMEM((ZS, depth, LANES), BF16),
        pltpu.VMEM((YS, toks, channels), BF16),
        pltpu.VMEM((CORES, xs_count, YS, toks, LANES), BF16),
        pltpu.VMEM((xs_count, YS, toks, LANES), BF16),
        pltpu.VMEM((xs_count, YS, toks, LANES), BF16),
        pltpu.VMEM((xs_count - 1, YS, toks, LANES), BF16),
        pltpu.VMEM((count, SLAB, block), BF16),
        pltpu.VMEM((count, SLAB, block), BF16),
        pltpu.VMEM((count, 8, LANES), F32),
        pltpu.VMEM((SLAB, width), BF16),
        pltpu.VMEM((YS, toks, LANES), BF16),
        pltpu.VMEM((YS, toks, LANES), BF16),
        pltpu.VMEM((YS, toks, LANES), BF16),
        pltpu.VMEM((YS, toks, LANES), BF16),
        pltpu.SemaphoreType.DMA((4 * ZS,)),
        pltpu.SemaphoreType.DMA((4 * ZS,)),
        pltpu.SemaphoreType.DMA((2 * len(W_STEPS),)),
        pltpu.SemaphoreType.DMA((2 * len(W_STEPS),)),
        pltpu.SemaphoreType.DMA((2 * len(GATED_STEPS),)),
        pltpu.SemaphoreType.DMA((2 * len(GATED_STEPS),)),
        pltpu.SemaphoreType.DMA((2 * YS - 1,)),
        pltpu.SemaphoreType.DMA((2 * YS - 1,)),
        pltpu.SemaphoreType.DMA((exp_sems,)),
        pltpu.SemaphoreType.DMA((exp_sems,)),
    ]
    assert len(mixer_scratch) == MIXER_SCRATCH
    expert_scratch = (
        held
        + held
        + [
            pltpu.VMEM((width, 2 * units), BF16),
            pltpu.VMEM((units, width), BF16),
            pltpu.VMEM((group_rows, width), BF16),
            pltpu.VMEM((group_rows, 2 * units), F32),
            pltpu.VMEM((group_rows, units), BF16),
            pltpu.VMEM((GROUP * 4, width), BF16),
            pltpu.VMEM((SLAB, width), BF16),
            pltpu.VMEM((count, SLAB, block), BF16),
            pltpu.VMEM((count, SLAB, block), BF16),
            pltpu.SemaphoreType.DMA((3,)),
        ]
        + [pltpu.SemaphoreType.DMA((len(MESSAGES),)) for _ in range(4)]
        + [pltpu.SemaphoreType.DMA((count - 1,)) for _ in range(2)]
    )
    return pl.pallas_call(
        layer_kernel,
        out_shape=jax.ShapeDtypeStruct((toks, block), BF16),
        in_specs=[vmem, smem, vmem, vmem, vmem, smem, vmem, vmem, vmem, vmem, vmem, hbm, hbm],
        out_specs=vmem,
        scratch_shapes=[pltpu.VMEM((toks, block), F32)] + held + mixer_scratch + expert_scratch,
        compiler_params=pltpu.CompilerParams(
            collective_id=1, has_side_effects=True, vmem_limit_bytes=62 * 1024 * 1024
        ),
        name="layer",
    )(
        mamba_in,
        bc,
        decay,
        conv_w,
        vec,
        doc_len,
        residual,
        w_out,
        gain.reshape(1, width),
        routes,
        gates,
        w1,
        w2,
    )


def shards(
    residual_in,
    mamba_in,
    bc_proj,
    decay,
    conv_w,
    mamba_vec,
    doc_len,
    w_out,
    norm_gain,
    routes,
    gate_w,
    w_gate_up,
    w_down,
):
    return layer(
        mamba_in,
        bc_proj,
        decay,
        conv_w,
        mamba_vec,
        doc_len,
        residual_in,
        w_out,
        norm_gain,
        routes.T,
        gate_w.T,
        w_gate_up[0],
        w_down[0],
    )


def solution(mesh):
    in_specs = (
        P("seq", None),
        P(None, "seq", "exp"),
        P(None, "seq"),
        P(None, "exp"),
        P(None, "exp"),
        P(None, "exp"),
        P(),
        P("exp", "seq"),
        P(),
        P("seq", None),
        P("seq", None),
        P("exp", None, None, "seq"),
        P("exp", "seq", None),
    )
    out_specs = P("seq", "exp")
    return jax.shard_map(shards, mesh=mesh, in_specs=in_specs, out_specs=out_specs, check_vma=False)
```

```python
import jax
import jax.numpy as jnp
from jax import lax
from jax.experimental import pallas as pl
from jax.experimental.pallas import tpu as pltpu
from jax.sharding import PartitionSpec as P

MESH = pl.DeviceIdType.MESH
LOG2E = 1.4426950408889634
LANES = 128
F32 = jnp.float32
BF16 = jnp.bfloat16
YS, ZS = 4, 8
CORES = 2
SLAB = 48
CAP_MAIN = 32

Y_OFFSETS = (0, 1, -1, 2)
Z_OFFSETS = (0, 1, -1, 2, -2, 3, -3, 4)
SLOTS = [(dy, dz) for dz in Z_OFFSETS for dy in Y_OFFSETS]
GROUP = 8


def far_steps(offset, size):
    top = size // 2
    if offset == 0:
        return [(1, 1, None), (-1, -1, None)]
    if offset == top:
        return []
    if offset > 0:
        return [(offset + 1, 1, 0 if offset + 1 == top else None)]
    return [(offset - 1, -1, None)] if offset - 1 > -top else [(top, -1, 1)]


def messages():
    found = []
    for tree in range(2):
        for dy, dz in SLOTS:
            if tree == 1 or dz == 0:
                for to, way, part in far_steps(dy, YS):
                    found.append((tree, (dy, dz), (to, dz), part, ("y", way)))
            if tree == 0 or dy == 0:
                for to, way, part in far_steps(dz, ZS):
                    found.append((tree, (dy, dz), (dy, to), part, ("z", way)))
    return found


MESSAGES = messages()
DEPTH = {slot: abs(slot[0]) + abs(slot[1]) for slot in SLOTS}
DEEPEST = max(DEPTH.values())


ORDER = [
    1, 2, 39, 40, 37, 38, 3, 4, -1, 5, 6, 7, -2, 8, -39, 43, 44, 45, -40, 50, -37, 41, -38, 42, 9,
    10, 48, 49, -3, -4, -5, -8, 13, 17, -6, -7, -43, 46, -44, 47, -45, 55, -50, 60, 53, 54, -41,
    -42, 11, 12, -48, 51, -49, 52, -9, -10, 14, 18, 58, 59, -13, -17, -46, -47, -55, 65, -60, 70,
    -53, 56, -54, 57, 15, 19, 63, 64, 21, 25, -11, -12, -51, -52, 16, 20, -58, 61, -59, 62, -14,
    -18, 68, 69, -65, -70, 22, 26, -56, -57, -15, -19, 23, 27, -63, 66, -64, 67, -21, -25, 29, 33,
    73, 74, -16, 24, -20, 28, -61, -62, -22, 30, -26, 34, -68, 71, -69, 72, -23, 31, -27, 35, -24,
    32, -28, 36, -73, 75, -74, 76, -66, -67, -29, -33, -30, -34, -71, -72, -31, -35, -32, -36, -75,
    -76,
]


def groups_full_at(at):
    last = {}
    for place, item in enumerate(ORDER):
        if item < 0:
            last[SLOTS.index(MESSAGES[-item - 1][2]) // GROUP] = place
    return [group for group in sorted(last) if last[group] == at]


def silu(v):
    return v / (1.0 + jnp.exp(-v))


def seq_id(index):
    return {"seq": index}


def exp_id(index):
    return {"exp": index}


def neighbour(axis, way):
    me = lax.axis_index("seq")
    y, z = me // ZS, me % ZS
    if axis == "y":
        return ((y + way + YS) % YS) * ZS + z
    return y * ZS + (z + way + ZS) % ZS


def spread(view, send_sems, recv_sems):
    def copy(k):
        tree, source, target, part, way = MESSAGES[k]
        return pltpu.make_async_remote_copy(
            src_ref=view(tree, SLOTS.index(source), part),
            dst_ref=view(tree, SLOTS.index(target), part),
            send_sem=send_sems.at[k],
            recv_sem=recv_sems.at[k],
            device_id=seq_id(neighbour(*way)),
            device_id_type=MESH,
        )

    def run(when_full, start=0, stop=len(ORDER)):
        for at in range(start, stop):
            item = ORDER[at]
            if item > 0:
                copy(item - 1).start()
            else:
                copy(-item - 1).wait_recv()
                for group in groups_full_at(at):
                    when_full(group)

    def finish():
        for k in range(len(MESSAGES)):
            copy(k).wait_send()

    return run, finish


def gather_sum(view, landing, add, send_sems, recv_sems):
    def copy(k):
        tree, _, child, part, (axis, way) = MESSAGES[k]
        return pltpu.make_async_remote_copy(
            src_ref=view(tree, SLOTS.index(child), part),
            dst_ref=landing(tree, SLOTS.index(child), part),
            send_sem=send_sems.at[k],
            recv_sem=recv_sems.at[k],
            device_id=seq_id(neighbour(axis, -way)),
            device_id_type=MESH,
        )

    def run():
        for item in reversed(ORDER):
            k = abs(item) - 1
            if item < 0:
                copy(k).start()
            else:
                copy(k).wait_recv()
                _, parent, child, part, _ = MESSAGES[k]
                add(MESSAGES[k][0], SLOTS.index(parent), SLOTS.index(child), part)

    def finish():
        for k in range(len(MESSAGES)):
            copy(k).wait_send()

    return run, finish


def dot(a, b):
    return jnp.dot(a, b, preferred_element_type=F32)


def one_hot(condition):
    return condition.astype(F32).astype(BF16)


def slot_table(routes_t):
    toks = routes_t.shape[1]
    expert = lax.broadcasted_iota(jnp.int32, (LANES, toks), 0)
    hits = jnp.logical_or(routes_t[0:1, :] == expert, routes_t[1:2, :] == expert)
    row = lax.broadcasted_iota(jnp.int32, (toks, toks), 0)
    col = lax.broadcasted_iota(jnp.int32, (toks, toks), 1)
    places = dot(one_hot(hits), one_hot(row <= col)) - 1.0
    return jnp.where(hits, places, -1.0)


def places_of(table_t, expert):
    place = lax.broadcasted_iota(jnp.int32, (SLAB, table_t.shape[1]), 0).astype(F32)
    return (place == table_t[expert : expert + 1, :]).astype(F32)


def split_lanes(width):
    first = (width * 13 // 32) // LANES * LANES
    quarter = width // 4
    rest = (quarter * 13 // 32) // LANES * LANES
    return (first, width - first), (rest, quarter - rest)


def ring_steps(offsets, size):
    return [
        (offset, to, way, part)
        for offset in offsets
        for to, way, part in far_steps(offset, size)
    ]


W_SLOTS = Z_OFFSETS
W_STEPS = ring_steps(Z_OFFSETS, ZS)
GATED_STEPS = ring_steps(Y_OFFSETS, YS)


def mixer_part(
    mamba_ref,
    bc_ref,
    decay_ref,
    conv_ref,
    vec_ref,
    doc_ref,
    residual_ref,
    w_ref,
    gain_ref,
    routes_ref,
    resid_ref,
    own_a,
    own_b,
    xs,
    dts,
    us,
    zs,
    neg,
    tail,
    end_out,
    end_in,
    start_out,
    start_in,
    held_w,
    gated,
    partial,
    pair_in,
    pair_sum,
    cross_in,
    disp,
    disp_in,
    squares,
    rows_n,
    mix_out,
    mix_in,
    final_out,
    final_in,
    send_sems,
    recv_sems,
    w_send_sems,
    w_recv_sems,
    g_send_sems,
    g_recv_sems,
    y_send_sems,
    y_recv_sems,
    exp_send_sems,
    exp_recv_sems,
):
    count = lax.axis_size("seq")
    me = lax.axis_index("seq")
    toks = mamba_ref.shape[1]
    blocks = mamba_ref.shape[2] // LANES
    nstate = decay_ref.shape[0]
    rows = blocks
    first = me * toks
    e = lax.axis_index("exp")
    experts_count = lax.axis_size("exp")
    x, core = e // CORES, e % CORES
    xs_count = experts_count // CORES

    barrier = pltpu.get_barrier_semaphore()

    def greet(step, _):
        pl.semaphore_signal(
            barrier, inc=1, device_id=seq_id(lax.rem(me + step, count)), device_id_type=MESH
        )
        return 0

    lax.fori_loop(1, count, greet, 0)
    for step in range(1, experts_count):
        pl.semaphore_signal(
            barrier,
            inc=1,
            device_id=exp_id(lax.rem(e + step, experts_count)),
            device_id_type=MESH,
        )

    depth = w_ref.shape[0]
    held_w[0] = w_ref[...]
    y, z = me // ZS, me % ZS
    for j in range(blocks):
        lanes = pl.ds(j * LANES, LANES)
        xs[pl.ds(8 * rows + j, toks, stride=rows), :] = mamba_ref[0, :, lanes].astype(F32)
        zs[pl.ds(j, toks, stride=rows), :] = mamba_ref[1, :, lanes].astype(F32)
        dts[pl.ds(j, toks, stride=rows), :] = mamba_ref[2, :, lanes].astype(F32)
    pl.semaphore_wait(barrier, count - 1 + experts_count - 1)

    flows = 2
    flow_rows = depth // flows

    def w_copy(k, flow):
        source, target, way, part = W_STEPS[k]
        size = flow_rows if part is None else flow_rows // 2
        here = pl.ds(flow * flow_rows + (part or 0) * size, size)
        return pltpu.make_async_remote_copy(
            src_ref=held_w.at[W_SLOTS.index(source), here],
            dst_ref=held_w.at[W_SLOTS.index(target), here],
            send_sem=w_send_sems.at[k * flows + flow],
            recv_sem=w_recv_sems.at[k * flows + flow],
            device_id=seq_id(neighbour("z", way)),
            device_id_type=MESH,
        )

    def forward(round):
        for flow in range(flows):
            for way in (1, -1):
                for k, step in enumerate(W_STEPS):
                    if step[2] == way and abs(step[0]) == round - 1:
                        w_copy(k, flow).wait_recv()
                for k, step in enumerate(W_STEPS):
                    if step[2] == way and abs(step[0]) == round:
                        w_copy(k, flow).start()


    tail_copy = pltpu.make_async_remote_copy(
        src_ref=mamba_ref.at[0, pl.ds(toks - 16, 16)],
        dst_ref=tail,
        send_sem=send_sems.at[0],
        recv_sem=recv_sems.at[0],
        device_id=seq_id(lax.rem(me + 1, count)),
        device_id_type=MESH,
    )
    tail_copy.start()

    forward(0)
    for j in range(blocks):
        lanes = pl.ds(j * LANES, LANES)
        neg[pl.ds(j, nstate, stride=rows), :] = decay_ref[:, lanes] * (-LOG2E)

    def tile_row(ref, n):
        return jnp.concatenate(
            [ref[n : n + 1, j * LANES : (j + 1) * LANES] for j in range(blocks)], axis=0
        )

    step_bias = tile_row(vec_ref, 1)

    def tok(t):
        return pl.ds(pl.multiple_of(t * rows, rows), rows)

    def prepare(t, total):
        raw = dts[tok(t), :] + step_bias
        step = jnp.maximum(raw, 0.0) + jnp.log1p(jnp.exp(-jnp.abs(raw)))
        dts[tok(t), :] = step
        zs[tok(t), :] = silu(zs[tok(t), :])
        return total + step

    total_step = lax.fori_loop(0, toks, prepare, jnp.zeros((rows, LANES), F32), unroll=8)

    tail_copy.wait()
    there = jnp.where(me > 0, jnp.float32(1.0), jnp.float32(0.0))
    for j in range(blocks):
        rest = tail[:, pl.ds(j * LANES, LANES)].astype(F32) * there
        xs[pl.ds(j, 8, stride=rows), :] = rest[8:16, :]

    ends = []
    so_far = jnp.int32(0)
    for j in range(doc_ref.shape[0]):
        so_far = so_far + doc_ref[j]
        ends.append(so_far)

    def goes_on(position):
        keep = jnp.float32(1.0)
        for end in ends:
            keep = jnp.where(end == position, jnp.float32(0.0), keep)
        return keep

    taps = [tile_row(conv_ref, k) for k in range(conv_ref.shape[0])]
    conv_bias = tile_row(vec_ref, 0)

    def advance(t, states, keep, step, drive):
        new = []
        for n in range(nstate):
            growth = jnp.exp2(step * neg[pl.ds(n * rows, rows), :]) * keep
            new.append(growth * states[n] + drive * bc_ref[n, t])
        return tuple(new)

    def local_pass(t, carry):
        states, before, before2 = carry
        keep = goes_on(first + t)
        x0, x1, x2, x3 = [xs[tok(t + 8 - 3 + k), :] for k in range(4)]
        v2 = keep
        v1 = keep * before
        v0 = v1 * before2
        total = conv_bias + (taps[0] * x0) * v0 + (taps[1] * x1) * v1
        total = total + (taps[2] * x2) * v2 + taps[3] * x3
        u_row = silu(total)
        us[tok(t), :] = u_row
        step = dts[tok(t), :]
        return advance(t, states, keep, step, step * u_row), keep, before

    zero = tuple(jnp.zeros((rows, LANES), F32) for _ in range(nstate))
    carry = (zero, goes_on(first - 1), goes_on(first - 2))
    states, _, _ = lax.fori_loop(0, toks, local_pass, carry, unroll=4)
    high = total_step.astype(BF16)
    low = (total_step - high.astype(F32)).astype(BF16)
    for n in range(0, nstate, 2):
        pair = jnp.concatenate([states[n], states[n + 1]], axis=0).astype(BF16)
        end_out[n // 2] = jnp.concatenate([pair, high, low], axis=0)
    before = 2
    end_in[before * ZS + z] = end_out[z]

    def scatter(i):
        row, step = i // ZS, i % ZS
        holder = lax.rem(z + step, ZS)
        return pltpu.make_async_remote_copy(
            src_ref=end_out.at[holder],
            dst_ref=end_in.at[(before - row) * ZS + z],
            send_sem=send_sems.at[i],
            recv_sem=recv_sems.at[i],
            device_id=seq_id(lax.rem(y + row, YS) * ZS + holder),
            device_id_type=MESH,
        )

    def give_back(step):
        return pltpu.make_async_remote_copy(
            src_ref=start_out.at[lax.rem(z + step, ZS)],
            dst_ref=start_in.at[z],
            send_sem=send_sems.at[(before + 1) * ZS + step],
            recv_sem=recv_sems.at[(before + 1) * ZS + step],
            device_id=seq_id(y * ZS + lax.rem(z + step, ZS)),
            device_id_type=MESH,
        )

    def send(i, _):
        scatter(later - i).start()
        return 0

    later = jnp.minimum(before + 1, YS - y) * ZS
    earlier = jnp.minimum(before, y)
    lax.fori_loop(1, later, send, 0)
    forward(1)

    def arrive(i, _):
        scatter(i).wait_recv()
        return 0

    lax.fori_loop(1, (earlier + 1) * ZS, arrive, 0)

    def fold(at, held):
        begin = ((y - before) * ZS + at) * toks
        unbroken = jnp.float32(1.0)
        for end in ends:
            inside = jnp.logical_and(end >= begin, end < begin + toks)
            unbroken = jnp.where(inside, jnp.float32(0.0), unbroken)
        halves = end_in[at, pl.ds(2 * rows, 2 * rows), :].astype(F32)
        sums = halves[:rows] + halves[rows:]
        pair = end_in[at, pl.ds(0, 2 * rows), :].astype(F32)
        new = []
        for n in range(2):
            rate = neg[pl.ds(pl.multiple_of((2 * z + n) * rows, rows), rows), :]
            growth = jnp.exp2(sums * rate) * unbroken
            new.append(growth * held[n] + pair[n * rows : (n + 1) * rows, :])
        return tuple(new)

    def fold_own(at, held):
        start_out[at - before * ZS] = jnp.concatenate(held, axis=0).astype(BF16)
        return fold(at, held)

    held = lax.fori_loop((before - earlier) * ZS, before * ZS, fold, zero[:2])
    lax.fori_loop(before * ZS, (before + 1) * ZS, fold_own, held)

    def return_start(step, _):
        give_back(step).start()
        return 0

    lax.fori_loop(1, ZS, return_start, 0)
    start_in[z] = start_out[z]
    forward(2)

    def return_arrive(step, _):
        give_back(step).wait_recv()
        return 0

    lax.fori_loop(1, ZS, return_arrive, 0)
    entering = []
    for n in range(0, nstate, 2):
        pair = start_in[n // 2].astype(F32)
        entering += [pair[:rows], pair[rows:]]
    entering = tuple(entering)
    skip = tile_row(vec_ref, 2)

    def full_pass(t, states):
        keep = goes_on(first + t)
        u_row = us[tok(t), :]
        step = dts[tok(t), :]
        states = advance(t, states, keep, step, step * u_row)
        total = skip * u_row
        for n in range(nstate):
            total = total + states[n] * bc_ref[nstate + n, t]
        zs[tok(t), :] = zs[tok(t), :] * total
        return states

    half = toks // 2

    def gated_copy(k, piece):
        source, target, way, part = GATED_STEPS[k]
        size = half if part is None else half // 2
        here = pl.ds(piece * half + (part or 0) * size, size)
        return pltpu.make_async_remote_copy(
            src_ref=gated.at[Y_OFFSETS.index(source), here],
            dst_ref=gated.at[Y_OFFSETS.index(target), here],
            send_sem=g_send_sems.at[k * 2 + piece],
            recv_sem=g_recv_sems.at[k * 2 + piece],
            device_id=seq_id(neighbour("y", way)),
            device_id_type=MESH,
        )

    states = entering
    for piece in range(2):
        states = lax.fori_loop(piece * half, (piece + 1) * half, full_pass, states, unroll=4)
        for j in range(blocks):
            gated[0, pl.ds(piece * half, half), pl.ds(j * LANES, LANES)] = zs[
                pl.ds(piece * half * rows + j, half, stride=rows), :
            ].astype(BF16)
        for k, step in enumerate(GATED_STEPS):
            if step[0] == 0:
                gated_copy(k, piece).start()
    forward(3)
    table_t = slot_table(routes_ref[...])

    def product(slots):
        left = jnp.concatenate([gated[i] for i in slots], axis=0)
        for pair in range(ZS // 2):
            right = jnp.concatenate([held_w[2 * pair], held_w[2 * pair + 1]], axis=1)
            made = dot(left, right).astype(BF16)
            for n in range(2):
                owner = (z - W_SLOTS[2 * pair + n] + ZS) % ZS
                for i, slot in enumerate(slots):
                    shard = (y - Y_OFFSETS[slot] + YS) % YS
                    partial[owner % CORES, owner // CORES, shard] = made[
                        i * toks : (i + 1) * toks, n * LANES : (n + 1) * LANES
                    ]

    for piece in range(2):
        for k, step in enumerate(GATED_STEPS):
            if step[0] == 0:
                gated_copy(k, piece).wait_recv()
                for k2, step2 in enumerate(GATED_STEPS):
                    if step2[0] == step[1]:
                        gated_copy(k2, piece).start()
    forward(4)
    product([0, 1, 2])
    for piece in range(2):
        for k, step in enumerate(GATED_STEPS):
            if step[0] != 0:
                gated_copy(k, piece).wait_recv()
    product([3])

    def pair_copy(k):
        to = lax.rem(x + k, xs_count)
        return pltpu.make_async_remote_copy(
            src_ref=partial.at[1 - core, to],
            dst_ref=pair_in.at[to],
            send_sem=exp_send_sems.at[k],
            recv_sem=exp_recv_sems.at[k],
            device_id=exp_id(x * CORES + 1 - core),
            device_id_type=MESH,
        )

    def cross_copy(k):
        to = lax.rem(x + k, xs_count)
        return pltpu.make_async_remote_copy(
            src_ref=pair_sum.at[to],
            dst_ref=cross_in.at[k - 1],
            send_sem=exp_send_sems.at[xs_count + k],
            recv_sem=exp_recv_sems.at[xs_count + k],
            device_id=exp_id(to * CORES + core),
            device_id_type=MESH,
        )

    order = [2, 1, 3, 0]
    for k in order:
        pair_copy(k).start()
    for k in order:
        pair_copy(k).wait_recv()
        to = lax.rem(x + k, xs_count)
        total = partial[core, to].astype(F32) + pair_in[to].astype(F32)
        if k > 0:
            pair_sum[to] = total.astype(BF16)
            cross_copy(k).start()
    for k in (1, 3, 2):
        cross_copy(k).wait_recv()
        total = total + cross_in[k - 1].astype(F32)

    mix_out[...] = total.astype(BF16)

    def shard_copy(k):
        to = lax.rem(y + k, YS)
        return pltpu.make_async_remote_copy(
            src_ref=mix_out.at[to],
            dst_ref=mix_in.at[y],
            send_sem=y_send_sems.at[k - 1],
            recv_sem=y_recv_sems.at[k - 1],
            device_id=seq_id(to * ZS + z),
            device_id_type=MESH,
        )

    for k in (2, 1, 3):
        shard_copy(k).start()
    mix_in[y] = mix_out[y]
    for k in (1, 3, 2):
        shard_copy(k).wait_recv()
    width = residual_ref.shape[1]
    block = width // experts_count
    quarter = width // YS
    sides = []
    for q in range(YS):
        lane = pl.multiple_of(q * quarter + e * LANES, LANES)
        sides.append(residual_ref[:, pl.ds(lane, LANES)].astype(F32) + mix_in[q].astype(F32))
        final_out[q] = sides[q].astype(BF16)
    total = jnp.concatenate(sides, axis=1)

    def final_copy(q):
        return pltpu.make_async_remote_copy(
            src_ref=final_out.at[q],
            dst_ref=final_in.at[e % YS],
            send_sem=y_send_sems.at[YS - 1 + q],
            recv_sem=y_recv_sems.at[YS - 1 + e % YS],
            device_id=exp_id(CORES * q + e // YS),
            device_id_type=MESH,
        )

    def final_wait(j):
        return pltpu.make_async_remote_copy(
            src_ref=final_out.at[0],
            dst_ref=final_in.at[j],
            send_sem=y_send_sems.at[YS - 1],
            recv_sem=y_recv_sems.at[YS - 1 + j],
            device_id=exp_id(lax.rem(e + 1, experts_count)),
            device_id_type=MESH,
        )

    square = jnp.sum(total * total, axis=1, keepdims=True)
    squares[e] = (square * jnp.ones((1, LANES), F32)).T[0:8, :]
    sent_rows = total.astype(BF16)
    for j in range(experts_count):
        disp[j] = dot(places_of(table_t, j).astype(BF16), sent_rows).astype(BF16)

    def deal(k):
        to = lax.rem(e + k, experts_count)
        base = 2 * xs_count + 2 * (k - 1)
        return [
            pltpu.make_async_remote_copy(
                src_ref=source,
                dst_ref=target,
                send_sem=exp_send_sems.at[base + i],
                recv_sem=exp_recv_sems.at[base + i],
                device_id=exp_id(to),
                device_id_type=MESH,
            )
            for i, (source, target) in enumerate(
                [(disp.at[to], disp_in.at[e]), (squares.at[e], squares.at[e])]
            )
        ]

    for k in range(1, experts_count):
        for copy in deal(k):
            copy.start()
    for q in range(YS):
        home = CORES * q + e // YS == e

        @pl.when(home)
        def _():
            final_in[e % YS] = final_out[q]

        @pl.when(jnp.logical_not(home))
        def _():
            final_copy(q).start()

    disp_in[e] = disp[e]
    expert_row = lax.broadcasted_iota(jnp.int32, (LANES, toks), 0)
    place_t = jnp.sum(jnp.where(expert_row == e, table_t, 0.0), axis=0, keepdims=True)
    at = lax.broadcasted_iota(jnp.int32, (SLAB, toks), 0).astype(F32)
    mine = (at == place_t).astype(F32)
    for k in range(1, experts_count):
        for copy in deal(k):
            copy.wait_recv()
    mean = squares[0]
    for j in range(1, experts_count):
        mean = mean + squares[j]
    inverse = lax.rsqrt(mean * (1.0 / width) + 1e-05)
    scale = jnp.sum(mine * inverse[0:1, :], axis=1, keepdims=True)
    for j in range(experts_count):
        for q in range(YS):
            here = pl.ds(q * quarter + j * LANES, LANES)
            dealt = disp_in[j, :, pl.ds(q * LANES, LANES)].astype(F32)
            rows_n[:, here] = (dealt * scale * gain_ref[:, here]).astype(BF16)
    mains, rests = split_lanes(width)
    small_row = lax.broadcasted_iota(jnp.int32, (16, 16), 0)
    small_col = lax.broadcasted_iota(jnp.int32, (16, 16), 1)
    packed = jnp.zeros((16, quarter), F32)
    for q in range(4):
        choose = one_hot(jnp.logical_and(small_col < 4, small_row == q * 4 + small_col))
        packed = packed + dot(choose, rows_n[pl.ds(CAP_MAIN, 16), pl.ds(q * quarter, quarter)])
    packed = packed.astype(BF16)
    start = 0
    rest_start = 0
    for tree, own in enumerate((own_a, own_b)):
        wide = mains[tree]
        for tile in range(2):
            own[:, pl.ds(tile * wide, wide)] = rows_n[pl.ds(tile * 16, 16), pl.ds(start, wide)]
        own[:, pl.ds(2 * wide, rests[tree])] = packed[:, rest_start : rest_start + rests[tree]]
        start += wide
        rest_start += rests[tree]

    def finish():
        for j in range(YS):
            source = (e % CORES) * YS + j

            @pl.when(source != e)
            def _():
                final_wait(j).wait_recv()

            resid_ref[:, pl.ds(j * LANES, LANES)] = final_in[j].astype(F32)
        for q in range(YS):

            @pl.when(CORES * q + e // YS != e)
            def _():
                final_copy(q).wait_send()

        for k in range(1, YS):
            shard_copy(k).wait_send()
        for k in range(len(GATED_STEPS)):
            for piece in range(2):
                gated_copy(k, piece).wait_send()
        for k in range(len(W_STEPS)):
            for flow in range(flows):
                w_copy(k, flow).wait_send()

        def sent(i, _):
            scatter(i).wait_send()
            return 0

        lax.fori_loop(1, later, sent, 0)

        def returned(step, _):
            give_back(step).wait_send()
            return 0

        lax.fori_loop(1, ZS, returned, 0)
        for k in range(xs_count):
            pair_copy(k).wait_send()
            if k > 0:
                cross_copy(k).wait_send()
        for k in range(1, experts_count):
            for copy in deal(k):
                copy.wait_send()

    return finish


def experts_part(
    mixer_end,
    loads,
    resid_ref,
    routes_ref,
    gate_ref,
    w1_ref,
    w2_ref,
    out_ref,
    held_a,
    held_b,
    outs_a,
    outs_b,
    sums_a,
    sums_b,
    w1,
    w2,
    rows_x,
    acc,
    hidden,
    few_acc,
    made_rows,
    sent,
    got,
    local_sems,
    send_sems,
    recv_sems,
    sum_send_sems,
    sum_recv_sems,
    out_send_sems,
    out_recv_sems,
):
    units, width = w2_ref.shape
    quarter = width // 4
    mains, rests = split_lanes(width)
    e = lax.axis_index("exp")
    count = lax.axis_size("exp")
    group_main = GROUP * CAP_MAIN
    group_rest = GROUP * 4

    held, outs, sums = (held_a, held_b), (outs_a, outs_b), (sums_a, sums_b)

    def lanes(tree, part):
        total = 2 * mains[tree] + rests[tree]
        cut = total // 2 // LANES * LANES
        if part is None:
            return pl.ds(0, total)
        return pl.ds(0, cut) if part == 0 else pl.ds(cut, total - cut)

    def view_of(refs):
        return lambda tree, slot, part: refs[tree].at[slot, :, lanes(tree, part)]

    gather, gather_end = spread(view_of(held), send_sems, recv_sems)

    row = lax.broadcasted_iota(jnp.int32, (group_rest, group_rest * 4), 0)
    col = lax.broadcasted_iota(jnp.int32, (group_rest, group_rest * 4), 1)
    row_t = lax.broadcasted_iota(jnp.int32, (group_rest * 4, group_rest), 0)
    col_t = lax.broadcasted_iota(jnp.int32, (group_rest * 4, group_rest), 1)

    def pick(q):
        return one_hot(col == (row // 4) * 16 + q * 4 + row % 4)

    def put(q):
        return one_hot(row_t == (col_t // 4) * 16 + q * 4 + col_t % 4)

    half = width // 2
    members = GROUP * 16

    def feed(g):
        base = pl.ds(g * GROUP, GROUP)
        start = 0
        packed = []
        for tree in range(2):
            wide = mains[tree]
            for tile in range(2):
                rows_x[pl.ds(tile * members, members), pl.ds(start, wide)] = held[tree][
                    base, :, pl.ds(tile * wide, wide)
                ].reshape(members, wide)
            packed.append(
                held[tree][base, :, pl.ds(2 * wide, rests[tree])].reshape(members, rests[tree])
            )
            start += wide
        packed = jnp.concatenate(packed, axis=1)
        for q in range(4):
            rows_x[pl.ds(group_main, group_rest), pl.ds(q * quarter, quarter)] = dot(
                pick(q), packed
            ).astype(BF16)
        acc[...] = dot(rows_x[:, pl.ds(0, half)], w1[pl.ds(0, half), :])
        both = acc[...] + dot(rows_x[:, pl.ds(half, half)], w1[pl.ds(half, half), :])
        hidden[...] = (silu(both[:, :units]) * both[:, units:]).astype(BF16)

        start = 0
        for tree in range(2):
            wide = mains[tree]
            made = dot(hidden[...], w2[:, pl.ds(start, wide)]).astype(BF16)
            for tile in range(2):
                outs[tree][base, :, pl.ds(tile * wide, wide)] = made[
                    tile * members : (tile + 1) * members
                ].reshape(GROUP, 16, wide)
            few_acc[:, pl.ds(start, wide)] = made[group_main:]
            start += wide
        few = jnp.zeros((members, quarter), F32)
        for q in range(4):
            few = few + dot(put(q), few_acc[:, pl.ds(q * quarter, quarter)])
        few = few.astype(BF16)
        outs_a[base, :, pl.ds(2 * mains[0], rests[0])] = few[:, : rests[0]].reshape(
            GROUP, 16, rests[0]
        )
        outs_b[base, :, pl.ds(2 * mains[1], rests[1])] = few[:, rests[0] :].reshape(
            GROUP, 16, rests[1]
        )

    def when_full(g):
        if g == 0:
            for load in loads:
                load.wait()
        feed(g)

    gather(when_full)

    def add(tree, slot, child, part):
        here = lanes(tree, part)
        total = outs[tree][slot, :, here].astype(F32) + sums[tree][child, :, here].astype(F32)
        outs[tree][slot, :, here] = total.astype(BF16)

    reduce, reduce_end = gather_sum(
        view_of(outs), view_of(sums), add, sum_send_sems, sum_recv_sems
    )
    reduce()

    start = 0
    for tree in range(2):
        wide = mains[tree]
        for tile in range(2):
            made_rows[pl.ds(tile * 16, 16), pl.ds(start, wide)] = outs[tree][
                0, :, pl.ds(tile * wide, wide)
            ]
        start += wide
    packed = jnp.concatenate(
        [outs[tree][0, :, pl.ds(2 * mains[tree], rests[tree])] for tree in range(2)], axis=1
    )
    small_row = lax.broadcasted_iota(jnp.int32, (16, 16), 0)
    small_col = lax.broadcasted_iota(jnp.int32, (16, 16), 1)
    for q in range(4):
        choose = one_hot(jnp.logical_and(small_row < 4, small_col == q * 4 + small_row))
        made_rows[pl.ds(CAP_MAIN, 16), pl.ds(q * quarter, quarter)] = dot(choose, packed).astype(
            BF16
        )
    routes_t = routes_ref[...]
    toks = routes_t.shape[1]
    table_t = slot_table(routes_t)
    table = table_t.T
    chosen = jnp.where(routes_t == e, gate_ref[...], 0.0)
    weight_t = chosen[0:1, :] + chosen[1:2, :]
    expert_row = lax.broadcasted_iota(jnp.int32, (LANES, toks), 0)
    place_t = jnp.sum(jnp.where(expert_row == e, table_t, 0.0), axis=0, keepdims=True)
    at = lax.broadcasted_iota(jnp.int32, (SLAB, toks), 0).astype(F32)
    mine = (at == place_t).astype(F32)
    row_weight = jnp.sum(mine * weight_t, axis=1, keepdims=True)
    block = width // count
    for j in range(count):
        part = made_rows[:, pl.ds(j * block, block)].astype(F32)
        sent[j] = (row_weight * part).astype(BF16)

    def give(k):
        to = lax.rem(e + k, count)
        return pltpu.make_async_remote_copy(
            src_ref=sent.at[to],
            dst_ref=got.at[e],
            send_sem=out_send_sems.at[k - 1],
            recv_sem=out_recv_sems.at[k - 1],
            device_id=exp_id(to),
            device_id_type=MESH,
        )

    for k in range(1, count):
        give(k).start()
    got[e] = sent[e]
    gather_end()
    mixer_end()
    reduce_end()
    for k in range(1, count):
        give(k).wait_recv()
    total = resid_ref[...]
    place_lane = lax.broadcasted_iota(jnp.int32, (toks, SLAB), 1).astype(F32)
    for j in range(count):
        total = total + dot(one_hot(place_lane == table[:, j : j + 1]), got[j])
    out_ref[...] = total.astype(BF16)

    for k in range(1, count):
        give(k).wait_send()


def layer_kernel(
    mamba_ref,
    bc_ref,
    decay_ref,
    conv_ref,
    vec_ref,
    doc_ref,
    residual_ref,
    w_ref,
    gain_ref,
    routes_ref,
    gate_ref,
    w1_ref,
    w2_ref,
    out_ref,
    resid,
    held_a,
    held_b,
    *scratch,
):
    mixer_refs, expert_refs = scratch[:MIXER_SCRATCH], scratch[MIXER_SCRATCH:]
    w1, w2, local_sems = expert_refs[4], expert_refs[5], expert_refs[13]
    units = w2_ref.shape[0]
    loads = [
        pltpu.make_async_copy(w1_ref.at[0], w1.at[:, pl.ds(0, units)], local_sems.at[0]),
        pltpu.make_async_copy(w1_ref.at[1], w1.at[:, pl.ds(units, units)], local_sems.at[1]),
        pltpu.make_async_copy(w2_ref, w2, local_sems.at[2]),
    ]
    for load in loads:
        load.start()
    mixer_end = mixer_part(
        mamba_ref,
        bc_ref,
        decay_ref,
        conv_ref,
        vec_ref,
        doc_ref,
        residual_ref,
        w_ref,
        gain_ref,
        routes_ref,
        resid,
        held_a.at[0],
        held_b.at[0],
        *mixer_refs,
    )
    experts_part(
        mixer_end,
        loads,
        resid,
        routes_ref,
        gate_ref,
        w1_ref,
        w2_ref,
        out_ref,
        held_a,
        held_b,
        *expert_refs,
    )


MIXER_SCRATCH = 34


def layer(mamba_in, bc, decay, conv_w, vec, doc_len, residual, w_out, gain, routes, gates, w1, w2):
    toks, channels = mamba_in.shape[1:]
    nstate = decay.shape[0]
    rows = channels // LANES
    units, width = w2.shape
    count = lax.axis_size("exp")
    block = width // count
    depth = w_out.shape[0]
    mains, rests = split_lanes(width)
    sizes = [2 * main + rest for main, rest in zip(mains, rests)]
    xs_count = count // CORES
    exp_sems = 2 * xs_count + 2 * (count - 1)
    group_rows = GROUP * (CAP_MAIN + 4)
    vmem = pl.BlockSpec(memory_space=pltpu.VMEM)
    smem = pl.BlockSpec(memory_space=pltpu.SMEM)
    hbm = pl.BlockSpec(memory_space=pl.ANY)
    held = [pltpu.VMEM((len(SLOTS), 16, size), BF16) for size in sizes]
    mixer_scratch = [
        pltpu.VMEM(((toks + 8) * rows, LANES), F32),
        pltpu.VMEM((toks * rows, LANES), F32),
        pltpu.VMEM((toks * rows, LANES), F32),
        pltpu.VMEM((toks * rows, LANES), F32),
        pltpu.VMEM((nstate * rows, LANES), F32),
        pltpu.VMEM((16, channels), BF16),
        pltpu.VMEM((ZS, 4 * rows, LANES), BF16),
        pltpu.VMEM((3 * ZS, 4 * rows, LANES), BF16),
        pltpu.VMEM((ZS, 2 * rows, LANES), BF16),
        pltpu.VMEM((ZS, 2 * rows, LANES), BF16),
        pltpu.VMEM((ZS, depth, LANES), BF16),
        pltpu.VMEM((YS, toks, channels), BF16),
        pltpu.VMEM((CORES, xs_count, YS, toks, LANES), BF16),
        pltpu.VMEM((xs_count, YS, toks, LANES), BF16),
        pltpu.VMEM((xs_count, YS, toks, LANES), BF16),
        pltpu.VMEM((xs_count - 1, YS, toks, LANES), BF16),
        pltpu.VMEM((count, SLAB, block), BF16),
        pltpu.VMEM((count, SLAB, block), BF16),
        pltpu.VMEM((count, 8, LANES), F32),
        pltpu.VMEM((SLAB, width), BF16),
        pltpu.VMEM((YS, toks, LANES), BF16),
        pltpu.VMEM((YS, toks, LANES), BF16),
        pltpu.VMEM((YS, toks, LANES), BF16),
        pltpu.VMEM((YS, toks, LANES), BF16),
        pltpu.SemaphoreType.DMA((4 * ZS,)),
        pltpu.SemaphoreType.DMA((4 * ZS,)),
        pltpu.SemaphoreType.DMA((2 * len(W_STEPS),)),
        pltpu.SemaphoreType.DMA((2 * len(W_STEPS),)),
        pltpu.SemaphoreType.DMA((2 * len(GATED_STEPS),)),
        pltpu.SemaphoreType.DMA((2 * len(GATED_STEPS),)),
        pltpu.SemaphoreType.DMA((2 * YS - 1,)),
        pltpu.SemaphoreType.DMA((2 * YS - 1,)),
        pltpu.SemaphoreType.DMA((exp_sems,)),
        pltpu.SemaphoreType.DMA((exp_sems,)),
    ]
    assert len(mixer_scratch) == MIXER_SCRATCH
    expert_scratch = (
        held
        + held
        + [
            pltpu.VMEM((width, 2 * units), BF16),
            pltpu.VMEM((units, width), BF16),
            pltpu.VMEM((group_rows, width), BF16),
            pltpu.VMEM((group_rows, 2 * units), F32),
            pltpu.VMEM((group_rows, units), BF16),
            pltpu.VMEM((GROUP * 4, width), BF16),
            pltpu.VMEM((SLAB, width), BF16),
            pltpu.VMEM((count, SLAB, block), BF16),
            pltpu.VMEM((count, SLAB, block), BF16),
            pltpu.SemaphoreType.DMA((3,)),
        ]
        + [pltpu.SemaphoreType.DMA((len(MESSAGES),)) for _ in range(4)]
        + [pltpu.SemaphoreType.DMA((count - 1,)) for _ in range(2)]
    )
    return pl.pallas_call(
        layer_kernel,
        out_shape=jax.ShapeDtypeStruct((toks, block), BF16),
        in_specs=[vmem, smem, vmem, vmem, vmem, smem, vmem, vmem, vmem, vmem, vmem, hbm, hbm],
        out_specs=vmem,
        scratch_shapes=[pltpu.VMEM((toks, block), F32)] + held + mixer_scratch + expert_scratch,
        compiler_params=pltpu.CompilerParams(
            collective_id=1, has_side_effects=True, vmem_limit_bytes=62 * 1024 * 1024
        ),
        name="layer",
    )(
        mamba_in,
        bc,
        decay,
        conv_w,
        vec,
        doc_len,
        residual,
        w_out,
        gain.reshape(1, width),
        routes,
        gates,
        w1,
        w2,
    )


def shards(
    residual_in,
    mamba_in,
    bc_proj,
    decay,
    conv_w,
    mamba_vec,
    doc_len,
    w_out,
    norm_gain,
    routes,
    gate_w,
    w_gate_up,
    w_down,
):
    return layer(
        mamba_in,
        bc_proj,
        decay,
        conv_w,
        mamba_vec,
        doc_len,
        residual_in,
        w_out,
        norm_gain,
        routes.T,
        gate_w.T,
        w_gate_up[0],
        w_down[0],
    )


def solution(mesh):
    in_specs = (
        P("seq", None),
        P(None, "seq", "exp"),
        P(None, "seq"),
        P(None, "exp"),
        P(None, "exp"),
        P(None, "exp"),
        P(),
        P("exp", "seq"),
        P(),
        P("seq", None),
        P("seq", None),
        P("exp", None, None, "seq"),
        P("exp", "seq", None),
    )
    out_specs = P("seq", "exp")
    return jax.shard_map(shards, mesh=mesh, in_specs=in_specs, out_specs=out_specs, check_vma=False)
```
